256 devices in a mesh: cuts: 8 (over x, y_lo), zero: 32 (over z, y_hi, core).
Axes of the slice: x: 4, y: 4 (y_hi: 2, y_lo: 2; y = y_hi * 2 + y_lo), z: 8, core: 2. Of those that a mesh axis runs over, the one named last changes fastest.
Arguments:
- inputs: bfloat16 [32768, 5632], P(('cuts', 'zero')), may hold values from -6 to 6
- cotangent: bfloat16 [32768, 5632], P(('cuts', 'zero')), may hold values from -6 to 6
- gate_a_weight: bfloat16 [5632, 176], P('zero'), may hold values from -0.4375 to 0.4375
- gate_x_weight: bfloat16 [5632, 176], P('zero'), may hold values from -0.4375 to 0.4375
- gate_a_bias: bfloat16 [5632], P('zero'), may hold values from -3 to 3
- gate_x_bias: bfloat16 [5632], P('zero'), may hold values from -3 to 3
- decay_param: bfloat16 [5632], P('zero'), may hold values from -9 to -4.28125
Outputs:
- input_grad: bfloat16 [32768, 5632], P(('cuts', 'zero'))
- gate_a_grad: float32 [5632, 176], P('zero')
- gate_x_grad: float32 [5632, 176], P('zero')
- bias_a_grad: float32 [5632], P('zero')
- bias_x_grad: float32 [5632], P('zero')
- decay_grad: float32 [5632], P('zero')
The draws below stay inside these ranges and needn't reach their ends.
All inputs are finite; a program needn't handle non-finite values.
Results may differ from the reference program's by a relative error of at most 0.008.
Values may be sent and summed in bfloat16 or wider, within the bound.
No kernel may reach another device: no remote copies, remote signals or barrier semaphores. Data moves between devices by JAX's collectives and lax.ppermute only.
A program may use at most 128 MiB of HBM per device.

```python
import jax
import jax.numpy as jnp
from jax import lax

R = 5632
B = 176
TOK_DEV = 128
TOKENS = 32768


def block_levels(own_key, shape, shards, smallest, high):
    def one(position, parts):
        draws = jax.random.uniform(jax.random.fold_in(jax.random.fold_in(own_key, 6), position), (parts,), jnp.float32, smallest / len(shards), high / len(shards))
        return jnp.repeat(jnp.exp(draws), shape[position] // parts).reshape((-1,) + (1,) * (len(shape) - position - 1))

    loudness = one(*shards[0])
    for cut in shards[1:]:
        loudness = loudness * one(*cut)
    return loudness


def bell_draw(own_key, extent, deviation, reach, cuts=(), kind=jnp.bfloat16):
    values = jax.random.normal(own_key, extent, jnp.float32) * deviation
    if len(cuts) > 0:
        values = block_levels(own_key, extent, cuts, -0.22, 0.18) * values
    return jnp.clip(values, min=-reach, max=reach).astype(kind)


def setup_inputs(seed: int = 0) -> dict:
    key_of = jax.random.split(jax.random.key(seed), 8)
    return {
        "inputs": bell_draw(key_of[0], (TOKENS, R), 1.0, 6.0, ((0, 256),)),
        "cotangent": bell_draw(key_of[1], (TOKENS, R), 1.0, 6.0, ((0, 256),)),
        "gate_a_weight": bell_draw(key_of[2], (R, B), B ** -0.5, 0.4375, ((0, 32),)),
        "gate_x_weight": bell_draw(key_of[3], (R, B), B ** -0.5, 0.4375, ((0, 32),)),
        "gate_a_bias": bell_draw(key_of[4], (R,), 1.0, 3.0, ((0, 32),)),
        "gate_x_bias": bell_draw(key_of[5], (R,), 1.0, 3.0, ((0, 32),)),
        "decay_param": jnp.clip(-9.0 + 4.71875 * jax.random.uniform(key_of[6], (R,), jnp.float32) ** block_levels(key_of[6], (R,), ((0, 32),), -0.2, 0.2), -9.0, -4.28125).astype(jnp.bfloat16),
    }


def linear_combine(first, second):
    coef_one, add_one = first
    coef_two, add_two = second
    return (coef_one * coef_two, coef_two * add_one + add_two)

def sequence_backward(values, upstream, weight_a, weight_x, bias_a, bias_x, decay_raw):
    length, hidden_width = values.shape
    block = weight_a.shape[1]
    heads = hidden_width // block
    blocks_in = values.astype(jnp.float32).reshape(length, heads, block)
    cube_a = weight_a.astype(jnp.float32).reshape(heads, block, block)
    cube_x = weight_x.astype(jnp.float32).reshape(heads, block, block)
    pre_gate = jnp.einsum('thb,hbk->thk', blocks_in, cube_a).reshape(length, hidden_width) + bias_a.astype(jnp.float32)
    pre_input = jnp.einsum('thb,hbk->thk', blocks_in, cube_x).reshape(length, hidden_width) + bias_x.astype(jnp.float32)
    recur_gate = jax.nn.sigmoid(pre_gate)
    input_gate = jax.nn.sigmoid(pre_input)
    softened = jax.nn.softplus(decay_raw.astype(jnp.float32))
    log_decay = -8.0 * softened * recur_gate
    decay = jnp.exp(log_decay)
    scaled = jnp.sqrt(-jnp.expm1(2.0 * log_decay))
    values_f = values.astype(jnp.float32)
    drive = scaled * input_gate * values_f
    _, states = lax.associative_scan(linear_combine, (decay, drive), axis=0)
    zero_row = jnp.zeros((1, hidden_width), jnp.float32)
    earlier = jnp.concatenate([zero_row, states[:-1]], axis=0)
    coeffs = jnp.concatenate([decay[1:], zero_row], axis=0)
    _, adjoint = lax.associative_scan(linear_combine, (coeffs, upstream.astype(jnp.float32)), axis=0, reverse=True)
    grad_log = adjoint * earlier * decay - adjoint * input_gate * values_f * decay * decay / scaled
    delta_gate = (grad_log * (-8.0 * softened) * recur_gate * (1.0 - recur_gate)).astype(jnp.bfloat16)
    delta_input = (adjoint * scaled * values_f * input_gate * (1.0 - input_gate)).astype(jnp.bfloat16)
    delta_gate3 = delta_gate.astype(jnp.float32).reshape(length, heads, block)
    delta_input3 = delta_input.astype(jnp.float32).reshape(length, heads, block)
    back = jnp.einsum('thk,hbk->thb', delta_gate3, cube_a) + jnp.einsum('thk,hbk->thb', delta_input3, cube_x)
    input_grad = (adjoint * scaled * input_gate + back.reshape(length, hidden_width)).astype(jnp.bfloat16)
    grad_wa = jnp.einsum('thb,thk->hbk', blocks_in, delta_gate3).reshape(hidden_width, block)
    grad_wx = jnp.einsum('thb,thk->hbk', blocks_in, delta_input3).reshape(hidden_width, block)
    grad_ba = lax.optimization_barrier(jnp.sum(delta_gate.astype(jnp.float32), axis=0))
    grad_bx = lax.optimization_barrier(jnp.sum(delta_input.astype(jnp.float32), axis=0))
    grad_soft = lax.optimization_barrier(jnp.sum(grad_log * (-8.0 * recur_gate), axis=0))
    return (input_grad, (grad_wa, grad_wx, grad_ba, grad_bx, grad_soft))

def reference(inputs, cotangent, gate_a_weight, gate_x_weight, gate_a_bias, gate_x_bias, decay_param):
    seq_count = TOKENS // TOK_DEV
    seq_inputs = inputs.reshape(seq_count, TOK_DEV, R)
    seq_cotan = cotangent.reshape(seq_count, TOK_DEV, R)

    def visit(totals, pair):
        grad_in, terms = sequence_backward(pair[0], pair[1], gate_a_weight, gate_x_weight, gate_a_bias, gate_x_bias, decay_param)
        return (jax.tree.map(lambda left, right: left + right, totals, terms), grad_in)
    start = (jnp.zeros((R, B), jnp.float32), jnp.zeros((R, B), jnp.float32), jnp.zeros((R,), jnp.float32), jnp.zeros((R,), jnp.float32), jnp.zeros((R,), jnp.float32))
    totals, grads_in = lax.scan(visit, start, (seq_inputs, seq_cotan))
    factor = 1.0 / jnp.sqrt(jnp.float32(TOKENS))
    decay_grad = totals[4] * jax.nn.sigmoid(decay_param.astype(jnp.float32)) * factor
    return (grads_in.reshape(TOKENS, R), totals[0] * factor, totals[1] * factor, totals[2] * factor, totals[3] * factor, decay_grad)
```

```python
import jax
import jax.numpy as jnp
from jax import lax
from jax.experimental import pallas as pl
from jax.experimental.pallas import tpu as pltpu
from jax.sharding import Mesh
from jax.sharding import PartitionSpec as P

BLK = 176
PAIR = 384
WROWS = 192
NZ, NY, NC = 8, 2, 2
NQ = NY * NC
NPAIR = NZ // 2
SEQ = 128
ROWS = NQ * SEQ
VMEM_LIMIT = 56 * 1024 * 1024


def lanes_of(shape):
    return lax.broadcasted_iota(jnp.int32, shape, len(shape) - 1)


def pack_kernel(ones_lane, who_ref, x_ref, *outs):
    who = who_ref[0]
    width = x_ref.shape[1]
    lane = lanes_of((SEQ, PAIR))

    def head_at(head, target):
        start = head * BLK
        base = min(start // 128 * 128, width - PAIR)
        window = x_ref[:, base : base + PAIR].astype(jnp.float32)
        return pltpu.roll(window, (target - (start - base)) % PAIR, 1)

    for p in range(NPAIR):
        for q in range(NQ):
            first = head_at(2 * NQ * p + q, 0)
            second = head_at(2 * NQ * p + NQ + q, BLK)
            fill = jnp.where(lane == 2 * BLK, ones_lane, 0.0)
            both = jnp.where(lane < BLK, first, jnp.where(lane < 2 * BLK, second, fill))
            both = both.astype(jnp.bfloat16)
            for k in range(NQ):

                @pl.when((who ^ k) == q)
                def _():
                    outs[k][:, p * PAIR : (p + 1) * PAIR] = both


def unpack_kernel(who_ref, *refs):
    who = who_ref[0]
    ins, out = refs[:NQ], refs[NQ]
    lane = lanes_of((SEQ, PAIR))
    for p in range(NPAIR):
        acc = [None] * (2 * NQ * BLK // 128)
        for q in range(NQ):
            slot = who ^ q
            val = ins[0][:, p * PAIR : (p + 1) * PAIR].astype(jnp.float32)
            for k in range(1, NQ):
                other = ins[k][:, p * PAIR : (p + 1) * PAIR].astype(jnp.float32)
                val = jnp.where(slot == k, other, val)
            for i in range(2):
                start = (i * NQ + q) * BLK
                base = min(start // 128 * 128, 2 * NQ * BLK - PAIR)
                off = start - base
                moved = pltpu.roll(val, (off - i * BLK) % PAIR, 1)
                moved = jnp.where((lane >= off) & (lane < off + BLK), moved, 0.0)
                for j in range(PAIR // 128):
                    if base + j * 128 < start + BLK and base + (j + 1) * 128 > start:
                        b = base // 128 + j
                        piece = moved[:, j * 128 : (j + 1) * 128]
                        acc[b] = piece if acc[b] is None else acc[b] + piece
        for b, block in enumerate(acc):
            at = p * 2 * NQ * BLK + b * 128
            out[:, at : at + 128] = block.astype(jnp.bfloat16)


def sigmoid(pre):
    base = 1.0 + jnp.exp(jnp.minimum(-pre, 80.0))
    rough = pl.reciprocal(base, approx=True)
    return rough * (2.0 - base * rough)


def one_minus_exp(log_a):
    series = -1.0 / 720.0
    for c in (-1.0 / 120.0, -1.0 / 24.0, -1.0 / 6.0, -0.5, -1.0):
        series = series * log_a + c
    return jnp.where(log_a > -0.25, series * log_a, 1.0 - jnp.exp(log_a))


CHUNK = 32


def main_kernel(factor, *refs):
    xs, cots = refs[:NQ], refs[NQ : 2 * NQ]
    w_ref = refs[2 * NQ]
    outs = refs[2 * NQ + 1 : 3 * NQ + 1]
    g_ref = refs[3 * NQ + 1]
    (wa, wx, x_all, da, dx, rg_s, e1_s, f1_s, g_s, a_s, d_s, c_s, dec_s, acc_s) = refs[3 * NQ + 2 :]
    nblk = PAIR // 128

    lane = lanes_of((WROWS, PAIR))
    w0 = w_ref[0].astype(jnp.float32)
    w1 = w_ref[1].astype(jnp.float32)
    low, high = lane < BLK, (lane >= BLK) & (lane < 2 * BLK)
    tail = jnp.zeros((2 * PAIR - 4 * BLK - 2 * (WROWS - BLK), PAIR), jnp.float32)[: PAIR - BLK - WROWS]
    parts = (
        (wa, jnp.where(low, w0, 0.0), jnp.where(high, pltpu.roll(w1, BLK, 1), 0.0)),
        (wx, jnp.where(low, pltpu.roll(w0, PAIR - BLK, 1), 0.0), jnp.where(high, w1, 0.0)),
    )
    for dst, a0, a1 in parts:
        dst[0:BLK, :] = a0[:BLK].astype(jnp.bfloat16)
        dst[BLK : 2 * BLK, :] = a1[:BLK].astype(jnp.bfloat16)
        dst[2 * BLK : BLK + WROWS, :] = (a0[BLK:] + a1[BLK:]).astype(jnp.bfloat16)
        dst[BLK + WROWS :, :] = tail.astype(jnp.bfloat16)
    dec = parts[0][1][BLK + 1 : BLK + 2] + parts[0][2][BLK + 1 : BLK + 2]
    soft = jnp.maximum(dec, 0.0) + jnp.log1p(jnp.exp(-jnp.abs(dec)))
    dec_s[...] = -8.0 * jnp.broadcast_to(soft, (8, PAIR))

    for s in range(NQ):
        rows = slice(s * SEQ, (s + 1) * SEQ)
        x_all[rows, :] = xs[s][...]
        pre_a = jnp.dot(xs[s][...], wa[...], preferred_element_type=jnp.float32)
        pre_x = jnp.dot(xs[s][...], wx[...], preferred_element_type=jnp.float32)
        for k in range(nblk):
            rg_s[k, rows, :] = pre_a[:, k * 128 : (k + 1) * 128]
            e1_s[k, rows, :] = pre_x[:, k * 128 : (k + 1) * 128]

    for k in range(nblk):
        coef = dec_s[0:1, k * 128 : (k + 1) * 128]
        for s in range(NQ):

            def gates(i, _, k=k, s=s, coef=coef):
                off = pl.multiple_of(i * CHUNK, CHUNK)
                rows = pl.ds(s * SEQ + off, CHUNK)
                x = xs[s][pl.ds(off, CHUNK), k * 128 : (k + 1) * 128].astype(jnp.float32)
                cot = cots[s][pl.ds(off, CHUNK), k * 128 : (k + 1) * 128].astype(jnp.float32)
                rgate = sigmoid(rg_s[k, rows, :])
                igate = sigmoid(e1_s[k, rows, :])
                less = one_minus_exp(coef * rgate)
                a = 1.0 - less
                var = less * (1.0 + a)
                inv = lax.rsqrt(var)
                scale = var * inv
                ix = igate * x
                drive = scale * ix
                c_s[k, rows, :] = cot
                rg_s[k, rows, :] = rgate
                a_s[k, rows, :] = a
                d_s[k, rows, :] = drive
                e1_s[k, rows, :] = ix * (a * inv)
                f1_s[k, rows, :] = drive * (1.0 - igate)
                g_s[k, rows, :] = scale * igate
                return 0

            lax.fori_loop(0, SEQ // CHUNK, gates, 0)

    def scan(t, carry):
        state, back = carry
        state, back = list(state), list(back)
        u = SEQ - 1 - t
        for k in range(nblk):
            here = pl.ds(t, NQ, stride=SEQ)
            a, d = a_s[k, here, :], d_s[k, here, :]
            d_s[k, here, :] = state[k]
            state[k] = a * state[k] + d
        for k in range(nblk):
            here = pl.ds(u, NQ, stride=SEQ)
            adj = c_s[k, here, :] + back[k]
            c_s[k, here, :] = adj
            back[k] = a_s[k, here, :] * adj
        return tuple(state), tuple(back)

    zero = tuple(jnp.zeros((NQ, 128), jnp.float32) for _ in range(nblk))
    lax.fori_loop(0, SEQ, scan, (zero, zero), unroll=8)

    for k in range(nblk):
        coef = dec_s[0:1, k * 128 : (k + 1) * 128]
        acc_s[:, k * 128 : (k + 1) * 128] = jnp.zeros((8, 128), jnp.float32)

        def deltas(i, _, k=k, coef=coef):
            rows = pl.ds(pl.multiple_of(i * CHUNK, CHUNK), CHUNK)
            adj, rgate = c_s[k, rows, :], rg_s[k, rows, :]
            q = adj * a_s[k, rows, :] * (d_s[k, rows, :] - e1_s[k, rows, :]) * rgate
            part = q[0:8]
            for j in range(1, CHUNK // 8):
                part = part + q[j * 8 : (j + 1) * 8]
            acc_s[:, k * 128 : (k + 1) * 128] += part
            da[rows, k * 128 : (k + 1) * 128] = (q * (coef - coef * rgate)).astype(jnp.bfloat16)
            dx[rows, k * 128 : (k + 1) * 128] = (adj * f1_s[k, rows, :]).astype(jnp.bfloat16)
            g_s[k, rows, :] = adj * g_s[k, rows, :]
            return 0

        lax.fori_loop(0, ROWS // CHUNK, deltas, 0)

    nt = (((1,), (1,)), ((), ()))
    tn = (((0,), (0,)), ((), ()))
    for s in range(NQ):
        rows = slice(s * SEQ, (s + 1) * SEQ)
        back = lax.dot_general(da[rows, :], wa[...], nt, preferred_element_type=jnp.float32)
        back += lax.dot_general(dx[rows, :], wx[...], nt, preferred_element_type=jnp.float32)
        for k in range(nblk):
            cols = slice(k * 128, (k + 1) * 128)
            outs[s][:, cols] = (back[:, cols] + g_s[k, rows, :]).astype(jnp.bfloat16)

    grad_a = lax.dot_general(x_all[...], da[...], tn, preferred_element_type=jnp.float32) * factor
    grad_x = lax.dot_general(x_all[...], dx[...], tn, preferred_element_type=jnp.float32) * factor
    dec_row = jnp.sum(acc_s[...], axis=0, keepdims=True) * (-8.0 * factor)
    extra = WROWS - BLK
    row16 = lax.broadcasted_iota(jnp.int32, (extra, PAIR), 0)
    low_a = jnp.where(row16 == 1, dec_row, grad_a[2 * BLK : 2 * BLK + extra])
    low_x = grad_x[2 * BLK : 2 * BLK + extra]
    head0_a = jnp.concatenate([grad_a[:BLK], low_a], axis=0)
    head0_x = jnp.concatenate([grad_x[:BLK], low_x], axis=0)
    head1_a = jnp.concatenate([grad_a[BLK : 2 * BLK], low_a], axis=0)
    head1_x = jnp.concatenate([grad_x[BLK : 2 * BLK], low_x], axis=0)
    first = jnp.where(low, head0_a, jnp.where(high, pltpu.roll(head0_x, BLK, 1), 0.0))
    second = jnp.where(low, pltpu.roll(head1_a, PAIR - BLK, 1), jnp.where(high, head1_x, 0.0))
    g_ref[0] = first.astype(g_ref.dtype)
    g_ref[1] = second.astype(g_ref.dtype)


def params():
    return pltpu.CompilerParams(vmem_limit_bytes=VMEM_LIMIT)


def pack(ones_lane, who, x, interpret=False):
    import functools

    return pl.pallas_call(
        functools.partial(pack_kernel, ones_lane),
        out_shape=[jax.ShapeDtypeStruct((SEQ, NPAIR * PAIR), jnp.bfloat16)] * NQ,
        in_specs=[pl.BlockSpec(memory_space=pltpu.SMEM), pl.BlockSpec(memory_space=pltpu.VMEM)],
        out_specs=[pl.BlockSpec(memory_space=pltpu.VMEM)] * NQ,
        compiler_params=params(),
        interpret=interpret,
    )(who, x)


def unpack(who, pieces, interpret=False):
    return pl.pallas_call(
        unpack_kernel,
        out_shape=jax.ShapeDtypeStruct((SEQ, NZ * NQ * BLK), jnp.bfloat16),
        in_specs=[pl.BlockSpec(memory_space=pltpu.SMEM)] + [pl.BlockSpec(memory_space=pltpu.VMEM)] * NQ,
        out_specs=pl.BlockSpec(memory_space=pltpu.VMEM),
        compiler_params=params(),
        interpret=interpret,
    )(who, *pieces)


def main_call(factor, xs, cots, w, grad_dtype=jnp.bfloat16, interpret=False):
    import functools

    npair = w.shape[0] // 2
    f32, bf16 = jnp.float32, jnp.bfloat16
    big = pltpu.VMEM((PAIR // 128, ROWS, 128), f32)
    tok = pl.BlockSpec((SEQ, PAIR), lambda p: (0, p))
    par = pl.BlockSpec((2, WROWS, PAIR), lambda p: (p, 0, 0))
    return pl.pallas_call(
        functools.partial(main_kernel, factor),
        grid=(npair,),
        out_shape=[jax.ShapeDtypeStruct((SEQ, npair * PAIR), bf16)] * NQ
        + [jax.ShapeDtypeStruct((2 * npair, WROWS, PAIR), grad_dtype)],
        in_specs=[tok] * (2 * NQ) + [par],
        out_specs=[tok] * NQ + [par],
        scratch_shapes=[
            pltpu.VMEM((PAIR, PAIR), bf16),
            pltpu.VMEM((PAIR, PAIR), bf16),
            pltpu.VMEM((ROWS, PAIR), bf16),
            pltpu.VMEM((ROWS, PAIR), bf16),
            pltpu.VMEM((ROWS, PAIR), bf16),
            big, big, big, big, big, big, big,
            pltpu.VMEM((8, PAIR), f32),
            pltpu.VMEM((8, PAIR), f32),
        ],
        compiler_params=params(),
        interpret=interpret,
    )(*xs, *cots, w)


def ring(n, k):
    return [(i, (i + k) % n) for i in range(n)]


def exchange(pieces):
    got = [pieces[0]]
    for k in range(1, NQ):
        perm = [(q, q ^ k) for q in range(NQ)]
        got.append(lax.ppermute(pieces[k], ("yh", "core"), perm))
    return got


def per_device(inputs, cotangent, wa, wx, ba, bx, decay):
    bf16, f32 = jnp.bfloat16, jnp.float32
    who = (lax.axis_index("yh") * NC + lax.axis_index("core")).astype(jnp.int32).reshape(1)
    zero = jnp.zeros((BLK,), bf16)
    tail = jnp.zeros((WROWS - BLK - 2, 2 * BLK), bf16)
    body = jnp.concatenate(
        [
            jnp.concatenate([wa, wx], axis=1),
            jnp.concatenate([ba, bx])[None],
            jnp.concatenate([decay, zero])[None],
            tail,
        ],
        axis=0,
    )
    mine = jnp.pad(body, ((0, 0), (0, PAIR - 2 * BLK)))
    weights = lax.all_gather(mine, "z")
    xs = exchange(pack(1.0, who, inputs))
    cots = exchange(pack(0.0, who, cotangent))
    total = SEQ * lax.axis_size("cuts") * lax.axis_size("z") * NQ
    res = main_call(float(total) ** -0.5, xs, cots, weights, f32)
    input_grad = unpack(who, exchange(res[:NQ]))
    share = lax.psum_scatter(res[NQ], "z", scatter_dimension=0, tiled=True)[0].astype(bf16)
    n = lax.axis_size("cuts")
    got = [share] + [lax.ppermute(share, "cuts", ring(n, k)) for k in range(1, n)]
    full = sum(g.astype(f32) for g in got)
    own = jax.nn.sigmoid(decay.astype(f32))
    return (
        input_grad,
        full[:BLK, :BLK],
        full[:BLK, BLK : 2 * BLK],
        full[BLK, :BLK],
        full[BLK, BLK : 2 * BLK],
        full[BLK + 1, :BLK] * own,
    )


def solution(mesh):
    sizes = dict(mesh.shape)
    fine = Mesh(mesh.devices.reshape(sizes["cuts"], NZ, NY, NC), ("cuts", "z", "yh", "core"))
    zero = ("z", "yh", "core")
    rows = P(("cuts",) + zero, None)
    return jax.shard_map(
        per_device,
        mesh=fine,
        in_specs=(rows, rows, P(zero, None), P(zero, None), P(zero), P(zero), P(zero)),
        out_specs=(rows, P(zero, None), P(zero, None), P(zero), P(zero), P(zero)),
        check_vma=False,
    )
```

```python
import functools

import jax
import jax.numpy as jnp
from jax import lax
from jax.experimental import pallas as pl
from jax.experimental.pallas import tpu as pltpu
from jax.sharding import Mesh
from jax.sharding import PartitionSpec as P

BLK = 176
TWO = 2 * BLK
WROWS = 192
WCOLS = 384
NZ, NY, NC = 8, 2, 2
NQ = NY * NC
NI = 8
SEQ = 128
NSEQ = NI * NQ
STEP = 8
VMEM_LIMIT = 56 * 1024 * 1024


def pack_kernel(z_ref, x_ref, out_ref, turned):
    half = pl.program_id(1)

    @pl.when(half == 0)
    def _():
        turned[...] = x_ref[...].T

    rows = pl.ds(pl.multiple_of(half * NQ * BLK, 16), NQ * BLK)
    out_ref[...] = turned[rows, :].reshape(NQ, BLK, SEQ)


def unpack_kernel(z_ref, in_ref, out_ref, turned):
    half = pl.program_id(1)
    rows = pl.ds(pl.multiple_of(half * NQ * BLK, 16), NQ * BLK)
    turned[rows, :] = in_ref[...].reshape(NQ * BLK, SEQ)

    @pl.when(half == 1)
    def _():
        out_ref[...] = turned[...].T


def params():
    return pltpu.CompilerParams(vmem_limit_bytes=VMEM_LIMIT)


def turn_specs():
    wide = pl.BlockSpec((SEQ, 2 * NQ * BLK), lambda p, j, z: (0, p))
    tall = pl.BlockSpec((NQ, BLK, SEQ), lambda p, j, z: (lax.rem(2 * p + j + NZ - z[0], NZ), 0, 0))
    return wide, tall


def pack(z, x, interpret=False):
    wide, tall = turn_specs()
    return pl.pallas_call(
        pack_kernel,
        grid_spec=pltpu.PrefetchScalarGridSpec(
            num_scalar_prefetch=1,
            grid=(NZ // 2, 2),
            in_specs=[wide],
            out_specs=tall,
            scratch_shapes=[pltpu.VMEM((2 * NQ * BLK, SEQ), x.dtype)],
        ),
        out_shape=jax.ShapeDtypeStruct((NSEQ, BLK, SEQ), x.dtype),
        compiler_params=params(),
        interpret=interpret,
    )(z, x)


def unpack(z, y, interpret=False):
    wide, tall = turn_specs()
    return pl.pallas_call(
        unpack_kernel,
        grid_spec=pltpu.PrefetchScalarGridSpec(
            num_scalar_prefetch=1,
            grid=(NZ // 2, 2),
            in_specs=[tall],
            out_specs=wide,
            scratch_shapes=[pltpu.VMEM((2 * NQ * BLK, SEQ), y.dtype)],
        ),
        out_shape=jax.ShapeDtypeStruct((SEQ, NSEQ * BLK), y.dtype),
        compiler_params=params(),
        interpret=interpret,
    )(z, y)


def sigmoid(pre):
    base = 1.0 + jnp.exp(jnp.minimum(-pre, 80.0))
    rough = pl.reciprocal(base, approx=True)
    return rough * (2.0 - base * rough)


def one_minus_exp(log_a):
    series = -1.0 / 720.0
    for c in (-1.0 / 120.0, -1.0 / 24.0, -1.0 / 6.0, -0.5, -1.0):
        series = series * log_a + c
    return jnp.where(log_a > -0.25, series * log_a, 1.0 - jnp.exp(log_a))


CH = 16


def main_kernel(factor, x_ref, c_ref, w_ref, wt_ref, coef_ref, out_ref, g_ref, x_s, pre_s, d_s, q_s, g_s):
    step = pl.program_id(0)

    @pl.when(step == 0)
    def _():
        row = lax.broadcasted_iota(jnp.int32, (WROWS - BLK, STEP * SEQ), 0)
        x_s[BLK:, :] = jnp.where(row == 0, 1.0, 0.0).astype(x_s.dtype)
        q_s[...] = jnp.zeros_like(q_s)
        g_s[...] = jnp.zeros_like(g_s)

    for s in range(STEP):
        x_s[:BLK, s * SEQ : (s + 1) * SEQ] = x_ref[s]
    pre_s[...] = jnp.dot(wt_ref[...], x_s[...], preferred_element_type=jnp.float32)

    def one(s, _):
        cols = pl.ds(pl.multiple_of(s * SEQ, SEQ), SEQ)
        lane = lax.broadcasted_iota(jnp.int32, (CH, SEQ), 1)
        for r in range(0, BLK, CH):
            rows, more = slice(r, r + CH), slice(BLK + r, BLK + r + CH)
            coef = coef_ref[rows, :]
            x = x_ref[s, rows, :].astype(jnp.float32)
            adj = c_ref[s, rows, :].astype(jnp.float32)
            rgate = sigmoid(pre_s[rows, cols])
            igate = sigmoid(pre_s[more, cols])
            less = one_minus_exp(coef * rgate)
            a = 1.0 - less
            var = less * (1.0 + a)
            inv = lax.rsqrt(var)
            scale = var * inv
            ix = igate * x
            drive = scale * ix
            own = ix * (a * a * inv)
            a_first = jnp.where(lane == 0, 0.0, a)
            prod, state = a_first, drive
            for k in range(7):
                d = 1 << k
                adj = adj + pltpu.roll(prod * adj, SEQ - d, 1)
                state = state + prod * pltpu.roll(state, d, 1)
                if k < 6:
                    prod = prod * pltpu.roll(prod, d, 1)
            q = adj * (a_first * pltpu.roll(state, 1, 1) - own) * rgate
            q_s[rows, :] += q
            d_s[rows, cols] = (q * (coef - coef * rgate)).astype(jnp.bfloat16)
            d_s[more, cols] = (adj * (drive * (1.0 - igate))).astype(jnp.bfloat16)
            pre_s[rows, cols] = adj * (scale * igate)
        return 0

    lax.fori_loop(0, STEP, one, 0)

    back = jnp.dot(w_ref[:BLK, :TWO], d_s[...], preferred_element_type=jnp.float32)
    for s in range(STEP):
        cols = slice(s * SEQ, (s + 1) * SEQ)
        out_ref[s] = (back[:, cols] + pre_s[:BLK, cols]).astype(out_ref.dtype)
    nt = (((1,), (1,)), ((), ()))
    g_s[:, :TWO] += lax.dot_general(x_s[...], d_s[...], nt, preferred_element_type=jnp.float32)

    @pl.when(step == pl.num_programs(0) - 1)
    def _():
        g_ref[...] = (g_s[...] * factor).astype(g_ref.dtype)
        decay = jnp.sum(q_s[...].T, axis=0, keepdims=True) * (-8.0 * factor)
        tail = g_s[BLK:, :BLK] * factor
        row = lax.broadcasted_iota(jnp.int32, tail.shape, 0)
        g_ref[BLK:, :BLK] = jnp.where(row == 1, decay, tail).astype(g_ref.dtype)


def main_call(factor, x, c, w, wt, coef, grad_dtype=jnp.bfloat16, interpret=False):
    f32, bf16 = jnp.float32, jnp.bfloat16
    n = x.shape[0]
    tok = pl.BlockSpec((STEP, BLK, SEQ), lambda p: (p, 0, 0))
    full = lambda shape: pl.BlockSpec(shape, lambda p: (0, 0))
    return pl.pallas_call(
        functools.partial(main_kernel, factor),
        grid=(n // STEP,),
        out_shape=[
            jax.ShapeDtypeStruct((n, BLK, SEQ), bf16),
            jax.ShapeDtypeStruct((WROWS, WCOLS), grad_dtype),
        ],
        in_specs=[tok, tok, full((WROWS, WCOLS)), full((TWO, WROWS)), full((BLK, SEQ))],
        out_specs=[tok, full((WROWS, WCOLS))],
        scratch_shapes=[
            pltpu.VMEM((WROWS, STEP * SEQ), bf16),
            pltpu.VMEM((TWO, STEP * SEQ), f32),
            pltpu.VMEM((TWO, STEP * SEQ), bf16),
            pltpu.VMEM((BLK, SEQ), f32),
            pltpu.VMEM((WROWS, WCOLS), f32),
        ],
        compiler_params=params(),
        interpret=interpret,
    )(x, c, w, wt, coef)


def wire(wa, wx, ba, bx, decay):
    bf16 = jnp.bfloat16
    tail = jnp.zeros((WROWS - BLK - 2, TWO), bf16)
    body = jnp.concatenate(
        [
            jnp.concatenate([wa, wx], axis=1),
            jnp.concatenate([ba, bx])[None],
            jnp.concatenate([decay, jnp.zeros((BLK,), bf16)])[None],
            tail,
        ],
        axis=0,
    )
    return jnp.pad(body, ((0, 0), (0, WCOLS - TWO)))


def unwire(w):
    wt = w[:, :TWO].T
    coef = -8.0 * jax.nn.softplus(w[BLK + 1, :BLK].astype(jnp.float32))
    return wt, jnp.broadcast_to(coef[:, None], (BLK, SEQ))


def per_device(inputs, cotangent, wa, wx, ba, bx, decay):
    bf16, f32 = jnp.bfloat16, jnp.float32
    plane, line = ("cuts", "yh", "core"), ("cuts", "z")
    z = lax.axis_index("z").astype(jnp.int32).reshape(1)
    pairs = [(i, k, (k + i) % NZ) for i in range(NI) for k in range(NZ)]
    fetch = [(i * NZ + src, i * NZ + k) for i, k, src in pairs]
    home = [(b, a) for a, b in fetch]

    x = lax.all_to_all(pack(z, inputs), plane, 0, 0, tiled=True)
    w = lax.ppermute(wire(wa, wx, ba, bx, decay), line, fetch)
    c = lax.all_to_all(pack(z, cotangent), plane, 0, 0, tiled=True)
    wt, coef = unwire(w)
    total = SEQ * NSEQ * NZ
    out, grads = main_call(float(total) ** -0.5, x, c, w, wt, coef)
    input_grad = unpack(z, lax.all_to_all(out, plane, 0, 0, tiled=True))
    share = lax.ppermute(grads, line, home)
    parts = lax.all_to_all(jnp.broadcast_to(share, (NI, WROWS, WCOLS)), "cuts", 0, 0, tiled=True)
    full = jnp.sum(parts.astype(f32), axis=0)
    own = jax.nn.sigmoid(decay.astype(f32))
    return (
        input_grad,
        full[:BLK, :BLK],
        full[:BLK, BLK:TWO],
        full[BLK, :BLK],
        full[BLK, BLK:TWO],
        full[BLK + 1, :BLK] * own,
    )


def solution(mesh):
    fine = Mesh(mesh.devices.reshape(NI, NZ, NY, NC), ("cuts", "z", "yh", "core"))
    zero = ("z", "yh", "core")
    rows = P(("cuts",) + zero, None)
    return jax.shard_map(
        per_device,
        mesh=fine,
        in_specs=(rows, rows, P(zero, None), P(zero, None), P(zero), P(zero), P(zero)),
        out_specs=(rows, P(zero, None), P(zero, None), P(zero), P(zero), P(zero)),
        check_vma=False,
    )
```

```python
import functools

import jax
import jax.numpy as jnp
from jax import lax
from jax.experimental import pallas as pl
from jax.experimental.pallas import tpu as pltpu
from jax.sharding import Mesh
from jax.sharding import PartitionSpec as P

BLK = 176
TWO = 2 * BLK
WROWS = 192
WCOLS = 384
NZ, NY, NC = 8, 2, 2
NQ = NY * NC
NI = 8
SEQ = 128
NSEQ = NI * NQ
STEP = 8
VMEM_LIMIT = 56 * 1024 * 1024


def pack_kernel(z_ref, x_ref, c_ref, out_ref):
    first = z_ref[0] * NQ
    for k, ref in enumerate((x_ref, c_ref)):
        for p in range(NZ // 2):
            turned = ref[:, p * 2 * NQ * BLK : (p + 1) * 2 * NQ * BLK].T
            for h in range(2 * NQ):
                slot = lax.rem(2 * NQ * p + h + NSEQ - first, NSEQ)
                out_ref[slot, k * BLK : (k + 1) * BLK, :] = turned[h * BLK : (h + 1) * BLK, :]


def unpack_kernel(z_ref, in_ref, out_ref):
    first = z_ref[0] * NQ
    for p in range(NZ // 2):
        heads = [in_ref[lax.rem(2 * NQ * p + h + NSEQ - first, NSEQ)] for h in range(2 * NQ)]
        out_ref[:, p * 2 * NQ * BLK : (p + 1) * 2 * NQ * BLK] = jnp.concatenate(heads, axis=0).T


def params():
    return pltpu.CompilerParams(vmem_limit_bytes=VMEM_LIMIT)


SMEM = pl.BlockSpec(memory_space=pltpu.SMEM)
VMEM = pl.BlockSpec(memory_space=pltpu.VMEM)


def pack(z, x, c, interpret=False):
    return pl.pallas_call(
        pack_kernel,
        in_specs=[SMEM, VMEM, VMEM],
        out_specs=VMEM,
        out_shape=jax.ShapeDtypeStruct((NSEQ, TWO, SEQ), x.dtype),
        compiler_params=params(),
        interpret=interpret,
    )(z, x, c)


def unpack(z, y, interpret=False):
    return pl.pallas_call(
        unpack_kernel,
        in_specs=[SMEM, VMEM],
        out_specs=VMEM,
        out_shape=jax.ShapeDtypeStruct((SEQ, NSEQ * BLK), y.dtype),
        compiler_params=params(),
        interpret=interpret,
    )(z, y)


LN2 = 0.6931471805599453
LOG2E = 1.4426950408889634


def sigmoid(pre):
    base = 1.0 + jnp.exp2(jnp.minimum(pre * -LOG2E, 115.0))
    rough = pl.reciprocal(base, approx=True)
    return rough * (2.0 - base * rough)


def one_minus_square(u):
    series, power = 0.0, 1.0
    terms = []
    for k in range(1, 8):
        power = power * (2.0 * LN2) / k
        terms.append(-power)
    series = terms[-1]
    for t in terms[-2::-1]:
        series = series * u + t
    return series * u


def split(v):
    high = v.astype(jnp.bfloat16)
    return high, (v - high.astype(jnp.float32)).astype(jnp.bfloat16)


CH = 16


def main_kernel(
    factor, m_ref, w_ref, wt_ref, coef_ref, out_ref, g_ref,
    tri, x_s, pre_s, d_s, u_s, rest_s, own_s, f1_s, gain_s, drive_s, lh_s, log_s, fh_s, rh_s, fwd_s, rev_s, q_s, g_s,
):
    step = pl.program_id(0)
    f32, bf16 = jnp.float32, jnp.bfloat16

    @pl.when(step == 0)
    def _():
        row = lax.broadcasted_iota(jnp.int32, (WROWS - BLK, STEP * SEQ), 0)
        x_s[BLK:, :] = jnp.where(row == 0, 1.0, 0.0).astype(x_s.dtype)
        q_s[...] = jnp.zeros_like(q_s)
        g_s[...] = jnp.zeros_like(g_s)
        src = lax.broadcasted_iota(jnp.int32, (SEQ, SEQ), 0)
        dst = lax.broadcasted_iota(jnp.int32, (SEQ, SEQ), 1)
        for k, seen in enumerate((src <= dst, src < dst, src >= dst)):
            one = jnp.where(seen, 1.0, 0.0).astype(bf16)
            tri[k, :SEQ, :] = one
            tri[k, SEQ:, :] = one

    for s in range(STEP):
        x_s[:BLK, s * SEQ : (s + 1) * SEQ] = m_ref[s, :BLK, :]
    pre_s[...] = jnp.dot(wt_ref[...], x_s[...], preferred_element_type=f32)

    def each(body):
        def one(s, _):
            cols = pl.ds(pl.multiple_of(s * SEQ, SEQ), SEQ)
            for r in range(0, BLK, CH):
                body(s, r, cols, pl.ds(pl.multiple_of(s * BLK + r, 16), CH))
            return 0

        lax.fori_loop(0, STEP, one, 0)

    def gates(s, r, cols, at):
        x = m_ref[s, r : r + CH, :].astype(f32)
        rgate = sigmoid(pre_s[r : r + CH, cols])
        igate = sigmoid(pre_s[BLK + r : BLK + r + CH, cols])
        u = coef_ref[r : r + CH, :] * rgate
        var = one_minus_square(u)
        inv = lax.rsqrt(var)
        scale = var * inv
        ix = igate * x
        drive = scale * ix
        u_s[at, :] = u
        rest_s[at, :] = LN2 - LN2 * rgate
        own_s[at, :] = ix * (inv - scale)
        f1_s[at, :] = drive - drive * igate
        gain_s[at, :] = scale * igate
        drive_s[at, :] = drive
        lh_s[at, :SEQ], lh_s[at, SEQ:] = split(u)

    each(gates)
    log_s[...] = jnp.dot(lh_s[...], tri[0], preferred_element_type=f32)

    def weigh(s, r, cols, at):
        total = log_s[at, :]
        cot = m_ref[s, BLK + r : BLK + r + CH, :].astype(f32)
        fh_s[at, :SEQ], fh_s[at, SEQ:] = split(drive_s[at, :] * jnp.exp2(-total))
        rh_s[at, :SEQ], rh_s[at, SEQ:] = split(cot * jnp.exp2(total))

    each(weigh)
    fwd_s[...] = jnp.dot(fh_s[...], tri[1], preferred_element_type=f32)
    rev_s[...] = jnp.dot(rh_s[...], tri[2], preferred_element_type=f32)

    def deltas(s, r, cols, at):
        total = log_s[at, :]
        adj = rev_s[at, :] * jnp.exp2(-total)
        dlog = adj * (fwd_s[at, :] * jnp.exp2(total) - own_s[at, :])
        v = dlog * u_s[at, :]
        q_s[r : r + CH, :] += v
        d_s[r : r + CH, cols] = (v * rest_s[at, :]).astype(bf16)
        d_s[BLK + r : BLK + r + CH, cols] = (adj * f1_s[at, :]).astype(bf16)
        pre_s[r : r + CH, cols] = adj * gain_s[at, :]

    each(deltas)

    back = jnp.dot(w_ref[:BLK, :TWO], d_s[...], preferred_element_type=f32)
    for s in range(STEP):
        cols = slice(s * SEQ, (s + 1) * SEQ)
        out_ref[s] = (back[:, cols] + pre_s[:BLK, cols]).astype(out_ref.dtype)
    nt = (((1,), (1,)), ((), ()))
    g_s[:, :TWO] += lax.dot_general(x_s[...], d_s[...], nt, preferred_element_type=f32)

    @pl.when(step == pl.num_programs(0) - 1)
    def _():
        g_ref[...] = (g_s[...] * factor).astype(g_ref.dtype)
        decay = jnp.sum((q_s[...] / coef_ref[...]).T, axis=0, keepdims=True) * (-8.0 * factor)
        tail = g_s[BLK:, :BLK] * factor
        row = lax.broadcasted_iota(jnp.int32, tail.shape, 0)
        g_ref[BLK:, :BLK] = jnp.where(row == 1, decay, tail).astype(g_ref.dtype)


def main_call(factor, m, w, wt, coef, grad_dtype=jnp.bfloat16, interpret=False):
    f32, bf16 = jnp.float32, jnp.bfloat16
    n = m.shape[0]
    tok = lambda rows: pl.BlockSpec((STEP, rows, SEQ), lambda p: (p, 0, 0))
    full = lambda shape: pl.BlockSpec(shape, lambda p: (0, 0))
    wide = lambda kind: pltpu.VMEM((STEP * BLK, 2 * SEQ), kind)
    flat = pltpu.VMEM((STEP * BLK, SEQ), f32)
    return pl.pallas_call(
        functools.partial(main_kernel, factor),
        grid=(n // STEP,),
        out_shape=[
            jax.ShapeDtypeStruct((n, BLK, SEQ), bf16),
            jax.ShapeDtypeStruct((WROWS, WCOLS), grad_dtype),
        ],
        in_specs=[tok(TWO), full((WROWS, WCOLS)), full((TWO, WROWS)), full((BLK, SEQ))],
        out_specs=[tok(BLK), full((WROWS, WCOLS))],
        scratch_shapes=[
            pltpu.VMEM((3, 2 * SEQ, SEQ), bf16),
            pltpu.VMEM((WROWS, STEP * SEQ), bf16),
            pltpu.VMEM((TWO, STEP * SEQ), f32),
            pltpu.VMEM((TWO, STEP * SEQ), bf16),
            flat, flat, flat, flat, flat, flat,
            wide(bf16), flat, wide(bf16), wide(bf16), flat, flat,
            pltpu.VMEM((BLK, SEQ), f32),
            pltpu.VMEM((WROWS, WCOLS), f32),
        ],
        compiler_params=params(),
        interpret=interpret,
    )(m, w, wt, coef)


def wire(wa, wx, ba, bx, decay):
    bf16 = jnp.bfloat16
    tail = jnp.zeros((WROWS - BLK - 2, TWO), bf16)
    body = jnp.concatenate(
        [
            jnp.concatenate([wa, wx], axis=1),
            jnp.concatenate([ba, bx])[None],
            jnp.concatenate([decay, jnp.zeros((BLK,), bf16)])[None],
            tail,
        ],
        axis=0,
    )
    return jnp.pad(body, ((0, 0), (0, WCOLS - TWO)))


def unwire(w):
    wt = w[:, :TWO].T
    coef = (-8.0 * LOG2E) * jax.nn.softplus(w[BLK + 1, :BLK].astype(jnp.float32))
    return wt, jnp.broadcast_to(coef[:, None], (BLK, SEQ))


def per_device(inputs, cotangent, wa, wx, ba, bx, decay):
    bf16, f32 = jnp.bfloat16, jnp.float32
    plane, line = ("cuts", "yh", "core"), ("cuts", "z")
    z = lax.axis_index("z").astype(jnp.int32).reshape(1)
    pairs = [(i, k, (k + i) % NZ) for i in range(NI) for k in range(NZ)]
    fetch = [(i * NZ + src, i * NZ + k) for i, k, src in pairs]
    home = [(b, a) for a, b in fetch]

    sent = pack(z, inputs, cotangent)
    got = lax.all_to_all(sent, plane, 0, 0, tiled=True)
    w = lax.ppermute(wire(wa, wx, ba, bx, decay), line, fetch)
    wt, coef = unwire(w)
    total = SEQ * NSEQ * NZ
    out, grads = main_call(float(total) ** -0.5, got, w, wt, coef)
    input_grad = unpack(z, lax.all_to_all(out, plane, 0, 0, tiled=True))
    share = lax.ppermute(grads, line, home)
    parts = [share]
    for k in range(1, NI):
        parts.append(lax.ppermute(share, "cuts", [(i, (i + k) % NI) for i in range(NI)]))
    full = sum(p.astype(f32) for p in parts)
    own = jax.nn.sigmoid(decay.astype(f32))
    return (
        input_grad,
        full[:BLK, :BLK],
        full[:BLK, BLK:TWO],
        full[BLK, :BLK],
        full[BLK, BLK:TWO],
        full[BLK + 1, :BLK] * own,
    )


def solution(mesh):
    fine = Mesh(mesh.devices.reshape(NI, NZ, NY, NC), ("cuts", "z", "yh", "core"))
    zero = ("z", "yh", "core")
    rows = P(("cuts",) + zero, None)
    return jax.shard_map(
        per_device,
        mesh=fine,
        in_specs=(rows, rows, P(zero, None), P(zero, None), P(zero), P(zero), P(zero)),
        out_specs=(rows, P(zero, None), P(zero, None), P(zero), P(zero), P(zero)),
        check_vma=False,
    )
```

```python
import functools

import jax
import jax.numpy as jnp
from jax import lax
from jax.experimental import pallas as pl
from jax.experimental.pallas import tpu as pltpu
from jax.sharding import Mesh
from jax.sharding import PartitionSpec as P

BLK = 176
TWO = 2 * BLK
WROWS = 192
WCOLS = 384
NZ, NY, NC = 8, 2, 2
NQ = NY * NC
NI = 8
SEQ = 128
NSEQ = NI * NQ
STEP = 8
VMEM_LIMIT = 56 * 1024 * 1024


def pack_kernel(z_ref, x_ref, after_ref, out_ref):
    first = z_ref[0] * NQ
    for p in range(NZ // 2):
        turned = x_ref[:, p * 2 * NQ * BLK : (p + 1) * 2 * NQ * BLK].T
        for h in range(2 * NQ):
            slot = lax.rem(2 * NQ * p + h + NSEQ - first, NSEQ)
            out_ref[slot] = turned[h * BLK : (h + 1) * BLK, :]


def unpack_kernel(z_ref, in_ref, out_ref):
    first = z_ref[0] * NQ
    for p in range(NZ // 2):
        heads = [in_ref[lax.rem(2 * NQ * p + h + NSEQ - first, NSEQ)] for h in range(2 * NQ)]
        out_ref[:, p * 2 * NQ * BLK : (p + 1) * 2 * NQ * BLK] = jnp.concatenate(heads, axis=0).T


def params():
    return pltpu.CompilerParams(vmem_limit_bytes=VMEM_LIMIT)


SMEM = pl.BlockSpec(memory_space=pltpu.SMEM)
VMEM = pl.BlockSpec(memory_space=pltpu.VMEM)


def pack(z, x, after, interpret=False):
    return pl.pallas_call(
        pack_kernel,
        in_specs=[SMEM, VMEM, pl.BlockSpec(memory_space=pl.ANY)],
        out_specs=VMEM,
        out_shape=jax.ShapeDtypeStruct((NSEQ, BLK, SEQ), x.dtype),
        compiler_params=params(),
        interpret=interpret,
    )(z, x, after)


def unpack(z, y, interpret=False):
    return pl.pallas_call(
        unpack_kernel,
        in_specs=[SMEM, VMEM],
        out_specs=VMEM,
        out_shape=jax.ShapeDtypeStruct((SEQ, NSEQ * BLK), y.dtype),
        compiler_params=params(),
        interpret=interpret,
    )(z, y)


LN2 = 0.6931471805599453
LOG2E = 1.4426950408889634


def sigmoid(pre):
    base = 1.0 + jnp.exp2(jnp.minimum(pre * -LOG2E, 115.0))
    rough = pl.reciprocal(base, approx=True)
    return rough * (2.0 - base * rough)


def one_minus_square(u):
    series, power = 0.0, 1.0
    terms = []
    for k in range(1, 8):
        power = power * (2.0 * LN2) / k
        terms.append(-power)
    series = terms[-1]
    for t in terms[-2::-1]:
        series = series * u + t
    return series * u


def split(v):
    high = v.astype(jnp.bfloat16)
    return high, (v - high.astype(jnp.float32)).astype(jnp.bfloat16)


CH = 16


def each(body):
    def one(s, _):
        cols = pl.ds(pl.multiple_of(s * SEQ, SEQ), SEQ)
        for r in range(0, BLK, CH):
            body(s, r, cols, pl.ds(pl.multiple_of(s * BLK + r, 16), CH))
        return 0

    lax.fori_loop(0, STEP, one, 0)


def fill_triangle(tri, seen):
    src = lax.broadcasted_iota(jnp.int32, (SEQ, SEQ), 0)
    dst = lax.broadcasted_iota(jnp.int32, (SEQ, SEQ), 1)
    one = jnp.where(seen(src, dst), 1.0, 0.0).astype(jnp.bfloat16)
    tri[:SEQ, :] = one
    tri[SEQ:, :] = one


def fill_ones_row(x_s):
    row = lax.broadcasted_iota(jnp.int32, (WROWS - BLK, STEP * SEQ), 0)
    x_s[BLK:, :] = jnp.where(row == 0, 1.0, 0.0).astype(x_s.dtype)


def forward_kernel(
    x_ref, wt_ref, coef_ref, log_ref, a1_ref, v1_ref, f1_ref, gain_ref,
    upto, before, x_s, pre_s, u_s, rest_s, own_s, drive_s, lh_s, log_s, fh_s, fwd_s,
):
    f32, bf16 = jnp.float32, jnp.bfloat16

    @pl.when(pl.program_id(0) == 0)
    def _():
        fill_ones_row(x_s)
        fill_triangle(upto, lambda src, dst: src <= dst)
        fill_triangle(before, lambda src, dst: src < dst)

    for s in range(STEP):
        x_s[:BLK, s * SEQ : (s + 1) * SEQ] = x_ref[s]
    pre_s[...] = jnp.dot(wt_ref[...], x_s[...], preferred_element_type=f32)

    def gates(s, r, cols, at):
        x = x_ref[s, r : r + CH, :].astype(f32)
        rgate = sigmoid(pre_s[r : r + CH, cols])
        igate = sigmoid(pre_s[BLK + r : BLK + r + CH, cols])
        u = coef_ref[r : r + CH, :] * rgate
        var = one_minus_square(u)
        inv = lax.rsqrt(var)
        scale = var * inv
        ix = igate * x
        drive = scale * ix
        u_s[at, :] = u
        rest_s[at, :] = LN2 - LN2 * rgate
        own_s[at, :] = ix * (inv - scale)
        drive_s[at, :] = drive
        f1_ref[s, r : r + CH, :] = drive - drive * igate
        gain_ref[s, r : r + CH, :] = scale * igate
        lh_s[at, :SEQ], lh_s[at, SEQ:] = split(u)

    each(gates)
    log_s[...] = jnp.dot(lh_s[...], upto[...], preferred_element_type=f32)

    def weigh(s, r, cols, at):
        total = log_s[at, :]
        log_ref[s, r : r + CH, :] = total
        fh_s[at, :SEQ], fh_s[at, SEQ:] = split(drive_s[at, :] * jnp.exp2(-total))

    each(weigh)
    fwd_s[...] = jnp.dot(fh_s[...], before[...], preferred_element_type=f32)

    def factors(s, r, cols, at):
        v1 = (fwd_s[at, :] * jnp.exp2(log_s[at, :]) - own_s[at, :]) * u_s[at, :]
        v1_ref[s, r : r + CH, :] = v1
        a1_ref[s, r : r + CH, :] = v1 * rest_s[at, :]

    each(factors)


def backward_kernel(
    factor, x_ref, c_ref, log_ref, a1_ref, v1_ref, f1_ref, gain_ref, w_ref, coef_ref, out_ref, g_ref,
    after, x_s, d_s, rh_s, rev_s, term_s, q_s, g_s,
):
    step = pl.program_id(0)
    f32, bf16 = jnp.float32, jnp.bfloat16

    @pl.when(step == 0)
    def _():
        fill_ones_row(x_s)
        fill_triangle(after, lambda src, dst: src >= dst)
        q_s[...] = jnp.zeros_like(q_s)
        g_s[...] = jnp.zeros_like(g_s)

    for s in range(STEP):
        x_s[:BLK, s * SEQ : (s + 1) * SEQ] = x_ref[s]

    def weigh(s, r, cols, at):
        cot = c_ref[s, r : r + CH, :].astype(f32)
        rh_s[at, :SEQ], rh_s[at, SEQ:] = split(cot * jnp.exp2(log_ref[s, r : r + CH, :]))

    each(weigh)
    rev_s[...] = jnp.dot(rh_s[...], after[...], preferred_element_type=f32)

    def deltas(s, r, cols, at):
        adj = rev_s[at, :] * jnp.exp2(-log_ref[s, r : r + CH, :])
        q_s[r : r + CH, :] += adj * v1_ref[s, r : r + CH, :]
        d_s[r : r + CH, cols] = (adj * a1_ref[s, r : r + CH, :]).astype(bf16)
        d_s[BLK + r : BLK + r + CH, cols] = (adj * f1_ref[s, r : r + CH, :]).astype(bf16)
        term_s[r : r + CH, cols] = adj * gain_ref[s, r : r + CH, :]

    each(deltas)

    back = jnp.dot(w_ref[:BLK, :TWO], d_s[...], preferred_element_type=f32)
    for s in range(STEP):
        cols = slice(s * SEQ, (s + 1) * SEQ)
        out_ref[s] = (back[:, cols] + term_s[:, cols]).astype(out_ref.dtype)
    nt = (((1,), (1,)), ((), ()))
    g_s[:, :TWO] += lax.dot_general(x_s[...], d_s[...], nt, preferred_element_type=f32)

    @pl.when(step == pl.num_programs(0) - 1)
    def _():
        g_ref[...] = (g_s[...] * factor).astype(g_ref.dtype)
        decay = jnp.sum((q_s[...] / coef_ref[...]).T, axis=0, keepdims=True) * (-8.0 * factor)
        tail = g_s[BLK:, :BLK] * factor
        row = lax.broadcasted_iota(jnp.int32, tail.shape, 0)
        g_ref[BLK:, :BLK] = jnp.where(row == 1, decay, tail).astype(g_ref.dtype)


TOK = pl.BlockSpec((STEP, BLK, SEQ), lambda p: (p, 0, 0))


def full(*shape):
    return pl.BlockSpec(shape, lambda p: (0, 0))


def flat(kind=jnp.float32, times=1):
    return pltpu.VMEM((STEP * BLK, times * SEQ), kind)


def forward_call(x, wt, coef, interpret=False):
    f32, bf16 = jnp.float32, jnp.bfloat16
    n = x.shape[0]
    return pl.pallas_call(
        forward_kernel,
        grid=(n // STEP,),
        out_shape=[jax.ShapeDtypeStruct((n, BLK, SEQ), f32) for _ in range(5)],
        in_specs=[TOK, full(TWO, WROWS), full(BLK, SEQ)],
        out_specs=[TOK] * 5,
        scratch_shapes=[
            pltpu.VMEM((2 * SEQ, SEQ), bf16),
            pltpu.VMEM((2 * SEQ, SEQ), bf16),
            pltpu.VMEM((WROWS, STEP * SEQ), bf16),
            pltpu.VMEM((TWO, STEP * SEQ), f32),
            flat(), flat(), flat(), flat(), flat(bf16, 2), flat(), flat(bf16, 2), flat(),
        ],
        compiler_params=params(),
        interpret=interpret,
    )(x, wt, coef)


def backward_call(factor, x, c, made, w, coef, grad_dtype=jnp.bfloat16, interpret=False):
    f32, bf16 = jnp.float32, jnp.bfloat16
    n = x.shape[0]
    return pl.pallas_call(
        functools.partial(backward_kernel, factor),
        grid=(n // STEP,),
        out_shape=[
            jax.ShapeDtypeStruct((n, BLK, SEQ), bf16),
            jax.ShapeDtypeStruct((WROWS, WCOLS), grad_dtype),
        ],
        in_specs=[TOK] * 7 + [full(WROWS, WCOLS), full(BLK, SEQ)],
        out_specs=[TOK, full(WROWS, WCOLS)],
        scratch_shapes=[
            pltpu.VMEM((2 * SEQ, SEQ), bf16),
            pltpu.VMEM((WROWS, STEP * SEQ), bf16),
            pltpu.VMEM((TWO, STEP * SEQ), bf16),
            flat(bf16, 2),
            flat(),
            pltpu.VMEM((BLK, STEP * SEQ), f32),
            pltpu.VMEM((BLK, SEQ), f32),
            pltpu.VMEM((WROWS, WCOLS), f32),
        ],
        compiler_params=params(),
        interpret=interpret,
    )(x, c, *made, w, coef)


def wire(wa, wx, ba, bx, decay):
    bf16 = jnp.bfloat16
    tail = jnp.zeros((WROWS - BLK - 2, TWO), bf16)
    body = jnp.concatenate(
        [
            jnp.concatenate([wa, wx], axis=1),
            jnp.concatenate([ba, bx])[None],
            jnp.concatenate([decay, jnp.zeros((BLK,), bf16)])[None],
            tail,
        ],
        axis=0,
    )
    return jnp.pad(body, ((0, 0), (0, WCOLS - TWO)))


def unwire(w):
    wt = w[:, :TWO].T
    coef = (-8.0 * LOG2E) * jax.nn.softplus(w[BLK + 1, :BLK].astype(jnp.float32))
    return wt, jnp.broadcast_to(coef[:, None], (BLK, SEQ))


def per_device(inputs, cotangent, wa, wx, ba, bx, decay):
    bf16, f32 = jnp.bfloat16, jnp.float32
    plane, line = ("cuts", "yh", "core"), ("cuts", "z")
    z = lax.axis_index("z").astype(jnp.int32).reshape(1)
    pairs = [(i, k, (k + i) % NZ) for i in range(NI) for k in range(NZ)]
    fetch = [(i * NZ + src, i * NZ + k) for i, k, src in pairs]
    home = [(b, a) for a, b in fetch]

    x = lax.all_to_all(pack(z, inputs, z), plane, 0, 0, tiled=True)
    w = lax.ppermute(wire(wa, wx, ba, bx, decay), line, fetch)
    c = lax.all_to_all(pack(z, cotangent, w), plane, 0, 0, tiled=True)
    wt, coef = unwire(w)
    made = forward_call(x, wt, coef)
    total = SEQ * NSEQ * NZ
    out, grads = backward_call(float(total) ** -0.5, x, c, made, w, coef)
    share = lax.ppermute(grads, line, home)
    input_grad = unpack(z, lax.all_to_all(out, plane, 0, 0, tiled=True))
    parts = [share] + [lax.ppermute(share, "cuts", [(i, (i + 2 * k) % NI) for i in range(NI)]) for k in (1, 2, 3)]
    half = sum(p.astype(f32) for p in parts).astype(bf16)
    other = lax.ppermute(half, "cuts", [(i, i ^ 1) for i in range(NI)])
    full_sum = half.astype(f32) + other.astype(f32)
    own = jax.nn.sigmoid(decay.astype(f32))
    return (
        input_grad,
        full_sum[:BLK, :BLK],
        full_sum[:BLK, BLK:TWO],
        full_sum[BLK, :BLK],
        full_sum[BLK, BLK:TWO],
        full_sum[BLK + 1, :BLK] * own,
    )


def solution(mesh):
    fine = Mesh(mesh.devices.reshape(NI, NZ, NY, NC), ("cuts", "z", "yh", "core"))
    zero = ("z", "yh", "core")
    rows = P(("cuts",) + zero, None)
    return jax.shard_map(
        per_device,
        mesh=fine,
        in_specs=(rows, rows, P(zero, None), P(zero, None), P(zero), P(zero), P(zero)),
        out_specs=(rows, P(zero, None), P(zero, None), P(zero), P(zero), P(zero)),
        check_vma=False,
    )
```

```python
import functools

import jax
import jax.numpy as jnp
from jax import lax
from jax.experimental import pallas as pl
from jax.experimental.pallas import tpu as pltpu
from jax.sharding import Mesh
from jax.sharding import PartitionSpec as P

BLK = 176
TWO = 2 * BLK
WROWS = 192
WCOLS = 384
NZ, NY, NC = 8, 2, 2
NQ = NY * NC
NI = 8
SEQ = 128
NSEQ = NI * NQ
STEP = 8
VMEM_LIMIT = 56 * 1024 * 1024


def pack_kernel(z_ref, x_ref, c_ref, out_ref):
    odd = z_ref[0] & 1
    for k, ref in enumerate((x_ref, c_ref)):
        turned = ref[...].T
        for h in range(2 * NQ):
            slot = (h // NQ ^ odd) * NQ + h % NQ
            out_ref[slot, k * BLK : (k + 1) * BLK, :] = turned[h * BLK : (h + 1) * BLK, :]


def unpack_kernel(z_ref, in_ref, out_ref):
    odd = z_ref[0] & 1
    heads = [in_ref[(h // NQ ^ odd) * NQ + h % NQ] for h in range(2 * NQ)]
    out_ref[...] = jnp.concatenate(heads, axis=0).T


def params():
    return pltpu.CompilerParams(vmem_limit_bytes=VMEM_LIMIT)


def turn_specs(rows):
    wide = pl.BlockSpec((SEQ, 2 * NQ * BLK), lambda p, z: (0, p))
    tall = pl.BlockSpec((2 * NQ, rows, SEQ), lambda p, z: (p ^ (z[0] >> 1), 0, 0))
    return wide, tall


def pack(z, x, c, interpret=False):
    wide, tall = turn_specs(TWO)
    return pl.pallas_call(
        pack_kernel,
        grid_spec=pltpu.PrefetchScalarGridSpec(
            num_scalar_prefetch=1, grid=(NZ // 2,), in_specs=[wide, wide], out_specs=tall
        ),
        out_shape=jax.ShapeDtypeStruct((NSEQ, TWO, SEQ), x.dtype),
        compiler_params=params(),
        interpret=interpret,
    )(z, x, c)


def unpack(z, y, interpret=False):
    wide, tall = turn_specs(BLK)
    return pl.pallas_call(
        unpack_kernel,
        grid_spec=pltpu.PrefetchScalarGridSpec(
            num_scalar_prefetch=1, grid=(NZ // 2,), in_specs=[tall], out_specs=wide
        ),
        out_shape=jax.ShapeDtypeStruct((SEQ, NSEQ * BLK), y.dtype),
        compiler_params=params(),
        interpret=interpret,
    )(z, y)


LN2 = 0.6931471805599453
LOG2E = 1.4426950408889634


def sigmoid(pre):
    base = 1.0 + jnp.exp2(jnp.minimum(pre * -LOG2E, 115.0))
    rough = pl.reciprocal(base, approx=True)
    return rough * (2.0 - base * rough)


def one_minus_square(u):
    series, power = 0.0, 1.0
    terms = []
    for k in range(1, 8):
        power = power * (2.0 * LN2) / k
        terms.append(-power)
    series = terms[-1]
    for t in terms[-2::-1]:
        series = series * u + t
    return series * u


CH = 16


def main_kernel(
    factor, m_ref, w_ref, wt_ref, coef_ref, out_ref, g_ref,
    tri, x_s, pre_s, d_s, u_s, rest_s, own_s, f1_s, gain_s, drive_s, ub_s, log_s, fwd_in, rev_in, fwd_s, rev_s, q_s, g_s,
):
    step = pl.program_id(0)
    f32, bf16 = jnp.float32, jnp.bfloat16

    @pl.when(step == 0)
    def _():
        row = lax.broadcasted_iota(jnp.int32, (WROWS - BLK, STEP * SEQ), 0)
        x_s[BLK:, :] = jnp.where(row == 0, 1.0, 0.0).astype(x_s.dtype)
        q_s[...] = jnp.zeros_like(q_s)
        g_s[...] = jnp.zeros_like(g_s)
        src = lax.broadcasted_iota(jnp.int32, (2 * SEQ, 2 * SEQ), 0)
        dst = lax.broadcasted_iota(jnp.int32, (2 * SEQ, 2 * SEQ), 1)
        same = (src < SEQ) == (dst < SEQ)
        for k, seen in enumerate((src <= dst, src < dst, src >= dst)):
            tri[k] = jnp.where(seen & same, 1.0, 0.0).astype(bf16)

    for s in range(STEP):
        x_s[:BLK, s * SEQ : (s + 1) * SEQ] = m_ref[s, :BLK, :]
    pre_s[...] = jnp.dot(wt_ref[...], x_s[...], preferred_element_type=f32)

    def each(body):
        def two(p, _):
            for half in range(2):
                s = 2 * p + half
                cols = pl.ds(pl.multiple_of(s * SEQ, SEQ), SEQ)
                for r in range(0, BLK, CH):
                    rows = pl.ds(pl.multiple_of(p * BLK + r, 16), CH)
                    body(s, r, cols, (rows, slice(half * SEQ, (half + 1) * SEQ)))
            return 0

        lax.fori_loop(0, STEP // 2, two, 0)

    def gates(s, r, cols, at):
        x = m_ref[s, r : r + CH, :].astype(f32)
        rgate = sigmoid(pre_s[r : r + CH, cols])
        igate = sigmoid(pre_s[BLK + r : BLK + r + CH, cols])
        u = coef_ref[r : r + CH, :] * rgate
        var = one_minus_square(u)
        inv = lax.rsqrt(var)
        scale = var * inv
        ix = igate * x
        drive = scale * ix
        u_s[at] = u
        rest_s[at] = LN2 - LN2 * rgate
        own_s[at] = ix * (inv - scale)
        f1_s[at] = drive - drive * igate
        gain_s[at] = scale * igate
        drive_s[at] = drive
        ub_s[at] = u.astype(bf16)

    each(gates)
    log_s[...] = jnp.dot(ub_s[...], tri[0], preferred_element_type=f32)

    def weigh(s, r, cols, at):
        total = log_s[at]
        cot = m_ref[s, BLK + r : BLK + r + CH, :].astype(f32)
        fwd_in[at] = (drive_s[at] * jnp.exp2(-total)).astype(bf16)
        rev_in[at] = (cot * jnp.exp2(total)).astype(bf16)

    each(weigh)
    fwd_s[...] = jnp.dot(fwd_in[...], tri[1], preferred_element_type=f32)
    rev_s[...] = jnp.dot(rev_in[...], tri[2], preferred_element_type=f32)

    def deltas(s, r, cols, at):
        total = log_s[at]
        adj = rev_s[at] * jnp.exp2(-total)
        dlog = adj * (fwd_s[at] * jnp.exp2(total) - own_s[at])
        v = dlog * u_s[at]
        q_s[r : r + CH, :] += v
        d_s[r : r + CH, cols] = (v * rest_s[at]).astype(bf16)
        d_s[BLK + r : BLK + r + CH, cols] = (adj * f1_s[at]).astype(bf16)
        pre_s[r : r + CH, cols] = adj * gain_s[at]

    each(deltas)

    back = jnp.dot(w_ref[:BLK, :TWO], d_s[...], preferred_element_type=f32)
    for s in range(STEP):
        cols = slice(s * SEQ, (s + 1) * SEQ)
        out_ref[s] = (back[:, cols] + pre_s[:BLK, cols]).astype(out_ref.dtype)
    nt = (((1,), (1,)), ((), ()))
    g_s[:, :TWO] += lax.dot_general(x_s[...], d_s[...], nt, preferred_element_type=f32)

    @pl.when(step == pl.num_programs(0) - 1)
    def _():
        g_ref[...] = (g_s[...] * factor).astype(g_ref.dtype)
        decay = jnp.sum((q_s[...] / coef_ref[...]).T, axis=0, keepdims=True) * (-8.0 * factor)
        tail = g_s[BLK:, :BLK] * factor
        row = lax.broadcasted_iota(jnp.int32, tail.shape, 0)
        g_ref[BLK:, :BLK] = jnp.where(row == 1, decay, tail).astype(g_ref.dtype)


def main_call(factor, m, w, wt, coef, grad_dtype=jnp.bfloat16, interpret=False):
    f32, bf16 = jnp.float32, jnp.bfloat16
    n = m.shape[0]
    tok = lambda rows: pl.BlockSpec((STEP, rows, SEQ), lambda p: (p, 0, 0))
    full = lambda shape: pl.BlockSpec(shape, lambda p: (0, 0))
    flat, half = (pltpu.VMEM((STEP // 2 * BLK, 2 * SEQ), kind) for kind in (f32, bf16))
    return pl.pallas_call(
        functools.partial(main_kernel, factor),
        grid=(n // STEP,),
        out_shape=[
            jax.ShapeDtypeStruct((n, BLK, SEQ), bf16),
            jax.ShapeDtypeStruct((WROWS, WCOLS), grad_dtype),
        ],
        in_specs=[tok(TWO), full((WROWS, WCOLS)), full((TWO, WROWS)), full((BLK, SEQ))],
        out_specs=[tok(BLK), full((WROWS, WCOLS))],
        scratch_shapes=[
            pltpu.VMEM((3, 2 * SEQ, 2 * SEQ), bf16),
            pltpu.VMEM((WROWS, STEP * SEQ), bf16),
            pltpu.VMEM((TWO, STEP * SEQ), f32),
            pltpu.VMEM((TWO, STEP * SEQ), bf16),
            flat, flat, flat, flat, flat, flat,
            half, flat, half, half, flat, flat,
            pltpu.VMEM((BLK, SEQ), f32),
            pltpu.VMEM((WROWS, WCOLS), f32),
        ],
        compiler_params=params(),
        interpret=interpret,
    )(m, w, wt, coef)


def wire(wa, wx, ba, bx, decay):
    bf16 = jnp.bfloat16
    tail = jnp.zeros((WROWS - BLK - 2, TWO), bf16)
    body = jnp.concatenate(
        [
            jnp.concatenate([wa, wx], axis=1),
            jnp.concatenate([ba, bx])[None],
            jnp.concatenate([decay, jnp.zeros((BLK,), bf16)])[None],
            tail,
        ],
        axis=0,
    )
    return jnp.pad(body, ((0, 0), (0, WCOLS - TWO)))


def unwire(w):
    wt = w[:, :TWO].T
    coef = (-8.0 * LOG2E) * jax.nn.softplus(w[BLK + 1, :BLK].astype(jnp.float32))
    return wt, jnp.broadcast_to(coef[:, None], (BLK, SEQ))


def per_device(inputs, cotangent, wa, wx, ba, bx, decay):
    bf16, f32 = jnp.bfloat16, jnp.float32
    plane, line = ("cuts", "yh", "core"), ("cuts", "z")
    z = lax.axis_index("z").astype(jnp.int32).reshape(1)
    everyone = [(i, k) for i in range(NI) for k in range(NZ)]
    fetch = [(i * NZ + (k ^ i), i * NZ + k) for i, k in everyone]
    across = [(i * NZ + (k ^ i), (i ^ 1) * NZ + k) for i, k in everyone]

    got = lax.all_to_all(pack(z, inputs, cotangent), plane, 0, 0, tiled=True)
    w = lax.ppermute(wire(wa, wx, ba, bx, decay), line, fetch)
    wt, coef = unwire(w)
    total = SEQ * NSEQ * NZ
    out, grads = main_call(float(total) ** -0.5, got, w, wt, coef)
    input_grad = unpack(z, lax.all_to_all(out, plane, 0, 0, tiled=True))
    pair = lax.ppermute(grads, line, fetch).astype(f32) + lax.ppermute(grads, line, across).astype(f32)
    pair = pair.astype(bf16)
    parts = [pair] + [lax.ppermute(pair, "cuts", [(i, (i + 2 * k) % NI) for i in range(NI)]) for k in (1, 2, 3)]
    parts, input_grad = lax.optimization_barrier((parts, input_grad))
    full = sum(p.astype(f32) for p in parts)
    own = jax.nn.sigmoid(decay.astype(f32))
    return (
        input_grad,
        full[:BLK, :BLK],
        full[:BLK, BLK:TWO],
        full[BLK, :BLK],
        full[BLK, BLK:TWO],
        full[BLK + 1, :BLK] * own,
    )


def solution(mesh):
    fine = Mesh(mesh.devices.reshape(NI, NZ, NY, NC), ("cuts", "z", "yh", "core"))
    zero = ("z", "yh", "core")
    rows = P(("cuts",) + zero, None)
    return jax.shard_map(
        per_device,
        mesh=fine,
        in_specs=(rows, rows, P(zero, None), P(zero, None), P(zero), P(zero), P(zero)),
        out_specs=(rows, P(zero, None), P(zero, None), P(zero), P(zero), P(zero)),
        check_vma=False,
    )
```

```python
import functools

import jax
import jax.numpy as jnp
from jax import lax
from jax.experimental import pallas as pl
from jax.experimental.pallas import tpu as pltpu
from jax.sharding import Mesh
from jax.sharding import PartitionSpec as P

BLK = 176
TWO = 2 * BLK
WROWS = 192
WCOLS = 384
NZ, NY, NC = 8, 2, 2
NQ = NY * NC
NI = 8
SEQ = 128
NSEQ = NI * NQ
STEP = 32
VMEM_LIMIT = 56 * 1024 * 1024


def pack_kernel(z_ref, x_ref, c_ref, out_ref):
    turn = z_ref[0] * NQ
    for k, ref in enumerate((x_ref, c_ref)):
        for p in range(NZ // 2):
            turned = ref[:, p * 2 * NQ * BLK : (p + 1) * 2 * NQ * BLK].T
            for h in range(2 * NQ):
                out_ref[(2 * NQ * p + h) ^ turn, k * BLK : (k + 1) * BLK, :] = turned[h * BLK : (h + 1) * BLK, :]


def unpack_kernel(z_ref, in_ref, out_ref):
    turn = z_ref[0] * NQ
    for p in range(NZ // 2):
        heads = [in_ref[(2 * NQ * p + h) ^ turn] for h in range(2 * NQ)]
        out_ref[:, p * 2 * NQ * BLK : (p + 1) * 2 * NQ * BLK] = jnp.concatenate(heads, axis=0).T


def params():
    return pltpu.CompilerParams(vmem_limit_bytes=VMEM_LIMIT)


SMEM = pl.BlockSpec(memory_space=pltpu.SMEM)
VMEM = pl.BlockSpec(memory_space=pltpu.VMEM)


def pack(z, x, c, interpret=False):
    return pl.pallas_call(
        pack_kernel,
        in_specs=[SMEM, VMEM, VMEM],
        out_specs=VMEM,
        out_shape=jax.ShapeDtypeStruct((NSEQ, TWO, SEQ), x.dtype),
        compiler_params=params(),
        interpret=interpret,
    )(z, x, c)


def unpack(z, y, interpret=False):
    return pl.pallas_call(
        unpack_kernel,
        in_specs=[SMEM, VMEM],
        out_specs=VMEM,
        out_shape=jax.ShapeDtypeStruct((SEQ, NSEQ * BLK), y.dtype),
        compiler_params=params(),
        interpret=interpret,
    )(z, y)


LN2 = 0.6931471805599453
LOG2E = 1.4426950408889634


def sigmoid(pre):
    return pl.reciprocal(1.0 + jnp.exp2(jnp.minimum(pre * -LOG2E, 115.0)), approx=True)


def one_minus_square(u):
    series, power = 0.0, 1.0
    terms = []
    for k in range(1, 7):
        power = power * (2.0 * LN2) / k
        terms.append(-power)
    series = terms[-1]
    for t in terms[-2::-1]:
        series = series * u + t
    return series * u


CH = 16


def main_kernel(
    factor, m_ref, w_ref, wt_ref, out_ref, g_ref,
    tri, x_s, pre_s, d_s, u_s, rest_s, own_s, f1_s, gain_s, drive_s, ub_s, log_s, fwd_in, rev_in, fwd_s, rev_s, coef_s, q_s, g_s,
):
    step = pl.program_id(0)
    f32, bf16 = jnp.float32, jnp.bfloat16

    @pl.when(step == 0)
    def _():
        row = lax.broadcasted_iota(jnp.int32, (WROWS - BLK, STEP * SEQ), 0)
        x_s[BLK:, :] = jnp.where(row == 0, 1.0, 0.0).astype(x_s.dtype)
        decay = wt_ref[:BLK, BLK + 1 : BLK + 2].astype(f32)
        soft = jnp.maximum(decay, 0.0) + jnp.log1p(jnp.exp(-jnp.abs(decay)))
        coef_s[...] = jnp.broadcast_to((-8.0 * LOG2E) * soft, (BLK, SEQ))
        q_s[...] = jnp.zeros_like(q_s)
        g_s[...] = jnp.zeros_like(g_s)
        src = lax.broadcasted_iota(jnp.int32, (2 * SEQ, 2 * SEQ), 0)
        dst = lax.broadcasted_iota(jnp.int32, (2 * SEQ, 2 * SEQ), 1)
        same = (src < SEQ) == (dst < SEQ)
        for k, seen in enumerate((src <= dst, src < dst, src >= dst)):
            tri[k] = jnp.where(seen & same, 1.0, 0.0).astype(bf16)

    for s in range(STEP):
        x_s[:BLK, s * SEQ : (s + 1) * SEQ] = m_ref[s, :BLK, :]
    pre_s[...] = jnp.dot(wt_ref[...], x_s[...], preferred_element_type=f32)

    def each(body):
        def two(p, _):
            for half in range(2):
                s = 2 * p + half
                cols = pl.ds(pl.multiple_of(s * SEQ, SEQ), SEQ)
                for r in range(0, BLK, CH):
                    rows = pl.ds(pl.multiple_of(p * BLK + r, 16), CH)
                    body(s, r, cols, (rows, slice(half * SEQ, (half + 1) * SEQ)))
            return 0

        lax.fori_loop(0, STEP // 2, two, 0)

    def gates(s, r, cols, at):
        x = m_ref[s, r : r + CH, :].astype(f32)
        rgate = sigmoid(pre_s[r : r + CH, cols])
        igate = 0.5 + 0.5 * jnp.tanh(0.5 * pre_s[BLK + r : BLK + r + CH, cols])
        u = coef_s[r : r + CH, :] * rgate
        var = one_minus_square(u)
        inv = lax.rsqrt(var)
        scale = var * inv
        ix = igate * x
        drive = scale * ix
        u_s[at] = u
        rest_s[at] = LN2 - LN2 * rgate
        own_s[at] = ix * (inv - scale)
        f1_s[at] = drive - drive * igate
        gain_s[at] = scale * igate
        drive_s[at] = drive
        ub_s[at] = u.astype(bf16)

    each(gates)
    log_s[...] = jnp.dot(ub_s[...], tri[0], preferred_element_type=f32)

    def weigh(s, r, cols, at):
        total = log_s[at]
        cot = m_ref[s, BLK + r : BLK + r + CH, :].astype(f32)
        fwd_in[at] = (drive_s[at] * jnp.exp2(-total)).astype(bf16)
        rev_in[at] = (cot * jnp.exp2(total)).astype(bf16)

    each(weigh)
    fwd_s[...] = jnp.dot(fwd_in[...], tri[1], preferred_element_type=f32)
    rev_s[...] = jnp.dot(rev_in[...], tri[2], preferred_element_type=f32)

    def deltas(s, r, cols, at):
        total = log_s[at]
        adj = rev_s[at] * jnp.exp2(-total)
        dlog = adj * (fwd_s[at] * jnp.exp2(total) - own_s[at])
        v = dlog * u_s[at]
        q_s[r : r + CH, :] += v
        d_s[r : r + CH, cols] = (v * rest_s[at]).astype(bf16)
        d_s[BLK + r : BLK + r + CH, cols] = (adj * f1_s[at]).astype(bf16)
        pre_s[r : r + CH, cols] = adj * gain_s[at]

    each(deltas)

    back = jnp.dot(w_ref[:BLK, :TWO], d_s[...], preferred_element_type=f32)
    for s in range(STEP):
        cols = slice(s * SEQ, (s + 1) * SEQ)
        out_ref[s] = (back[:, cols] + pre_s[:BLK, cols]).astype(out_ref.dtype)
    nt = (((1,), (1,)), ((), ()))
    g_s[:, :TWO] += lax.dot_general(x_s[...], d_s[...], nt, preferred_element_type=f32)

    @pl.when(step == pl.num_programs(0) - 1)
    def _():
        g_ref[...] = (g_s[...] * factor).astype(g_ref.dtype)
        decay = jnp.sum((q_s[...] / coef_s[...]).T, axis=0, keepdims=True) * (-8.0 * factor)
        tail = g_s[BLK:, :BLK] * factor
        row = lax.broadcasted_iota(jnp.int32, tail.shape, 0)
        g_ref[BLK:, :BLK] = jnp.where(row == 1, decay, tail).astype(g_ref.dtype)


def main_call(factor, m, w, wt, grad_dtype=jnp.bfloat16, interpret=False):
    f32, bf16 = jnp.float32, jnp.bfloat16
    n = m.shape[0]
    tok = lambda rows: pl.BlockSpec((STEP, rows, SEQ), lambda p: (p, 0, 0))
    full = lambda shape: pl.BlockSpec(shape, lambda p: (0, 0))
    flat, half = (pltpu.VMEM((STEP // 2 * BLK, 2 * SEQ), kind) for kind in (f32, bf16))
    return pl.pallas_call(
        functools.partial(main_kernel, factor),
        grid=(n // STEP,),
        out_shape=[
            jax.ShapeDtypeStruct((n, BLK, SEQ), bf16),
            jax.ShapeDtypeStruct((WROWS, WCOLS), grad_dtype),
        ],
        in_specs=[tok(TWO), full((WROWS, WCOLS)), full((TWO, WROWS))],
        out_specs=[tok(BLK), full((WROWS, WCOLS))],
        scratch_shapes=[
            pltpu.VMEM((3, 2 * SEQ, 2 * SEQ), bf16),
            pltpu.VMEM((WROWS, STEP * SEQ), bf16),
            pltpu.VMEM((TWO, STEP * SEQ), f32),
            pltpu.VMEM((TWO, STEP * SEQ), bf16),
            flat, flat, flat, flat, flat, flat,
            half, flat, half, half, flat, flat,
            pltpu.VMEM((BLK, SEQ), f32),
            pltpu.VMEM((BLK, SEQ), f32),
            pltpu.VMEM((WROWS, WCOLS), f32),
        ],
        compiler_params=params(),
        interpret=interpret,
    )(m, w, wt)


def wire(wa, wx, ba, bx, decay):
    bf16 = jnp.bfloat16
    tail = jnp.zeros((WROWS - BLK - 2, TWO), bf16)
    body = jnp.concatenate(
        [
            jnp.concatenate([wa, wx], axis=1),
            jnp.concatenate([ba, bx])[None],
            jnp.concatenate([decay, jnp.zeros((BLK,), bf16)])[None],
            tail,
        ],
        axis=0,
    )
    return jnp.pad(body, ((0, 0), (0, WCOLS - TWO)))


def per_device(inputs, cotangent, wa, wx, ba, bx, decay):
    bf16, f32 = jnp.bfloat16, jnp.float32
    plane, line = ("cuts", "yh", "core"), ("cuts", "z")
    z = lax.axis_index("z").astype(jnp.int32).reshape(1)
    everyone = [(i, k) for i in range(NI) for k in range(NZ)]
    fetch = [(i * NZ + (k ^ i), i * NZ + k) for i, k in everyone]
    homes = [[(i * NZ + (k ^ i), (i ^ j) * NZ + k) for i, k in everyone] for j in range(NI // 2)]
    got = lax.all_to_all(pack(z, inputs, cotangent), plane, 0, 0, tiled=True)
    w = lax.ppermute(wire(wa, wx, ba, bx, decay), line, fetch)
    total = SEQ * NSEQ * NZ
    out, grads = main_call(float(total) ** -0.5, got, w, w[:, :TWO].T)
    input_grad = unpack(z, lax.all_to_all(out, plane, 0, 0, tiled=True))
    some = sum(lax.ppermute(grads, line, home).astype(f32) for home in homes).astype(bf16)
    other = lax.ppermute(some, "cuts", [(i, i ^ (NI // 2)) for i in range(NI)])
    some, other, input_grad = lax.optimization_barrier((some, other, input_grad))
    full = some.astype(f32) + other.astype(f32)
    own = jax.nn.sigmoid(decay.astype(f32))
    return (
        input_grad,
        full[:BLK, :BLK],
        full[:BLK, BLK:TWO],
        full[BLK, :BLK],
        full[BLK, BLK:TWO],
        full[BLK + 1, :BLK] * own,
    )


def solution(mesh):
    fine = Mesh(mesh.devices.reshape(NI, NZ, NY, NC), ("cuts", "z", "yh", "core"))
    zero = ("z", "yh", "core")
    rows = P(("cuts",) + zero, None)
    return jax.shard_map(
        per_device,
        mesh=fine,
        in_specs=(rows, rows, P(zero, None), P(zero, None), P(zero), P(zero), P(zero)),
        out_specs=(rows, P(zero, None), P(zero, None), P(zero), P(zero), P(zero)),
        check_vma=False,
    )
```

```python
import functools

import jax
import jax.numpy as jnp
from jax import lax
from jax.experimental import pallas as pl
from jax.experimental.pallas import tpu as pltpu
from jax.sharding import Mesh
from jax.sharding import PartitionSpec as P

BLK = 176
TWO = 2 * BLK
WROWS = 192
WCOLS = 384
NZ, NY, NC = 8, 2, 2
NQ = NY * NC
NI = 8
SEQ = 128
NSEQ = NI * NQ
STEP = 8
VMEM_LIMIT = 56 * 1024 * 1024


def pack_kernel(z_ref, x_hbm, c_hbm, out_hbm, x_s, c_s, out_s, in_sem, out_sem):
    wide = 2 * NQ * BLK
    loads = []
    for p in range(NZ // 2):
        for k, (src, dst) in enumerate(((x_hbm, x_s), (c_hbm, c_s))):
            cols = slice(p * wide, (p + 1) * wide)
            loads.append(pltpu.make_async_copy(src.at[:, cols], dst.at[:, cols], in_sem.at[k, p]))
            loads[-1].start()
    stores = []
    for p in range(NZ // 2):
        turned = []
        for k, ref in enumerate((x_s, c_s)):
            loads[2 * p + k].wait()
            turned.append(ref[:, p * wide : (p + 1) * wide].T)
        for half in range(2):
            group = (2 * p + half) ^ z_ref[0]
            for q in range(NQ):
                rows = slice((half * NQ + q) * BLK, (half * NQ + q + 1) * BLK)
                for k in range(2):
                    out_s[group * NQ + q, k * BLK : (k + 1) * BLK, :] = turned[k][rows]
            slots = pl.ds(group * NQ, NQ)
            stores.append(pltpu.make_async_copy(out_s.at[slots], out_hbm.at[slots], out_sem.at[2 * p + half]))
            stores[-1].start()
    for copy in stores:
        copy.wait()


def unpack_kernel(z_ref, in_hbm, out_hbm, in_s, out_s, in_sem, out_sem):
    wide = 2 * NQ * BLK
    loads = []
    for g in range(NZ):
        slots = pl.ds((g ^ z_ref[0]) * NQ, NQ)
        loads.append(pltpu.make_async_copy(in_hbm.at[slots], in_s.at[g], in_sem.at[g]))
        loads[-1].start()
    stores = []
    for p in range(NZ // 2):
        loads[2 * p].wait()
        loads[2 * p + 1].wait()
        cols = slice(p * wide, (p + 1) * wide)
        out_s[:, cols] = in_s[2 * p : 2 * p + 2].reshape(wide, SEQ).T
        stores.append(pltpu.make_async_copy(out_s.at[:, cols], out_hbm.at[:, cols], out_sem.at[p]))
        stores[-1].start()
    for copy in stores:
        copy.wait()


def params():
    return pltpu.CompilerParams(vmem_limit_bytes=VMEM_LIMIT)


SMEM = pl.BlockSpec(memory_space=pltpu.SMEM)
ANY = pl.BlockSpec(memory_space=pl.ANY)


def pack(z, x, c, interpret=False):
    sem = pltpu.SemaphoreType.DMA
    return pl.pallas_call(
        pack_kernel,
        in_specs=[SMEM, ANY, ANY],
        out_specs=ANY,
        out_shape=jax.ShapeDtypeStruct((NSEQ, TWO, SEQ), x.dtype),
        scratch_shapes=[
            pltpu.VMEM(x.shape, x.dtype),
            pltpu.VMEM(x.shape, x.dtype),
            pltpu.VMEM((NSEQ, TWO, SEQ), x.dtype),
            sem((2, NZ // 2)),
            sem((NZ,)),
        ],
        compiler_params=params(),
        interpret=interpret,
    )(z, x, c)


def unpack(z, y, interpret=False):
    sem = pltpu.SemaphoreType.DMA
    return pl.pallas_call(
        unpack_kernel,
        in_specs=[SMEM, ANY],
        out_specs=ANY,
        out_shape=jax.ShapeDtypeStruct((SEQ, NSEQ * BLK), y.dtype),
        scratch_shapes=[
            pltpu.VMEM((NZ, NQ, BLK, SEQ), y.dtype),
            pltpu.VMEM((SEQ, NSEQ * BLK), y.dtype),
            sem((NZ,)),
            sem((NZ // 2,)),
        ],
        compiler_params=params(),
        interpret=interpret,
    )(z, y)


LN2 = 0.6931471805599453
LOG2E = 1.4426950408889634


def sigmoid(pre):
    return pl.reciprocal(1.0 + jnp.exp2(jnp.minimum(pre * -LOG2E, 115.0)), approx=True)


def one_minus_square(u):
    series, power = 0.0, 1.0
    terms = []
    for k in range(1, 7):
        power = power * (2.0 * LN2) / k
        terms.append(-power)
    series = terms[-1]
    for t in terms[-2::-1]:
        series = series * u + t
    return series * u


CH = 16


def main_kernel(
    factor, m_hbm, w_ref, wt_ref, out_hbm, g_ref,
    m_ref, out_ref, tri, x_s, pre_s, d_s, u_s, rest_s, own_s, f1_s, gain_s, drive_s, ub_s, log_s,
    fwd_in, rev_in, fwd_s, rev_s, coef_s, q_s, in_sem, out_sem,
):
    f32, bf16 = jnp.float32, jnp.bfloat16
    blocks = [pl.ds(j * STEP, STEP) for j in range(NSEQ // STEP)]
    loads = [pltpu.make_async_copy(m_hbm.at[b], m_ref.at[b], in_sem.at[j]) for j, b in enumerate(blocks)]
    stores = [pltpu.make_async_copy(out_ref.at[b], out_hbm.at[b], out_sem.at[j]) for j, b in enumerate(blocks)]
    for copy in loads:
        copy.start()

    row = lax.broadcasted_iota(jnp.int32, (WROWS - BLK, NSEQ * SEQ), 0)
    x_s[BLK:, :] = jnp.where(row == 0, 1.0, 0.0).astype(x_s.dtype)
    decay = wt_ref[:BLK, BLK + 1 : BLK + 2].astype(f32)
    soft = jnp.maximum(decay, 0.0) + jnp.log1p(jnp.exp(-jnp.abs(decay)))
    coef_s[...] = jnp.broadcast_to((-8.0 * LOG2E) * soft, (BLK, SEQ))
    q_s[...] = jnp.zeros_like(q_s)
    src = lax.broadcasted_iota(jnp.int32, (2 * SEQ, 2 * SEQ), 0)
    dst = lax.broadcasted_iota(jnp.int32, (2 * SEQ, 2 * SEQ), 1)
    same = (src < SEQ) == (dst < SEQ)
    for k, seen in enumerate((src <= dst, src < dst, src >= dst)):
        tri[k] = jnp.where(seen & same, 1.0, 0.0).astype(bf16)

    def each(body, first=0, last=NSEQ // 2):
        def two(p, _):
            for half in range(2):
                s = 2 * p + half
                cols = pl.ds(pl.multiple_of(s * SEQ, SEQ), SEQ)
                for r in range(0, BLK, CH):
                    rows = pl.ds(pl.multiple_of(p * BLK + r, 16), CH)
                    body(s, r, cols, (rows, slice(half * SEQ, (half + 1) * SEQ)))
            return 0

        lax.fori_loop(first, last, two, 0)

    def gates(s, r, cols, at):
        x = m_ref[s, r : r + CH, :].astype(f32)
        rgate = sigmoid(pre_s[r : r + CH, cols])
        igate = 0.5 + 0.5 * jnp.tanh(0.5 * pre_s[BLK + r : BLK + r + CH, cols])
        u = coef_s[r : r + CH, :] * rgate
        var = one_minus_square(u)
        inv = lax.rsqrt(var)
        scale = var * inv
        ix = igate * x
        drive = scale * ix
        u_s[at] = u
        rest_s[at] = LN2 - LN2 * rgate
        own_s[at] = ix * (inv - scale)
        f1_s[at] = drive - drive * igate
        gain_s[at] = scale * igate
        drive_s[at] = drive
        ub_s[at] = u.astype(bf16)

    for j in range(NSEQ // STEP):
        loads[j].wait()
        cols = slice(j * STEP * SEQ, (j + 1) * STEP * SEQ)
        for s in range(j * STEP, (j + 1) * STEP):
            x_s[:BLK, s * SEQ : (s + 1) * SEQ] = m_ref[s, :BLK, :]
        pre_s[:, cols] = jnp.dot(wt_ref[...], x_s[:, cols], preferred_element_type=f32)
    each(gates)
    log_s[...] = jnp.dot(ub_s[...], tri[0], preferred_element_type=f32)

    def weigh(s, r, cols, at):
        total = log_s[at]
        cot = m_ref[s, BLK + r : BLK + r + CH, :].astype(f32)
        fwd_in[at] = (drive_s[at] * jnp.exp2(-total)).astype(bf16)
        rev_in[at] = (cot * jnp.exp2(total)).astype(bf16)

    each(weigh)
    fwd_s[...] = jnp.dot(fwd_in[...], tri[1], preferred_element_type=f32)
    rev_s[...] = jnp.dot(rev_in[...], tri[2], preferred_element_type=f32)

    def deltas(s, r, cols, at):
        total = log_s[at]
        adj = rev_s[at] * jnp.exp2(-total)
        dlog = adj * (fwd_s[at] * jnp.exp2(total) - own_s[at])
        v = dlog * u_s[at]
        q_s[r : r + CH, :] += v
        d_s[r : r + CH, cols] = (v * rest_s[at]).astype(bf16)
        d_s[BLK + r : BLK + r + CH, cols] = (adj * f1_s[at]).astype(bf16)
        pre_s[r : r + CH, cols] = adj * gain_s[at]

    each(deltas)

    for j in range(NSEQ // STEP):
        cols = slice(j * STEP * SEQ, (j + 1) * STEP * SEQ)
        back = jnp.dot(w_ref[:BLK, :TWO], d_s[:, cols], preferred_element_type=f32) + pre_s[:BLK, cols]
        for s in range(STEP):
            out_ref[j * STEP + s] = back[:, s * SEQ : (s + 1) * SEQ].astype(out_ref.dtype)
        stores[j].start()

    nt = (((1,), (1,)), ((), ()))
    grad = lax.dot_general(x_s[...], d_s[...], nt, preferred_element_type=f32) * factor
    g_ref[:, :TWO] = grad.astype(g_ref.dtype)
    g_ref[:, TWO:] = jnp.zeros((WROWS, WCOLS - TWO), g_ref.dtype)
    decay_row = jnp.sum((q_s[...] / coef_s[...]).T, axis=0, keepdims=True) * (-8.0 * factor)
    tail = grad[BLK:, :BLK]
    row = lax.broadcasted_iota(jnp.int32, tail.shape, 0)
    g_ref[BLK:, :BLK] = jnp.where(row == 1, decay_row, tail).astype(g_ref.dtype)
    for copy in stores:
        copy.wait()


def main_call(factor, m, w, wt, grad_dtype=jnp.bfloat16, interpret=False):
    f32, bf16 = jnp.float32, jnp.bfloat16
    vmem, sem = pltpu.VMEM, pltpu.SemaphoreType.DMA
    inside = pl.BlockSpec(memory_space=vmem)
    flat, half = (vmem((NSEQ // 2 * BLK, 2 * SEQ), kind) for kind in (f32, bf16))
    return pl.pallas_call(
        functools.partial(main_kernel, factor),
        out_shape=[
            jax.ShapeDtypeStruct((NSEQ, BLK, SEQ), bf16),
            jax.ShapeDtypeStruct((WROWS, WCOLS), grad_dtype),
        ],
        in_specs=[ANY, inside, inside],
        out_specs=[ANY, inside],
        scratch_shapes=[
            vmem((NSEQ, TWO, SEQ), bf16),
            vmem((NSEQ, BLK, SEQ), bf16),
            vmem((3, 2 * SEQ, 2 * SEQ), bf16),
            vmem((WROWS, NSEQ * SEQ), bf16),
            vmem((TWO, NSEQ * SEQ), f32),
            vmem((TWO, NSEQ * SEQ), bf16),
            flat, flat, flat, flat, flat, flat,
            half, flat, half, half, flat, flat,
            vmem((BLK, SEQ), f32),
            vmem((BLK, SEQ), f32),
            sem((NSEQ // STEP,)),
            sem((NSEQ // STEP,)),
        ],
        compiler_params=params(),
        interpret=interpret,
    )(m, w, wt)


def wire(wa, wx, ba, bx, decay):
    bf16 = jnp.bfloat16
    tail = jnp.zeros((WROWS - BLK - 2, TWO), bf16)
    body = jnp.concatenate(
        [
            jnp.concatenate([wa, wx], axis=1),
            jnp.concatenate([ba, bx])[None],
            jnp.concatenate([decay, jnp.zeros((BLK,), bf16)])[None],
            tail,
        ],
        axis=0,
    )
    return jnp.pad(body, ((0, 0), (0, WCOLS - TWO)))


def per_device(inputs, cotangent, wa, wx, ba, bx, decay):
    bf16, f32 = jnp.bfloat16, jnp.float32
    plane, line = ("cuts", "yh", "core"), ("cuts", "z")
    z = lax.axis_index("z").astype(jnp.int32).reshape(1)
    everyone = [(i, k) for i in range(NI) for k in range(NZ)]
    fetch = [(i * NZ + (k ^ i), i * NZ + k) for i, k in everyone]
    across = [(i * NZ + (k ^ i), (i ^ 1) * NZ + k) for i, k in everyone]

    got = lax.all_to_all(pack(z, inputs, cotangent), plane, 0, 0, tiled=True)
    w = lax.ppermute(wire(wa, wx, ba, bx, decay), line, fetch)
    total = SEQ * NSEQ * NZ
    out, grads = main_call(float(total) ** -0.5, got, w, w[:, :TWO].T)
    near, far = lax.ppermute(grads, line, fetch), lax.ppermute(grads, line, across)
    back = lax.all_to_all(out, plane, 0, 0, tiled=True)
    near, far, back = lax.optimization_barrier((near, far, back))
    pair = (near.astype(f32) + far.astype(f32)).astype(bf16)
    parts = [pair] + [lax.ppermute(pair, "cuts", [(i, (i + 2 * k) % NI) for i in range(NI)]) for k in (1, 2, 3)]
    input_grad = unpack(z, back)
    parts, input_grad = lax.optimization_barrier((parts, input_grad))
    full = sum(p.astype(f32) for p in parts)
    own = jax.nn.sigmoid(decay.astype(f32))
    return (
        input_grad,
        full[:BLK, :BLK],
        full[:BLK, BLK:TWO],
        full[BLK, :BLK],
        full[BLK, BLK:TWO],
        full[BLK + 1, :BLK] * own,
    )


def solution(mesh):
    fine = Mesh(mesh.devices.reshape(NI, NZ, NY, NC), ("cuts", "z", "yh", "core"))
    zero = ("z", "yh", "core")
    rows = P(("cuts",) + zero, None)
    return jax.shard_map(
        per_device,
        mesh=fine,
        in_specs=(rows, rows, P(zero, None), P(zero, None), P(zero), P(zero), P(zero)),
        out_specs=(rows, P(zero, None), P(zero, None), P(zero), P(zero), P(zero)),
        check_vma=False,
    )
```

```python
import functools

import jax
import jax.numpy as jnp
from jax import lax
from jax.experimental import pallas as pl
from jax.experimental.pallas import tpu as pltpu
from jax.sharding import Mesh
from jax.sharding import PartitionSpec as P

BLK = 176
TWO = 2 * BLK
WROWS = 192
WCOLS = 384
NZ, NY, NC = 8, 2, 2
NQ = NY * NC
NI = 8
SEQ = 128
NSEQ = NI * NQ


def pack_kernel(z_ref, x_hbm, c_hbm, out_ref, x_s, c_s, in_sem):
    wide = 2 * NQ * BLK
    loads = []
    for p in range(NZ // 2):
        for k, (src, dst) in enumerate(((x_hbm, x_s), (c_hbm, c_s))):
            cols = slice(p * wide, (p + 1) * wide)
            loads.append(pltpu.make_async_copy(src.at[:, cols], dst.at[:, cols], in_sem.at[k, p]))
            loads[-1].start()
    turn = z_ref[0] * NQ
    for p in range(NZ // 2):
        for k, ref in enumerate((x_s, c_s)):
            loads[2 * p + k].wait()
            turned = ref[:, p * wide : (p + 1) * wide].T
            for h in range(2 * NQ):
                out_ref[(2 * NQ * p + h) ^ turn, k * BLK : (k + 1) * BLK, :] = turned[h * BLK : (h + 1) * BLK]


def unpack_kernel(z_ref, in_ref, out_hbm, out_s, out_sem):
    wide = 2 * NQ * BLK
    turn = z_ref[0] * NQ
    stores = []
    for p in range(NZ // 2):
        cols = slice(p * wide, (p + 1) * wide)
        heads = [in_ref[(2 * NQ * p + h) ^ turn] for h in range(2 * NQ)]
        out_s[:, cols] = jnp.concatenate(heads, axis=0).T
        stores.append(pltpu.make_async_copy(out_s.at[:, cols], out_hbm.at[:, cols], out_sem.at[p]))
        stores[-1].start()
    for copy in stores:
        copy.wait()


SMEM = pl.BlockSpec(memory_space=pltpu.SMEM)
ANY = pl.BlockSpec(memory_space=pl.ANY)
VMEM = pl.BlockSpec(memory_space=pltpu.VMEM)


def kept(*arrays, where=pltpu.VMEM):
    return [pltpu.with_memory_space_constraint(a, where) for a in arrays]


def params(mebibytes):
    return pltpu.CompilerParams(vmem_limit_bytes=mebibytes * 1024 * 1024)


def pack(z, x, c, interpret=False):
    return pl.pallas_call(
        pack_kernel,
        in_specs=[SMEM, ANY, ANY],
        out_specs=VMEM,
        out_shape=pltpu.VMEM((NSEQ, TWO, SEQ), x.dtype),
        scratch_shapes=[
            pltpu.VMEM(x.shape, x.dtype),
            pltpu.VMEM(x.shape, x.dtype),
            pltpu.SemaphoreType.DMA((2, NZ // 2)),
        ],
        compiler_params=params(16),
        interpret=interpret,
    )(z, *kept(x, c, where=pltpu.HBM))


def unpack(z, y, interpret=False):
    return pl.pallas_call(
        unpack_kernel,
        in_specs=[SMEM, VMEM],
        out_specs=ANY,
        out_shape=pltpu.HBM((SEQ, NSEQ * BLK), y.dtype),
        scratch_shapes=[pltpu.VMEM((SEQ, NSEQ * BLK), y.dtype), pltpu.SemaphoreType.DMA((NZ // 2,))],
        compiler_params=params(16),
        interpret=interpret,
    )(z, *kept(y))


LN2 = 0.6931471805599453
LOG2E = 1.4426950408889634


def sigmoid(pre):
    return pl.reciprocal(1.0 + jnp.exp2(jnp.minimum(pre * -LOG2E, 115.0)), approx=True)


def one_minus_square(u):
    series, power = 0.0, 1.0
    terms = []
    for k in range(1, 7):
        power = power * (2.0 * LN2) / k
        terms.append(-power)
    series = terms[-1]
    for t in terms[-2::-1]:
        series = series * u + t
    return series * u


CH = 16


def main_kernel(
    factor, m_ref, w_ref, wt_ref, out_ref, g_ref,
    tri, x_s, pre_s, d_s, u_s, rest_s, own_s, f1_s, gain_s, drive_s, ub_s, log_s,
    fwd_in, rev_in, fwd_s, rev_s, coef_s, q_s,
):
    f32, bf16 = jnp.float32, jnp.bfloat16
    row = lax.broadcasted_iota(jnp.int32, (WROWS - BLK, NSEQ * SEQ), 0)
    x_s[BLK:, :] = jnp.where(row == 0, 1.0, 0.0).astype(x_s.dtype)
    decay = wt_ref[:BLK, BLK + 1 : BLK + 2].astype(f32)
    soft = jnp.maximum(decay, 0.0) + jnp.log1p(jnp.exp(-jnp.abs(decay)))
    coef_s[...] = jnp.broadcast_to((-8.0 * LOG2E) * soft, (BLK, SEQ))
    q_s[...] = jnp.zeros_like(q_s)
    src = lax.broadcasted_iota(jnp.int32, (2 * SEQ, 2 * SEQ), 0)
    dst = lax.broadcasted_iota(jnp.int32, (2 * SEQ, 2 * SEQ), 1)
    same = (src < SEQ) == (dst < SEQ)
    for k, seen in enumerate((src <= dst, src < dst, src >= dst)):
        tri[k] = jnp.where(seen & same, 1.0, 0.0).astype(bf16)

    def each(body, first=0, last=NSEQ // 2):
        def two(p, _):
            for half in range(2):
                s = 2 * p + half
                cols = pl.ds(pl.multiple_of(s * SEQ, SEQ), SEQ)
                for r in range(0, BLK, CH):
                    rows = pl.ds(pl.multiple_of(p * BLK + r, 16), CH)
                    body(s, r, cols, (rows, slice(half * SEQ, (half + 1) * SEQ)))
            return 0

        lax.fori_loop(first, last, two, 0)

    def gates(s, r, cols, at):
        x = m_ref[s, r : r + CH, :].astype(f32)
        rgate = sigmoid(pre_s[r : r + CH, cols])
        igate = 0.5 + 0.5 * jnp.tanh(0.5 * pre_s[BLK + r : BLK + r + CH, cols])
        u = coef_s[r : r + CH, :] * rgate
        var = one_minus_square(u)
        inv = lax.rsqrt(var)
        scale = var * inv
        ix = igate * x
        drive = scale * ix
        u_s[at] = u
        rest_s[at] = LN2 - LN2 * rgate
        own_s[at] = ix * (inv - scale)
        f1_s[at] = drive - drive * igate
        gain_s[at] = scale * igate
        drive_s[at] = drive
        ub_s[at] = u.astype(bf16)

    for s in range(NSEQ):
        x_s[:BLK, s * SEQ : (s + 1) * SEQ] = m_ref[s, :BLK, :]
    pre_s[...] = jnp.dot(wt_ref[...], x_s[...], preferred_element_type=f32)
    each(gates)
    log_s[...] = jnp.dot(ub_s[...], tri[0], preferred_element_type=f32)

    def weigh(s, r, cols, at):
        total = log_s[at]
        cot = m_ref[s, BLK + r : BLK + r + CH, :].astype(f32)
        fwd_in[at] = (drive_s[at] * jnp.exp2(-total)).astype(bf16)
        rev_in[at] = (cot * jnp.exp2(total)).astype(bf16)

    each(weigh)
    fwd_s[...] = jnp.dot(fwd_in[...], tri[1], preferred_element_type=f32)
    rev_s[...] = jnp.dot(rev_in[...], tri[2], preferred_element_type=f32)

    def deltas(s, r, cols, at):
        total = log_s[at]
        adj = rev_s[at] * jnp.exp2(-total)
        dlog = adj * (fwd_s[at] * jnp.exp2(total) - own_s[at])
        v = dlog * u_s[at]
        q_s[r : r + CH, :] += v
        d_s[r : r + CH, cols] = (v * rest_s[at]).astype(bf16)
        d_s[BLK + r : BLK + r + CH, cols] = (adj * f1_s[at]).astype(bf16)
        pre_s[r : r + CH, cols] = adj * gain_s[at]

    each(deltas)

    back = jnp.dot(w_ref[:BLK, :TWO], d_s[...], preferred_element_type=f32)
    for s in range(NSEQ):
        cols = slice(s * SEQ, (s + 1) * SEQ)
        out_ref[s] = (back[:, cols] + pre_s[:BLK, cols]).astype(out_ref.dtype)

    nt = (((1,), (1,)), ((), ()))
    grad = lax.dot_general(x_s[...], d_s[...], nt, preferred_element_type=f32) * factor
    g_ref[:, :TWO] = grad.astype(g_ref.dtype)
    g_ref[:, TWO:] = jnp.zeros((WROWS, WCOLS - TWO), g_ref.dtype)
    decay_row = jnp.sum((q_s[...] / coef_s[...]).T, axis=0, keepdims=True) * (-8.0 * factor)
    tail = grad[BLK:, :BLK]
    row = lax.broadcasted_iota(jnp.int32, tail.shape, 0)
    g_ref[BLK:, :BLK] = jnp.where(row == 1, decay_row, tail).astype(g_ref.dtype)


def main_call(factor, m, w, wt, grad_dtype=jnp.bfloat16, interpret=False):
    f32, bf16 = jnp.float32, jnp.bfloat16
    vmem = pltpu.VMEM
    flat, half = (vmem((NSEQ // 2 * BLK, 2 * SEQ), kind) for kind in (f32, bf16))
    return pl.pallas_call(
        functools.partial(main_kernel, factor),
        out_shape=[vmem((NSEQ, BLK, SEQ), bf16), vmem((WROWS, WCOLS), grad_dtype)],
        in_specs=[VMEM] * 3,
        out_specs=[VMEM] * 2,
        scratch_shapes=[
            vmem((3, 2 * SEQ, 2 * SEQ), bf16),
            vmem((WROWS, NSEQ * SEQ), bf16),
            vmem((TWO, NSEQ * SEQ), f32),
            vmem((TWO, NSEQ * SEQ), bf16),
            flat, flat, flat, flat, flat, flat,
            half, flat, half, half, flat, flat,
            vmem((BLK, SEQ), f32),
            vmem((BLK, SEQ), f32),
        ],
        compiler_params=params(48),
        interpret=interpret,
    )(*kept(m, w, wt))


def finish_kernel(count, *refs):
    parts, decay_ref, outs = refs[:count], refs[count], refs[count + 2 :]
    f32 = jnp.float32
    full = sum(p[...].astype(f32) for p in parts)
    wa, wx, ba, bx, da = outs
    right = pltpu.roll(full, WCOLS - BLK, 1)
    wa[...] = full[:BLK, :BLK]
    wx[...] = right[:BLK, :BLK]
    ba[...] = full[BLK : BLK + 1, :BLK]
    bx[...] = right[BLK : BLK + 1, :BLK]
    own = 1.0 / (1.0 + jnp.exp(-decay_ref[...].astype(f32)))
    da[...] = full[BLK + 1 : BLK + 2, :BLK] * own


def finish(parts, decay, after):
    square, row = (jax.ShapeDtypeStruct((n, BLK), jnp.float32) for n in (BLK, 1))
    return pl.pallas_call(
        functools.partial(finish_kernel, len(parts)),
        in_specs=[VMEM] * (len(parts) + 1) + [ANY],
        out_specs=[VMEM] * 5,
        out_shape=[square, square, row, row, row],
        compiler_params=params(16),
    )(*kept(*parts, decay.reshape(1, BLK)), *kept(after, where=pltpu.HBM))


def wire(wa, wx, ba, bx, decay):
    bf16 = jnp.bfloat16
    tail = jnp.zeros((WROWS - BLK - 2, TWO), bf16)
    body = jnp.concatenate(
        [
            jnp.concatenate([wa, wx], axis=1),
            jnp.concatenate([ba, bx])[None],
            jnp.concatenate([decay, jnp.zeros((BLK,), bf16)])[None],
            tail,
        ],
        axis=0,
    )
    return jnp.pad(body, ((0, 0), (0, WCOLS - TWO)))


def per_device(inputs, cotangent, wa, wx, ba, bx, decay):
    bf16, f32 = jnp.bfloat16, jnp.float32
    plane, line = ("cuts", "yh", "core"), ("cuts", "z")
    z = lax.axis_index("z").astype(jnp.int32).reshape(1)
    everyone = [(i, k) for i in range(NI) for k in range(NZ)]
    fetch = [(i * NZ + (k ^ i), i * NZ + k) for i, k in everyone]
    across = [(i * NZ + (k ^ i), (i ^ 1) * NZ + k) for i, k in everyone]

    got = lax.all_to_all(pack(z, inputs, cotangent), plane, 0, 0, tiled=True)
    w = lax.ppermute(wire(wa, wx, ba, bx, decay), line, fetch)
    total = SEQ * NSEQ * NZ
    out, grads = main_call(float(total) ** -0.5, got, w, w[:, :TWO].T)
    near, far = lax.ppermute(grads, line, fetch), lax.ppermute(grads, line, across)
    back = lax.all_to_all(out, plane, 0, 0, tiled=True)
    near, far, back = lax.optimization_barrier((near, far, back))
    pair = (near.astype(f32) + far.astype(f32)).astype(bf16)
    parts = [pair] + [lax.ppermute(pair, "cuts", [(i, (i + 2 * k) % NI) for i in range(NI)]) for k in (1, 2, 3)]
    input_grad = unpack(z, back)
    grad_a, grad_x, *rows = finish(parts, decay, input_grad)
    return (input_grad, grad_a, grad_x, *(row.reshape(BLK) for row in rows))


def solution(mesh):
    fine = Mesh(mesh.devices.reshape(NI, NZ, NY, NC), ("cuts", "z", "yh", "core"))
    zero = ("z", "yh", "core")
    rows = P(("cuts",) + zero, None)
    return jax.shard_map(
        per_device,
        mesh=fine,
        in_specs=(rows, rows, P(zero, None), P(zero, None), P(zero), P(zero), P(zero)),
        out_specs=(rows, P(zero, None), P(zero, None), P(zero), P(zero), P(zero)),
        check_vma=False,
    )
```

```python
import functools

import jax
import jax.numpy as jnp
from jax import lax
from jax.experimental import pallas as pl
from jax.experimental.pallas import tpu as pltpu
from jax.sharding import Mesh
from jax.sharding import PartitionSpec as P

BLK = 176
TWO = 2 * BLK
WROWS = 192
WCOLS = 384
NZ, NY, NC = 8, 2, 2
NQ = NY * NC
NI = 8
SEQ = 128
NSEQ = NI * NQ


def pack_kernel(z_ref, x_hbm, c_hbm, out_hbm, x_s, c_s, out_s, in_sem, out_sem):
    wide = 2 * NQ * BLK
    loads = []
    for p in range(NZ // 2):
        for k, (src, dst) in enumerate(((x_hbm, x_s), (c_hbm, c_s))):
            cols = slice(p * wide, (p + 1) * wide)
            loads.append(pltpu.make_async_copy(src.at[:, cols], dst.at[:, cols], in_sem.at[k, p]))
            loads[-1].start()
    stores = []
    for p in range(NZ // 2):
        turned = []
        for k, ref in enumerate((x_s, c_s)):
            loads[2 * p + k].wait()
            turned.append(ref[:, p * wide : (p + 1) * wide].T)
        for half in range(2):
            group = (2 * p + half) ^ z_ref[0]
            for q in range(NQ):
                rows = slice((half * NQ + q) * BLK, (half * NQ + q + 1) * BLK)
                for k in range(2):
                    out_s[group * NQ + q, k * BLK : (k + 1) * BLK, :] = turned[k][rows]
            slots = pl.ds(group * NQ, NQ)
            stores.append(pltpu.make_async_copy(out_s.at[slots], out_hbm.at[slots], out_sem.at[2 * p + half]))
            stores[-1].start()
    for copy in stores:
        copy.wait()


def unpack_kernel(z_ref, in_ref, out_hbm, out_s, out_sem):
    wide = 2 * NQ * BLK
    turn = z_ref[0] * NQ
    stores = []
    for p in range(NZ // 2):
        cols = slice(p * wide, (p + 1) * wide)
        heads = [in_ref[(2 * NQ * p + h) ^ turn] for h in range(2 * NQ)]
        out_s[:, cols] = jnp.concatenate(heads, axis=0).T
        stores.append(pltpu.make_async_copy(out_s.at[:, cols], out_hbm.at[:, cols], out_sem.at[p]))
        stores[-1].start()
    for copy in stores:
        copy.wait()


SMEM = pl.BlockSpec(memory_space=pltpu.SMEM)
ANY = pl.BlockSpec(memory_space=pl.ANY)
VMEM = pl.BlockSpec(memory_space=pltpu.VMEM)


def kept(*arrays, where=pltpu.VMEM):
    return [pltpu.with_memory_space_constraint(a, where) for a in arrays]


def params(mebibytes):
    return pltpu.CompilerParams(vmem_limit_bytes=mebibytes * 1024 * 1024)


def pack(z, x, c, interpret=False):
    sem = pltpu.SemaphoreType.DMA
    return pl.pallas_call(
        pack_kernel,
        in_specs=[SMEM, ANY, ANY],
        out_specs=ANY,
        out_shape=pltpu.HBM((NSEQ, TWO, SEQ), x.dtype),
        scratch_shapes=[
            pltpu.VMEM(x.shape, x.dtype),
            pltpu.VMEM(x.shape, x.dtype),
            pltpu.VMEM((NSEQ, TWO, SEQ), x.dtype),
            sem((2, NZ // 2)),
            sem((NZ,)),
        ],
        compiler_params=params(16),
        interpret=interpret,
    )(z, *kept(x, c, where=pltpu.HBM))


def unpack(z, y, interpret=False):
    return pl.pallas_call(
        unpack_kernel,
        in_specs=[SMEM, VMEM],
        out_specs=ANY,
        out_shape=pltpu.HBM((SEQ, NSEQ * BLK), y.dtype),
        scratch_shapes=[pltpu.VMEM((SEQ, NSEQ * BLK), y.dtype), pltpu.SemaphoreType.DMA((NZ // 2,))],
        compiler_params=params(16),
        interpret=interpret,
    )(z, *kept(y))


LN2 = 0.6931471805599453
LOG2E = 1.4426950408889634


def sigmoid(pre):
    return pl.reciprocal(1.0 + jnp.exp2(jnp.minimum(pre * -LOG2E, 115.0)), approx=True)


def one_minus_square(u):
    series, power = 0.0, 1.0
    terms = []
    for k in range(1, 7):
        power = power * (2.0 * LN2) / k
        terms.append(-power)
    series = terms[-1]
    for t in terms[-2::-1]:
        series = series * u + t
    return series * u


CH = 16
PART = 8


def main_kernel(
    m_ref, w_ref, wt_ref, out_hbm, x_s, d_s, q_s, coef_s,
    out_ref, tri, pre_s, u_s, own_s, f1_s, gain_s, ub_s, log_s, fwd_in, rev_in, fwd_s, rev_s, back_s, out_sem,
):
    f32, bf16 = jnp.float32, jnp.bfloat16
    row = lax.broadcasted_iota(jnp.int32, (WROWS - BLK, NSEQ * SEQ), 0)
    x_s[BLK:, :] = jnp.where(row == 0, 1.0, 0.0).astype(x_s.dtype)
    decay = wt_ref[:BLK, BLK + 1 : BLK + 2].astype(f32)
    soft = jnp.maximum(decay, 0.0) + jnp.log1p(jnp.exp(-jnp.abs(decay)))
    coef_s[...] = jnp.broadcast_to((-8.0 * LOG2E) * soft, (BLK, SEQ))
    back_s[...] = LN2 / coef_s[...]
    q_s[...] = jnp.zeros_like(q_s)
    src = lax.broadcasted_iota(jnp.int32, (2 * SEQ, 2 * SEQ), 0)
    dst = lax.broadcasted_iota(jnp.int32, (2 * SEQ, 2 * SEQ), 1)
    same = (src < SEQ) == (dst < SEQ)
    for k, seen in enumerate((src <= dst, src < dst, src >= dst)):
        tri[k] = jnp.where(seen & same, 1.0, 0.0).astype(bf16)

    for s in range(NSEQ):
        x_s[:BLK, s * SEQ : (s + 1) * SEQ] = m_ref[s, :BLK, :]
    pre_s[...] = jnp.dot(wt_ref[...], x_s[...], preferred_element_type=f32)

    def each(body):
        def two(p, _):
            for r in range(0, BLK, CH):
                body(p, r, pl.ds(pl.multiple_of(p * BLK + r, 16), CH))
            return 0

        lax.fori_loop(0, NSEQ // 2, two, 0, unroll=2)

    def halves(p):
        for half in range(2):
            s = 2 * p + half
            yield s, pl.ds(pl.multiple_of(s * SEQ, SEQ), SEQ), slice(half * SEQ, (half + 1) * SEQ)

    def gates(p, r, rows):
        for s, cols, side in halves(p):
            x = m_ref[s, r : r + CH, :].astype(f32)
            rgate = sigmoid(pre_s[r : r + CH, cols])
            igate = 0.5 + 0.5 * jnp.tanh(0.5 * pre_s[BLK + r : BLK + r + CH, cols])
            u = coef_s[r : r + CH, :] * rgate
            var = one_minus_square(u)
            inv = lax.rsqrt(var)
            scale = var * inv
            gain = scale * igate
            drive = gain * x
            u_s[rows, side] = u
            own_s[rows, side] = igate * x * (inv - scale)
            f1_s[rows, side] = drive - drive * igate
            gain_s[rows, side] = gain
            ub_s[rows, side] = u.astype(bf16)

    each(gates)
    log_s[...] = jnp.dot(ub_s[...], tri[0], preferred_element_type=f32)

    def weigh(p, r, rows):
        for s, cols, side in halves(p):
            total = log_s[rows, side]
            x = m_ref[s, r : r + CH, :].astype(f32)
            cot = m_ref[s, BLK + r : BLK + r + CH, :].astype(f32)
            fwd_in[rows, side] = (gain_s[rows, side] * x * jnp.exp2(-total)).astype(bf16)
            rev_in[rows, side] = (cot * jnp.exp2(total)).astype(bf16)

    each(weigh)
    fwd_s[...] = jnp.dot(fwd_in[...], tri[1], preferred_element_type=f32)
    rev_s[...] = jnp.dot(rev_in[...], tri[2], preferred_element_type=f32)

    def deltas(p, r, rows):
        part = q_s[r : r + CH, :]
        for _, cols, side in halves(p):
            total = log_s[rows, side]
            u = u_s[rows, side]
            adj = rev_s[rows, side] * jnp.exp2(-total)
            v = adj * (fwd_s[rows, side] * jnp.exp2(total) - own_s[rows, side]) * u
            part = part + v
            rest = LN2 - u * back_s[r : r + CH, :]
            d_s[r : r + CH, cols] = (v * rest).astype(bf16)
            d_s[BLK + r : BLK + r + CH, cols] = (adj * f1_s[rows, side]).astype(bf16)
            pre_s[r : r + CH, cols] = adj * gain_s[rows, side]
        q_s[r : r + CH, :] = part

    each(deltas)

    stores = []
    for j in range(0, NSEQ, PART):
        cols = slice(j * SEQ, (j + PART) * SEQ)
        back = jnp.dot(w_ref[:BLK, :TWO], d_s[:, cols], preferred_element_type=f32) + pre_s[:BLK, cols]
        for s in range(PART):
            out_ref[j + s] = back[:, s * SEQ : (s + 1) * SEQ].astype(out_ref.dtype)
        block = pl.ds(j, PART)
        stores.append(pltpu.make_async_copy(out_ref.at[block], out_hbm.at[block], out_sem.at[j // PART]))
        stores[-1].start()
    for copy in stores:
        copy.wait()


def sums_kernel(factor, x_ref, d_ref, q_ref, coef_ref, g_ref):
    nt = (((1,), (1,)), ((), ()))
    grad = lax.dot_general(x_ref[...], d_ref[...], nt, preferred_element_type=jnp.float32) * factor
    g_ref[:, :TWO] = grad.astype(g_ref.dtype)
    g_ref[:, TWO:] = jnp.zeros((WROWS, WCOLS - TWO), g_ref.dtype)
    decay = jnp.sum((q_ref[...] / coef_ref[...]).T, axis=0, keepdims=True) * (-8.0 * factor)
    tail = grad[BLK:, :BLK]
    row = lax.broadcasted_iota(jnp.int32, tail.shape, 0)
    g_ref[BLK:, :BLK] = jnp.where(row == 1, decay, tail).astype(g_ref.dtype)


def main_call(m, w, wt, interpret=False):
    f32, bf16 = jnp.float32, jnp.bfloat16
    vmem = pltpu.VMEM
    flat, half = (vmem((NSEQ // 2 * BLK, 2 * SEQ), kind) for kind in (f32, bf16))
    return pl.pallas_call(
        main_kernel,
        out_shape=[
            pltpu.HBM((NSEQ, BLK, SEQ), bf16),
            vmem((WROWS, NSEQ * SEQ), bf16),
            vmem((TWO, NSEQ * SEQ), bf16),
            vmem((BLK, SEQ), f32),
            vmem((BLK, SEQ), f32),
        ],
        in_specs=[VMEM] * 3,
        out_specs=[ANY] + [VMEM] * 4,
        scratch_shapes=[
            vmem((NSEQ, BLK, SEQ), bf16),
            vmem((3, 2 * SEQ, 2 * SEQ), bf16),
            vmem((TWO, NSEQ * SEQ), f32),
            flat, flat, flat, flat,
            half, flat, half, half, flat, flat,
            vmem((BLK, SEQ), f32),
            pltpu.SemaphoreType.DMA((NSEQ // PART,)),
        ],
        compiler_params=params(44),
        interpret=interpret,
    )(*kept(m, w, wt))


def sums_call(factor, x, d, q, coef, grad_dtype=jnp.bfloat16, interpret=False):
    return pl.pallas_call(
        functools.partial(sums_kernel, factor),
        out_shape=pltpu.VMEM((WROWS, WCOLS), grad_dtype),
        in_specs=[VMEM] * 4,
        out_specs=VMEM,
        compiler_params=params(16),
        interpret=interpret,
    )(*kept(x, d, q, coef))


def finish_kernel(count, *refs):
    parts, decay_ref, outs = refs[:count], refs[count], refs[count + 2 :]
    f32 = jnp.float32
    full = sum(p[...].astype(f32) for p in parts)
    wa, wx, ba, bx, da = outs
    right = pltpu.roll(full, WCOLS - BLK, 1)
    wa[...] = full[:BLK, :BLK]
    wx[...] = right[:BLK, :BLK]
    ba[...] = full[BLK : BLK + 1, :BLK]
    bx[...] = right[BLK : BLK + 1, :BLK]
    own = 1.0 / (1.0 + jnp.exp(-decay_ref[...].astype(f32)))
    da[...] = full[BLK + 1 : BLK + 2, :BLK] * own


def finish(parts, decay, after):
    square, row = (jax.ShapeDtypeStruct((n, BLK), jnp.float32) for n in (BLK, 1))
    return pl.pallas_call(
        functools.partial(finish_kernel, len(parts)),
        in_specs=[VMEM] * (len(parts) + 1) + [ANY],
        out_specs=[VMEM] * 5,
        out_shape=[square, square, row, row, row],
        compiler_params=params(16),
    )(*kept(*parts, decay.reshape(1, BLK)), *kept(after, where=pltpu.HBM))


def wire(wa, wx, ba, bx, decay):
    bf16 = jnp.bfloat16
    tail = jnp.zeros((WROWS - BLK - 2, TWO), bf16)
    body = jnp.concatenate(
        [
            jnp.concatenate([wa, wx], axis=1),
            jnp.concatenate([ba, bx])[None],
            jnp.concatenate([decay, jnp.zeros((BLK,), bf16)])[None],
            tail,
        ],
        axis=0,
    )
    return jnp.pad(body, ((0, 0), (0, WCOLS - TWO)))


def per_device(inputs, cotangent, wa, wx, ba, bx, decay):
    bf16, f32 = jnp.bfloat16, jnp.float32
    plane, line = ("cuts", "yh", "core"), ("cuts", "z")
    z = lax.axis_index("z").astype(jnp.int32).reshape(1)
    everyone = [(i, k) for i in range(NI) for k in range(NZ)]
    fetch = [(i * NZ + (k ^ i), i * NZ + k) for i, k in everyone]
    across = [(i * NZ + (k ^ i), (i ^ 1) * NZ + k) for i, k in everyone]

    got = lax.all_to_all(pack(z, inputs, cotangent), plane, 0, 0, tiled=True)
    w = lax.ppermute(wire(wa, wx, ba, bx, decay), line, fetch)
    total = SEQ * NSEQ * NZ
    out, *kept_here = main_call(got, w, w[:, :TWO].T)
    back = lax.all_to_all(out, plane, 0, 0, tiled=True)
    grads = sums_call(float(total) ** -0.5, *kept_here)
    near, far = lax.ppermute(grads, line, fetch), lax.ppermute(grads, line, across)
    near, far, back = lax.optimization_barrier((near, far, back))
    pair = (near.astype(f32) + far.astype(f32)).astype(bf16)
    parts = [pair] + [lax.ppermute(pair, "cuts", [(i, (i + 2 * k) % NI) for i in range(NI)]) for k in (1, 2, 3)]
    input_grad = unpack(z, back)
    grad_a, grad_x, *rows = finish(parts, decay, input_grad)
    return (input_grad, grad_a, grad_x, *(row.reshape(BLK) for row in rows))


def solution(mesh):
    fine = Mesh(mesh.devices.reshape(NI, NZ, NY, NC), ("cuts", "z", "yh", "core"))
    zero = ("z", "yh", "core")
    rows = P(("cuts",) + zero, None)
    return jax.shard_map(
        per_device,
        mesh=fine,
        in_specs=(rows, rows, P(zero, None), P(zero, None), P(zero), P(zero), P(zero)),
        out_specs=(rows, P(zero, None), P(zero, None), P(zero), P(zero), P(zero)),
        check_vma=False,
    )
```

```python
import functools

import jax
import jax.numpy as jnp
from jax import lax
from jax.experimental import pallas as pl
from jax.experimental.pallas import tpu as pltpu
from jax.sharding import Mesh
from jax.sharding import PartitionSpec as P

BLK = 176
TWO = 2 * BLK
WROWS = 192
WCOLS = 384
NZ, NY, NC = 8, 2, 2
NQ = NY * NC
NI = 8
SEQ = 128
NSEQ = NI * NQ


def pack_kernel(z_ref, x_hbm, c_hbm, out_hbm, x_s, c_s, out_s, in_sem, out_sem):
    wide = 2 * NQ * BLK
    loads = []
    for p in range(NZ // 2):
        for k, (src, dst) in enumerate(((x_hbm, x_s), (c_hbm, c_s))):
            cols = slice(p * wide, (p + 1) * wide)
            loads.append(pltpu.make_async_copy(src.at[:, cols], dst.at[:, cols], in_sem.at[k, p]))
            loads[-1].start()
    stores = []
    for p in range(NZ // 2):
        turned = []
        for k, ref in enumerate((x_s, c_s)):
            loads[2 * p + k].wait()
            turned.append(ref[:, p * wide : (p + 1) * wide].T)
        for half in range(2):
            group = (2 * p + half) ^ z_ref[0]
            for q in range(NQ):
                rows = slice((half * NQ + q) * BLK, (half * NQ + q + 1) * BLK)
                for k in range(2):
                    out_s[group * NQ + q, k * BLK : (k + 1) * BLK, :] = turned[k][rows]
            slots = pl.ds(group * NQ, NQ)
            stores.append(pltpu.make_async_copy(out_s.at[slots], out_hbm.at[slots], out_sem.at[2 * p + half]))
            stores[-1].start()
    for copy in stores:
        copy.wait()


def unpack_kernel(z_ref, in_ref, out_hbm, out_s, out_sem):
    wide = 2 * NQ * BLK
    turn = z_ref[0] * NQ
    stores = []
    for p in range(NZ // 2):
        cols = slice(p * wide, (p + 1) * wide)
        heads = [in_ref[(2 * NQ * p + h) ^ turn] for h in range(2 * NQ)]
        out_s[:, cols] = jnp.concatenate(heads, axis=0).T
        stores.append(pltpu.make_async_copy(out_s.at[:, cols], out_hbm.at[:, cols], out_sem.at[p]))
        stores[-1].start()
    for copy in stores:
        copy.wait()


SMEM = pl.BlockSpec(memory_space=pltpu.SMEM)
ANY = pl.BlockSpec(memory_space=pl.ANY)
VMEM = pl.BlockSpec(memory_space=pltpu.VMEM)


def kept(*arrays, where=pltpu.VMEM):
    return [pltpu.with_memory_space_constraint(a, where) for a in arrays]


def params(mebibytes):
    return pltpu.CompilerParams(vmem_limit_bytes=mebibytes * 1024 * 1024)


def pack(z, x, c, interpret=False):
    sem = pltpu.SemaphoreType.DMA
    return pl.pallas_call(
        pack_kernel,
        in_specs=[SMEM, ANY, ANY],
        out_specs=ANY,
        out_shape=pltpu.HBM((NSEQ, TWO, SEQ), x.dtype),
        scratch_shapes=[
            pltpu.VMEM(x.shape, x.dtype),
            pltpu.VMEM(x.shape, x.dtype),
            pltpu.VMEM((NSEQ, TWO, SEQ), x.dtype),
            sem((2, NZ // 2)),
            sem((NZ,)),
        ],
        compiler_params=params(16),
        interpret=interpret,
    )(z, *kept(x, c, where=pltpu.HBM))


def unpack(z, y, interpret=False):
    return pl.pallas_call(
        unpack_kernel,
        in_specs=[SMEM, VMEM],
        out_specs=ANY,
        out_shape=pltpu.HBM((SEQ, NSEQ * BLK), y.dtype),
        scratch_shapes=[pltpu.VMEM((SEQ, NSEQ * BLK), y.dtype), pltpu.SemaphoreType.DMA((NZ // 2,))],
        compiler_params=params(16),
        interpret=interpret,
    )(z, *kept(y))


LN2 = 0.6931471805599453
LOG2E = 1.4426950408889634


def sigmoid(pre):
    return pl.reciprocal(1.0 + jnp.exp2(jnp.minimum(pre * -LOG2E, 115.0)), approx=True)


def one_minus_square(u):
    series, power = 0.0, 1.0
    terms = []
    for k in range(1, 7):
        power = power * (2.0 * LN2) / k
        terms.append(-power)
    series = terms[-1]
    for t in terms[-2::-1]:
        series = series * u + t
    return series * u


CH = 16
PART = 8


def main_kernel(
    factor, m_ref, w_ref, wt_ref, out_hbm, g_ref,
    x_s, d_s, q_s, coef_s, out_ref, tri, pre_s, u_s, own_s, f1_s, gain_s, ub_s, log_s, fwd_in, rev_in, fwd_s, rev_s, back_s, out_sem,
):
    f32, bf16 = jnp.float32, jnp.bfloat16
    row = lax.broadcasted_iota(jnp.int32, (WROWS - BLK, NSEQ * SEQ), 0)
    x_s[BLK:, :] = jnp.where(row == 0, 1.0, 0.0).astype(x_s.dtype)
    decay = wt_ref[:BLK, BLK + 1 : BLK + 2].astype(f32)
    soft = jnp.maximum(decay, 0.0) + jnp.log1p(jnp.exp(-jnp.abs(decay)))
    coef_s[...] = jnp.broadcast_to((-8.0 * LOG2E) * soft, (BLK, SEQ))
    back_s[...] = LN2 / coef_s[...]
    q_s[...] = jnp.zeros_like(q_s)
    src = lax.broadcasted_iota(jnp.int32, (2 * SEQ, 2 * SEQ), 0)
    dst = lax.broadcasted_iota(jnp.int32, (2 * SEQ, 2 * SEQ), 1)
    same = (src < SEQ) == (dst < SEQ)
    for k, seen in enumerate((src <= dst, src < dst, src >= dst)):
        tri[k] = jnp.where(seen & same, 1.0, 0.0).astype(bf16)

    for s in range(NSEQ):
        x_s[:BLK, s * SEQ : (s + 1) * SEQ] = m_ref[s, :BLK, :]
    pre_s[...] = jnp.dot(wt_ref[...], x_s[...], preferred_element_type=f32)

    def each(body):
        def two(p, _):
            for r in range(0, BLK, CH):
                body(p, r, pl.ds(pl.multiple_of(p * BLK + r, 16), CH))
            return 0

        lax.fori_loop(0, NSEQ // 2, two, 0, unroll=2)

    def halves(p):
        for half in range(2):
            s = 2 * p + half
            yield s, pl.ds(pl.multiple_of(s * SEQ, SEQ), SEQ), slice(half * SEQ, (half + 1) * SEQ)

    def gates(p, r, rows):
        for s, cols, side in halves(p):
            x = m_ref[s, r : r + CH, :].astype(f32)
            rgate = sigmoid(pre_s[r : r + CH, cols])
            igate = 0.5 + 0.5 * jnp.tanh(0.5 * pre_s[BLK + r : BLK + r + CH, cols])
            u = coef_s[r : r + CH, :] * rgate
            var = one_minus_square(u)
            inv = lax.rsqrt(var)
            scale = var * inv
            gain = scale * igate
            drive = gain * x
            u_s[rows, side] = u
            own_s[rows, side] = igate * x * (inv - scale)
            f1_s[rows, side] = drive - drive * igate
            gain_s[rows, side] = gain
            ub_s[rows, side] = u.astype(bf16)

    each(gates)
    log_s[...] = jnp.dot(ub_s[...], tri[0], preferred_element_type=f32)

    def weigh(p, r, rows):
        for s, cols, side in halves(p):
            total = log_s[rows, side]
            x = m_ref[s, r : r + CH, :].astype(f32)
            cot = m_ref[s, BLK + r : BLK + r + CH, :].astype(f32)
            fwd_in[rows, side] = (gain_s[rows, side] * x * jnp.exp2(-total)).astype(bf16)
            rev_in[rows, side] = (cot * jnp.exp2(total)).astype(bf16)

    each(weigh)
    fwd_s[...] = jnp.dot(fwd_in[...], tri[1], preferred_element_type=f32)
    rev_s[...] = jnp.dot(rev_in[...], tri[2], preferred_element_type=f32)

    def deltas(p, r, rows):
        part = q_s[r : r + CH, :]
        for _, cols, side in halves(p):
            total = log_s[rows, side]
            u = u_s[rows, side]
            adj = rev_s[rows, side] * jnp.exp2(-total)
            v = adj * (fwd_s[rows, side] * jnp.exp2(total) - own_s[rows, side]) * u
            part = part + v
            rest = LN2 - u * back_s[r : r + CH, :]
            d_s[r : r + CH, cols] = (v * rest).astype(bf16)
            d_s[BLK + r : BLK + r + CH, cols] = (adj * f1_s[rows, side]).astype(bf16)
            pre_s[r : r + CH, cols] = adj * gain_s[rows, side]
        q_s[r : r + CH, :] = part

    each(deltas)

    stores = []
    for j in range(0, NSEQ, PART):
        cols = slice(j * SEQ, (j + PART) * SEQ)
        back = jnp.dot(w_ref[:BLK, :TWO], d_s[:, cols], preferred_element_type=f32) + pre_s[:BLK, cols]
        for s in range(PART):
            out_ref[j + s] = back[:, s * SEQ : (s + 1) * SEQ].astype(out_ref.dtype)
        block = pl.ds(j, PART)
        stores.append(pltpu.make_async_copy(out_ref.at[block], out_hbm.at[block], out_sem.at[j // PART]))
        stores[-1].start()

    nt = (((1,), (1,)), ((), ()))
    grad = lax.dot_general(x_s[...], d_s[...], nt, preferred_element_type=f32) * factor
    g_ref[:, :TWO] = grad.astype(g_ref.dtype)
    g_ref[:, TWO:] = jnp.zeros((WROWS, WCOLS - TWO), g_ref.dtype)
    decay_row = jnp.sum((q_s[...] / coef_s[...]).T, axis=0, keepdims=True) * (-8.0 * factor)
    tail = grad[BLK:, :BLK]
    row = lax.broadcasted_iota(jnp.int32, tail.shape, 0)
    g_ref[BLK:, :BLK] = jnp.where(row == 1, decay_row, tail).astype(g_ref.dtype)
    for copy in stores:
        copy.wait()


def main_call(factor, m, w, wt, grad_dtype=jnp.bfloat16, interpret=False):
    f32, bf16 = jnp.float32, jnp.bfloat16
    vmem = pltpu.VMEM
    flat, half = (vmem((NSEQ // 2 * BLK, 2 * SEQ), kind) for kind in (f32, bf16))
    return pl.pallas_call(
        functools.partial(main_kernel, factor),
        out_shape=[pltpu.HBM((NSEQ, BLK, SEQ), bf16), vmem((WROWS, WCOLS), grad_dtype)],
        in_specs=[VMEM] * 3,
        out_specs=[ANY, VMEM],
        scratch_shapes=[
            vmem((WROWS, NSEQ * SEQ), bf16),
            vmem((TWO, NSEQ * SEQ), bf16),
            vmem((BLK, SEQ), f32),
            vmem((BLK, SEQ), f32),
            vmem((NSEQ, BLK, SEQ), bf16),
            vmem((3, 2 * SEQ, 2 * SEQ), bf16),
            vmem((TWO, NSEQ * SEQ), f32),
            flat, flat, flat, flat,
            half, flat, half, half, flat, flat,
            vmem((BLK, SEQ), f32),
            pltpu.SemaphoreType.DMA((NSEQ // PART,)),
        ],
        compiler_params=params(48),
        interpret=interpret,
    )(*kept(m, w, wt))


def finish_kernel(count, *refs):
    parts, decay_ref, outs = refs[:count], refs[count], refs[count + 2 :]
    f32 = jnp.float32
    full = sum(p[...].astype(f32) for p in parts)
    wa, wx, ba, bx, da = outs
    right = pltpu.roll(full, WCOLS - BLK, 1)
    wa[...] = full[:BLK, :BLK]
    wx[...] = right[:BLK, :BLK]
    ba[...] = full[BLK : BLK + 1, :BLK]
    bx[...] = right[BLK : BLK + 1, :BLK]
    own = 1.0 / (1.0 + jnp.exp(-decay_ref[...].astype(f32)))
    da[...] = full[BLK + 1 : BLK + 2, :BLK] * own


def finish(parts, decay, after):
    square, row = (jax.ShapeDtypeStruct((n, BLK), jnp.float32) for n in (BLK, 1))
    return pl.pallas_call(
        functools.partial(finish_kernel, len(parts)),
        in_specs=[VMEM] * (len(parts) + 1) + [ANY],
        out_specs=[VMEM] * 5,
        out_shape=[square, square, row, row, row],
        compiler_params=params(16),
    )(*kept(*parts, decay.reshape(1, BLK)), *kept(after, where=pltpu.HBM))


def wire(wa, wx, ba, bx, decay):
    bf16 = jnp.bfloat16
    tail = jnp.zeros((WROWS - BLK - 2, TWO), bf16)
    body = jnp.concatenate(
        [
            jnp.concatenate([wa, wx], axis=1),
            jnp.concatenate([ba, bx])[None],
            jnp.concatenate([decay, jnp.zeros((BLK,), bf16)])[None],
            tail,
        ],
        axis=0,
    )
    return jnp.pad(body, ((0, 0), (0, WCOLS - TWO)))


def per_device(inputs, cotangent, wa, wx, ba, bx, decay):
    bf16, f32 = jnp.bfloat16, jnp.float32
    plane, line = ("cuts", "yh", "core"), ("cuts", "z")
    z = lax.axis_index("z").astype(jnp.int32).reshape(1)
    everyone = [(i, k) for i in range(NI) for k in range(NZ)]
    fetch = [(i * NZ + (k ^ i), i * NZ + k) for i, k in everyone]
    across = [(i * NZ + (k ^ i), (i ^ 1) * NZ + k) for i, k in everyone]

    got = lax.all_to_all(pack(z, inputs, cotangent), plane, 0, 0, tiled=True)
    w = lax.ppermute(wire(wa, wx, ba, bx, decay), line, fetch)
    total = SEQ * NSEQ * NZ
    out, grads = main_call(float(total) ** -0.5, got, w, w[:, :TWO].T)
    back = lax.all_to_all(out, plane, 0, 0, tiled=True)
    near, far = lax.ppermute(grads, line, fetch), lax.ppermute(grads, line, across)
    near, far, back = lax.optimization_barrier((near, far, back))
    pair = (near.astype(f32) + far.astype(f32)).astype(bf16)
    parts = [pair] + [lax.ppermute(pair, "cuts", [(i, (i + 2 * k) % NI) for i in range(NI)]) for k in (1, 2, 3)]
    input_grad = unpack(z, back)
    grad_a, grad_x, *rows = finish(parts, decay, input_grad)
    return (input_grad, grad_a, grad_x, *(row.reshape(BLK) for row in rows))


def solution(mesh):
    fine = Mesh(mesh.devices.reshape(NI, NZ, NY, NC), ("cuts", "z", "yh", "core"))
    zero = ("z", "yh", "core")
    rows = P(("cuts",) + zero, None)
    return jax.shard_map(
        per_device,
        mesh=fine,
        in_specs=(rows, rows, P(zero, None), P(zero, None), P(zero), P(zero), P(zero)),
        out_specs=(rows, P(zero, None), P(zero, None), P(zero), P(zero), P(zero)),
        check_vma=False,
    )
```

```python
import functools

import jax
import jax.numpy as jnp
from jax import lax
from jax.experimental import pallas as pl
from jax.experimental.pallas import tpu as pltpu
from jax.sharding import Mesh
from jax.sharding import PartitionSpec as P

BLK = 176
TWO = 2 * BLK
WROWS = 192
WCOLS = 384
NZ, NY, NC = 8, 2, 2
NQ = NY * NC
NI = 8
SEQ = 128
NSEQ = NI * NQ


def pack_kernel(z_ref, x_hbm, c_hbm, out_hbm, x_s, c_s, out_s, in_sem, out_sem):
    wide = 2 * NQ * BLK
    loads = []
    for p in range(NZ // 2):
        for k, (src, dst) in enumerate(((x_hbm, x_s), (c_hbm, c_s))):
            cols = slice(p * wide, (p + 1) * wide)
            loads.append(pltpu.make_async_copy(src.at[:, cols], dst.at[:, cols], in_sem.at[k, p]))
            loads[-1].start()
    stores = []
    for p in range(NZ // 2):
        turned = []
        for k, ref in enumerate((x_s, c_s)):
            loads[2 * p + k].wait()
            turned.append(ref[:, p * wide : (p + 1) * wide].T)
        for half in range(2):
            group = (2 * p + half) ^ z_ref[0]
            for q in range(NQ):
                rows = slice((half * NQ + q) * BLK, (half * NQ + q + 1) * BLK)
                for k in range(2):
                    out_s[group * NQ + q, k * BLK : (k + 1) * BLK, :] = turned[k][rows]
            slots = pl.ds(group * NQ, NQ)
            stores.append(pltpu.make_async_copy(out_s.at[slots], out_hbm.at[slots], out_sem.at[2 * p + half]))
            stores[-1].start()
    for copy in stores:
        copy.wait()


def unpack_kernel(z_ref, in_ref, out_hbm, out_s, out_sem):
    wide = 2 * NQ * BLK
    turn = z_ref[0] * NQ
    stores = []
    for p in range(NZ // 2):
        cols = slice(p * wide, (p + 1) * wide)
        heads = [in_ref[(2 * NQ * p + h) ^ turn] for h in range(2 * NQ)]
        out_s[:, cols] = jnp.concatenate(heads, axis=0).T
        stores.append(pltpu.make_async_copy(out_s.at[:, cols], out_hbm.at[:, cols], out_sem.at[p]))
        stores[-1].start()
    for copy in stores:
        copy.wait()


SMEM = pl.BlockSpec(memory_space=pltpu.SMEM)
ANY = pl.BlockSpec(memory_space=pl.ANY)
VMEM = pl.BlockSpec(memory_space=pltpu.VMEM)


def kept(*arrays, where=pltpu.VMEM):
    return [pltpu.with_memory_space_constraint(a, where) for a in arrays]


def params(mebibytes):
    return pltpu.CompilerParams(vmem_limit_bytes=mebibytes * 1024 * 1024)


def pack(z, x, c, interpret=False):
    sem = pltpu.SemaphoreType.DMA
    return pl.pallas_call(
        pack_kernel,
        in_specs=[SMEM, ANY, ANY],
        out_specs=ANY,
        out_shape=pltpu.HBM((NSEQ, TWO, SEQ), x.dtype),
        scratch_shapes=[
            pltpu.VMEM(x.shape, x.dtype),
            pltpu.VMEM(x.shape, x.dtype),
            pltpu.VMEM((NSEQ, TWO, SEQ), x.dtype),
            sem((2, NZ // 2)),
            sem((NZ,)),
        ],
        compiler_params=params(16),
        interpret=interpret,
    )(z, *kept(x, c, where=pltpu.HBM))


def unpack(z, y, interpret=False):
    return pl.pallas_call(
        unpack_kernel,
        in_specs=[SMEM, VMEM],
        out_specs=ANY,
        out_shape=pltpu.HBM((SEQ, NSEQ * BLK), y.dtype),
        scratch_shapes=[pltpu.VMEM((SEQ, NSEQ * BLK), y.dtype), pltpu.SemaphoreType.DMA((NZ // 2,))],
        compiler_params=params(16),
        interpret=interpret,
    )(z, *kept(y))


LN2 = 0.6931471805599453
LOG2E = 1.4426950408889634


def sigmoid(pre):
    return pl.reciprocal(1.0 + jnp.exp2(jnp.minimum(pre * -LOG2E, 115.0)), approx=True)


def one_minus_square(u):
    series, power = 0.0, 1.0
    terms = []
    for k in range(1, 7):
        power = power * (2.0 * LN2) / k
        terms.append(-power)
    series = terms[-1]
    for t in terms[-2::-1]:
        series = series * u + t
    return series * u


CH = 16
LOTS = 2
PART = 8


def main_kernel(
    factor, m_ref, w_ref, wt_ref, out_hbm, g_ref,
    x_s, d_s, q_s, coef_s, out_ref, tri, pre_s, u_s, own_s, f1_s, gain_s, ub_s, log_s, fwd_in, rev_in, fwd_s, rev_s, back_s, out_sem,
):
    f32, bf16 = jnp.float32, jnp.bfloat16
    row = lax.broadcasted_iota(jnp.int32, (WROWS - BLK, NSEQ * SEQ), 0)
    x_s[BLK:, :] = jnp.where(row == 0, 1.0, 0.0).astype(x_s.dtype)
    decay = wt_ref[:BLK, BLK + 1 : BLK + 2].astype(f32)
    soft = jnp.maximum(decay, 0.0) + jnp.log1p(jnp.exp(-jnp.abs(decay)))
    coef_s[...] = jnp.broadcast_to((-8.0 * LOG2E) * soft, (BLK, SEQ))
    back_s[...] = LN2 / coef_s[...]
    q_s[...] = jnp.zeros_like(q_s)
    src = lax.broadcasted_iota(jnp.int32, (2 * SEQ, 2 * SEQ), 0)
    dst = lax.broadcasted_iota(jnp.int32, (2 * SEQ, 2 * SEQ), 1)
    same = (src < SEQ) == (dst < SEQ)
    for k, seen in enumerate((src <= dst, src < dst, src >= dst)):
        tri[k] = jnp.where(seen & same, 1.0, 0.0).astype(bf16)

    for s in range(NSEQ):
        x_s[:BLK, s * SEQ : (s + 1) * SEQ] = m_ref[s, :BLK, :]
    pre_s[...] = jnp.dot(wt_ref[...], x_s[...], preferred_element_type=f32)

    def gates(p, lot):
        for r in range(0, BLK, CH):
            for s, cols, side in halves(p):
                rows = slice(r, r + CH)
                x = m_ref[s, rows, :].astype(f32)
                rgate = sigmoid(pre_s[rows, cols])
                igate = 0.5 + 0.5 * jnp.tanh(0.5 * pre_s[BLK + r : BLK + r + CH, cols])
                u = coef_s[rows, :] * rgate
                var = one_minus_square(u)
                inv = lax.rsqrt(var)
                scale = var * inv
                gain = scale * igate
                drive = gain * x
                u_s[lot, rows, side] = u
                own_s[lot, rows, side] = igate * x * (inv - scale)
                f1_s[lot, rows, side] = drive - drive * igate
                gain_s[lot, rows, side] = gain
                ub_s[lot, rows, side] = u.astype(bf16)

    def weigh(p, lot):
        for r in range(0, BLK, CH):
            for s, cols, side in halves(p):
                rows = slice(r, r + CH)
                total = log_s[lot, rows, side]
                x = m_ref[s, rows, :].astype(f32)
                cot = m_ref[s, BLK + r : BLK + r + CH, :].astype(f32)
                fwd_in[lot, rows, side] = (gain_s[lot, rows, side] * x * jnp.exp2(-total)).astype(bf16)
                rev_in[lot, rows, side] = (cot * jnp.exp2(total)).astype(bf16)

    def deltas(p, lot):
        for r in range(0, BLK, CH):
            rows = slice(r, r + CH)
            part = q_s[rows, :]
            for _, cols, side in halves(p):
                total = log_s[lot, rows, side]
                u = u_s[lot, rows, side]
                adj = rev_s[lot, rows, side] * jnp.exp2(-total)
                v = adj * (fwd_s[lot, rows, side] * jnp.exp2(total) - own_s[lot, rows, side]) * u
                part = part + v
                rest = LN2 - u * back_s[rows, :]
                d_s[rows, cols] = (v * rest).astype(bf16)
                d_s[BLK + r : BLK + r + CH, cols] = (adj * f1_s[lot, rows, side]).astype(bf16)
                pre_s[rows, cols] = adj * gain_s[lot, rows, side]
            q_s[rows, :] = part

    def halves(p):
        for half in range(2):
            s = 2 * p + half
            yield s, pl.ds(pl.multiple_of(s * SEQ, SEQ), SEQ), slice(half * SEQ, (half + 1) * SEQ)

    def sums(dst, src, lot, k):
        dst[lot] = jnp.dot(src[lot], tri[k], preferred_element_type=f32)

    def several(i, _):
        for lot in range(LOTS + 2):
            if lot < LOTS:
                gates(LOTS * i + lot, lot)
                sums(log_s, ub_s, lot, 0)
            if 1 <= lot <= LOTS:
                weigh(LOTS * i + lot - 1, lot - 1)
                sums(fwd_s, fwd_in, lot - 1, 1)
                sums(rev_s, rev_in, lot - 1, 2)
            if lot >= 2:
                deltas(LOTS * i + lot - 2, lot - 2)
        return 0

    lax.fori_loop(0, NSEQ // (2 * LOTS), several, 0)

    stores = []
    for j in range(0, NSEQ, PART):
        cols = slice(j * SEQ, (j + PART) * SEQ)
        back = jnp.dot(w_ref[:BLK, :TWO], d_s[:, cols], preferred_element_type=f32) + pre_s[:BLK, cols]
        for s in range(PART):
            out_ref[j + s] = back[:, s * SEQ : (s + 1) * SEQ].astype(out_ref.dtype)
        block = pl.ds(j, PART)
        stores.append(pltpu.make_async_copy(out_ref.at[block], out_hbm.at[block], out_sem.at[j // PART]))
        stores[-1].start()

    nt = (((1,), (1,)), ((), ()))
    grad = lax.dot_general(x_s[...], d_s[...], nt, preferred_element_type=f32) * factor
    g_ref[:, :TWO] = grad.astype(g_ref.dtype)
    g_ref[:, TWO:] = jnp.zeros((WROWS, WCOLS - TWO), g_ref.dtype)
    decay_row = jnp.sum((q_s[...] / coef_s[...]).T, axis=0, keepdims=True) * (-8.0 * factor)
    tail = grad[BLK:, :BLK]
    row = lax.broadcasted_iota(jnp.int32, tail.shape, 0)
    g_ref[BLK:, :BLK] = jnp.where(row == 1, decay_row, tail).astype(g_ref.dtype)
    for copy in stores:
        copy.wait()


def main_call(factor, m, w, wt, grad_dtype=jnp.bfloat16, interpret=False):
    f32, bf16 = jnp.float32, jnp.bfloat16
    vmem = pltpu.VMEM
    flat, half = (vmem((LOTS, BLK, 2 * SEQ), kind) for kind in (f32, bf16))
    return pl.pallas_call(
        functools.partial(main_kernel, factor),
        out_shape=[pltpu.HBM((NSEQ, BLK, SEQ), bf16), vmem((WROWS, WCOLS), grad_dtype)],
        in_specs=[VMEM] * 3,
        out_specs=[ANY, VMEM],
        scratch_shapes=[
            vmem((WROWS, NSEQ * SEQ), bf16),
            vmem((TWO, NSEQ * SEQ), bf16),
            vmem((BLK, SEQ), f32),
            vmem((BLK, SEQ), f32),
            vmem((NSEQ, BLK, SEQ), bf16),
            vmem((3, 2 * SEQ, 2 * SEQ), bf16),
            vmem((TWO, NSEQ * SEQ), f32),
            flat, flat, flat, flat,
            half, flat, half, half, flat, flat,
            vmem((BLK, SEQ), f32),
            pltpu.SemaphoreType.DMA((NSEQ // PART,)),
        ],
        compiler_params=params(48),
        interpret=interpret,
    )(*kept(m, w, wt))


def finish_kernel(count, *refs):
    parts, decay_ref, outs = refs[:count], refs[count], refs[count + 2 :]
    f32 = jnp.float32
    full = sum(p[...].astype(f32) for p in parts)
    wa, wx, ba, bx, da = outs
    right = pltpu.roll(full, WCOLS - BLK, 1)
    wa[...] = full[:BLK, :BLK]
    wx[...] = right[:BLK, :BLK]
    ba[...] = full[BLK : BLK + 1, :BLK]
    bx[...] = right[BLK : BLK + 1, :BLK]
    own = 1.0 / (1.0 + jnp.exp(-decay_ref[...].astype(f32)))
    da[...] = full[BLK + 1 : BLK + 2, :BLK] * own


def finish(parts, decay, after):
    square, row = (jax.ShapeDtypeStruct((n, BLK), jnp.float32) for n in (BLK, 1))
    return pl.pallas_call(
        functools.partial(finish_kernel, len(parts)),
        in_specs=[VMEM] * (len(parts) + 1) + [ANY],
        out_specs=[VMEM] * 5,
        out_shape=[square, square, row, row, row],
        compiler_params=params(16),
    )(*kept(*parts, decay.reshape(1, BLK)), *kept(after, where=pltpu.HBM))


def wire(wa, wx, ba, bx, decay):
    bf16 = jnp.bfloat16
    tail = jnp.zeros((WROWS - BLK - 2, TWO), bf16)
    body = jnp.concatenate(
        [
            jnp.concatenate([wa, wx], axis=1),
            jnp.concatenate([ba, bx])[None],
            jnp.concatenate([decay, jnp.zeros((BLK,), bf16)])[None],
            tail,
        ],
        axis=0,
    )
    return jnp.pad(body, ((0, 0), (0, WCOLS - TWO)))


def per_device(inputs, cotangent, wa, wx, ba, bx, decay):
    bf16, f32 = jnp.bfloat16, jnp.float32
    plane, line = ("cuts", "yh", "core"), ("cuts", "z")
    z = lax.axis_index("z").astype(jnp.int32).reshape(1)
    everyone = [(i, k) for i in range(NI) for k in range(NZ)]
    fetch = [(i * NZ + (k ^ i), i * NZ + k) for i, k in everyone]
    across = [(i * NZ + (k ^ i), (i ^ 1) * NZ + k) for i, k in everyone]

    got = lax.all_to_all(pack(z, inputs, cotangent), plane, 0, 0, tiled=True)
    w = lax.ppermute(wire(wa, wx, ba, bx, decay), line, fetch)
    total = SEQ * NSEQ * NZ
    out, grads = main_call(float(total) ** -0.5, got, w, w[:, :TWO].T)
    back = lax.all_to_all(out, plane, 0, 0, tiled=True)
    near, far = lax.ppermute(grads, line, fetch), lax.ppermute(grads, line, across)
    near, far, back = lax.optimization_barrier((near, far, back))
    pair = (near.astype(f32) + far.astype(f32)).astype(bf16)
    parts = [pair] + [lax.ppermute(pair, "cuts", [(i, (i + 2 * k) % NI) for i in range(NI)]) for k in (1, 2, 3)]
    input_grad = unpack(z, back)
    grad_a, grad_x, *rows = finish(parts, decay, input_grad)
    return (input_grad, grad_a, grad_x, *(row.reshape(BLK) for row in rows))


def solution(mesh):
    fine = Mesh(mesh.devices.reshape(NI, NZ, NY, NC), ("cuts", "z", "yh", "core"))
    zero = ("z", "yh", "core")
    rows = P(("cuts",) + zero, None)
    return jax.shard_map(
        per_device,
        mesh=fine,
        in_specs=(rows, rows, P(zero, None), P(zero, None), P(zero), P(zero), P(zero)),
        out_specs=(rows, P(zero, None), P(zero, None), P(zero), P(zero), P(zero)),
        check_vma=False,
    )
```

```python
import functools

import jax
import jax.numpy as jnp
from jax import lax
from jax.experimental import pallas as pl
from jax.experimental.pallas import tpu as pltpu
from jax.sharding import Mesh
from jax.sharding import PartitionSpec as P

BLK = 176
TWO = 2 * BLK
WROWS = 192
WCOLS = 384
NZ, NY, NC = 8, 2, 2
NQ = NY * NC
NI = 8
SEQ = 128
NSEQ = NI * NQ


def pack_kernel(z_ref, x_hbm, c_hbm, out_hbm, x_s, c_s, out_s, in_sem, out_sem):
    wide = 2 * NQ * BLK
    loads = []
    for p in range(NZ // 2):
        for k, (src, dst) in enumerate(((x_hbm, x_s), (c_hbm, c_s))):
            cols = slice(p * wide, (p + 1) * wide)
            loads.append(pltpu.make_async_copy(src.at[:, cols], dst.at[:, cols], in_sem.at[k, p]))
            loads[-1].start()
    stores = []
    for p in range(NZ // 2):
        turned = []
        for k, ref in enumerate((x_s, c_s)):
            loads[2 * p + k].wait()
            turned.append(ref[:, p * wide : (p + 1) * wide].T)
        for half in range(2):
            group = (2 * p + half) ^ z_ref[0]
            for q in range(NQ):
                rows = slice((half * NQ + q) * BLK, (half * NQ + q + 1) * BLK)
                for k in range(2):
                    out_s[group * NQ + q, k * BLK : (k + 1) * BLK, :] = turned[k][rows]
            slots = pl.ds(group * NQ, NQ)
            stores.append(pltpu.make_async_copy(out_s.at[slots], out_hbm.at[slots], out_sem.at[2 * p + half]))
            stores[-1].start()
    for copy in stores:
        copy.wait()


def unpack_kernel(z_ref, in_ref, out_hbm, out_s, out_sem):
    wide = 2 * NQ * BLK
    turn = z_ref[0] * NQ
    stores = []
    for p in range(NZ // 2):
        cols = slice(p * wide, (p + 1) * wide)
        heads = [in_ref[(2 * NQ * p + h) ^ turn] for h in range(2 * NQ)]
        out_s[:, cols] = jnp.concatenate(heads, axis=0).T
        stores.append(pltpu.make_async_copy(out_s.at[:, cols], out_hbm.at[:, cols], out_sem.at[p]))
        stores[-1].start()
    for copy in stores:
        copy.wait()


SMEM = pl.BlockSpec(memory_space=pltpu.SMEM)
ANY = pl.BlockSpec(memory_space=pl.ANY)
VMEM = pl.BlockSpec(memory_space=pltpu.VMEM)


def kept(*arrays, where=pltpu.VMEM):
    return [pltpu.with_memory_space_constraint(a, where) for a in arrays]


def params(mebibytes):
    return pltpu.CompilerParams(vmem_limit_bytes=mebibytes * 1024 * 1024)


def pack(z, x, c, interpret=False):
    sem = pltpu.SemaphoreType.DMA
    return pl.pallas_call(
        pack_kernel,
        in_specs=[SMEM, ANY, ANY],
        out_specs=ANY,
        out_shape=pltpu.HBM((NSEQ, TWO, SEQ), x.dtype),
        scratch_shapes=[
            pltpu.VMEM(x.shape, x.dtype),
            pltpu.VMEM(x.shape, x.dtype),
            pltpu.VMEM((NSEQ, TWO, SEQ), x.dtype),
            sem((2, NZ // 2)),
            sem((NZ,)),
        ],
        compiler_params=params(16),
        interpret=interpret,
    )(z, *kept(x, c, where=pltpu.HBM))


def unpack(z, y, interpret=False):
    return pl.pallas_call(
        unpack_kernel,
        in_specs=[SMEM, VMEM],
        out_specs=ANY,
        out_shape=pltpu.HBM((SEQ, NSEQ * BLK), y.dtype),
        scratch_shapes=[pltpu.VMEM((SEQ, NSEQ * BLK), y.dtype), pltpu.SemaphoreType.DMA((NZ // 2,))],
        compiler_params=params(16),
        interpret=interpret,
    )(z, *kept(y))


LN2 = 0.6931471805599453
LOG2E = 1.4426950408889634


def sigmoid(pre):
    return pl.reciprocal(1.0 + jnp.exp2(jnp.minimum(pre * -LOG2E, 115.0)), approx=True)


def one_minus_square(u):
    series, power = 0.0, 1.0
    terms = []
    for k in range(1, 7):
        power = power * (2.0 * LN2) / k
        terms.append(-power)
    series = terms[-1]
    for t in terms[-2::-1]:
        series = series * u + t
    return series * u


CH = 16
LOTS = 2
PART = 8


def main_kernel(
    factor, m_ref, w_ref, wt_ref, out_hbm, g_ref,
    x_s, d_s, q_s, coef_s, out_ref, tri, pre_s, u_s, own_s, f1_s, gain_s, ub_s, log_s, fwd_in, rev_in, fwd_s, rev_s, back_s, out_sem,
):
    f32, bf16 = jnp.float32, jnp.bfloat16
    row = lax.broadcasted_iota(jnp.int32, (WROWS - BLK, NSEQ * SEQ), 0)
    x_s[BLK:, :] = jnp.where(row == 0, 1.0, 0.0).astype(x_s.dtype)
    decay = wt_ref[:BLK, BLK + 1 : BLK + 2].astype(f32)
    soft = jnp.maximum(decay, 0.0) + jnp.log1p(jnp.exp(-jnp.abs(decay)))
    coef_s[...] = jnp.broadcast_to((-8.0 * LOG2E) * soft, (BLK, SEQ))
    back_s[...] = LN2 / coef_s[...]
    q_s[...] = jnp.zeros_like(q_s)
    src = lax.broadcasted_iota(jnp.int32, (2 * SEQ, 2 * SEQ), 0)
    dst = lax.broadcasted_iota(jnp.int32, (2 * SEQ, 2 * SEQ), 1)
    same = (src < SEQ) == (dst < SEQ)
    for k, seen in enumerate((src <= dst, src < dst, src >= dst)):
        tri[k] = jnp.where(seen & same, 1.0, 0.0).astype(bf16)

    for s in range(NSEQ):
        x_s[:BLK, s * SEQ : (s + 1) * SEQ] = m_ref[s, :BLK, :]
    pre_s[...] = jnp.dot(wt_ref[...], x_s[...], preferred_element_type=f32)

    def gates(p, lot):
        for r in range(0, BLK, CH):
            for s, cols, side in halves(p):
                rows = slice(r, r + CH)
                x = m_ref[s, rows, :].astype(f32)
                rgate = sigmoid(pre_s[rows, cols])
                igate = 0.5 + 0.5 * jnp.tanh(0.5 * pre_s[BLK + r : BLK + r + CH, cols])
                u = coef_s[rows, :] * rgate
                var = one_minus_square(u)
                inv = lax.rsqrt(var)
                scale = var * inv
                gain = scale * igate
                drive = gain * x
                u_s[lot, rows, side] = u
                own_s[lot, rows, side] = igate * x * (inv - scale)
                f1_s[lot, rows, side] = drive - drive * igate
                gain_s[lot, rows, side] = gain
                ub_s[lot, rows, side] = u.astype(bf16)

    def weigh(p, lot):
        for r in range(0, BLK, CH):
            for s, cols, side in halves(p):
                rows = slice(r, r + CH)
                total = log_s[lot, rows, side]
                x = m_ref[s, rows, :].astype(f32)
                cot = m_ref[s, BLK + r : BLK + r + CH, :].astype(f32)
                fwd_in[lot, rows, side] = (gain_s[lot, rows, side] * x * jnp.exp2(-total)).astype(bf16)
                rev_in[lot, rows, side] = (cot * jnp.exp2(total)).astype(bf16)

    def deltas(p, lot):
        for r in range(0, BLK, CH):
            rows = slice(r, r + CH)
            part = q_s[rows, :]
            for _, cols, side in halves(p):
                total = log_s[lot, rows, side]
                u = u_s[lot, rows, side]
                adj = rev_s[lot, rows, side] * jnp.exp2(-total)
                v = adj * (fwd_s[lot, rows, side] * jnp.exp2(total) - own_s[lot, rows, side]) * u
                part = part + v
                rest = LN2 - u * back_s[rows, :]
                d_s[rows, cols] = (v * rest).astype(bf16)
                d_s[BLK + r : BLK + r + CH, cols] = (adj * f1_s[lot, rows, side]).astype(bf16)
                pre_s[rows, cols] = adj * gain_s[lot, rows, side]
            q_s[rows, :] = part

    def halves(p):
        for half in range(2):
            s = 2 * p + half
            yield s, pl.ds(pl.multiple_of(s * SEQ, SEQ), SEQ), slice(half * SEQ, (half + 1) * SEQ)

    def sums(dst, src, lot, k):
        dst[lot] = jnp.dot(src[lot], tri[k], preferred_element_type=f32)

    def several(i, _):
        for lot in range(LOTS + 2):
            if lot < LOTS:
                gates(LOTS * i + lot, lot)
                sums(log_s, ub_s, lot, 0)
            if 1 <= lot <= LOTS:
                weigh(LOTS * i + lot - 1, lot - 1)
                sums(fwd_s, fwd_in, lot - 1, 1)
                sums(rev_s, rev_in, lot - 1, 2)
            if lot >= 2:
                deltas(LOTS * i + lot - 2, lot - 2)
        return 0

    lax.fori_loop(0, NSEQ // (2 * LOTS), several, 0)

    stores = []
    for j in range(0, NSEQ, PART):
        cols = slice(j * SEQ, (j + PART) * SEQ)
        back = jnp.dot(w_ref[:BLK, :TWO], d_s[:, cols], preferred_element_type=f32) + pre_s[:BLK, cols]
        for s in range(PART):
            out_ref[j + s] = back[:, s * SEQ : (s + 1) * SEQ].astype(out_ref.dtype)
        block = pl.ds(j, PART)
        stores.append(pltpu.make_async_copy(out_ref.at[block], out_hbm.at[block], out_sem.at[j // PART]))
        stores[-1].start()

    nt = (((1,), (1,)), ((), ()))
    grad = lax.dot_general(x_s[...], d_s[...], nt, preferred_element_type=f32) * factor
    g_ref[:, :TWO] = grad.astype(g_ref.dtype)
    g_ref[:, TWO:] = jnp.zeros((WROWS, WCOLS - TWO), g_ref.dtype)
    decay_row = jnp.sum((q_s[...] / coef_s[...]).T, axis=0, keepdims=True) * (-8.0 * factor)
    tail = grad[BLK:, :BLK]
    row = lax.broadcasted_iota(jnp.int32, tail.shape, 0)
    g_ref[BLK:, :BLK] = jnp.where(row == 1, decay_row, tail).astype(g_ref.dtype)
    for copy in stores:
        copy.wait()


def main_call(factor, m, w, wt, grad_dtype=jnp.bfloat16, interpret=False):
    f32, bf16 = jnp.float32, jnp.bfloat16
    vmem = pltpu.VMEM
    flat, half = (vmem((LOTS, BLK, 2 * SEQ), kind) for kind in (f32, bf16))
    return pl.pallas_call(
        functools.partial(main_kernel, factor),
        out_shape=[pltpu.HBM((NSEQ, BLK, SEQ), bf16), vmem((WROWS, WCOLS), grad_dtype)],
        in_specs=[VMEM] * 3,
        out_specs=[ANY, VMEM],
        scratch_shapes=[
            vmem((WROWS, NSEQ * SEQ), bf16),
            vmem((TWO, NSEQ * SEQ), bf16),
            vmem((BLK, SEQ), f32),
            vmem((BLK, SEQ), f32),
            vmem((NSEQ, BLK, SEQ), bf16),
            vmem((3, 2 * SEQ, 2 * SEQ), bf16),
            vmem((TWO, NSEQ * SEQ), f32),
            flat, flat, flat, flat,
            half, flat, half, half, flat, flat,
            vmem((BLK, SEQ), f32),
            pltpu.SemaphoreType.DMA((NSEQ // PART,)),
        ],
        compiler_params=params(48),
        interpret=interpret,
    )(*kept(m, w, wt))


def finish_kernel(count, *refs):
    parts, decay_ref, outs = refs[:count], refs[count], refs[count + 2 :]
    f32 = jnp.float32
    full = sum(p[...].astype(f32) for p in parts)
    wa, wx, ba, bx, da = outs
    right = pltpu.roll(full, WCOLS - BLK, 1)
    wa[...] = full[:BLK, :BLK]
    wx[...] = right[:BLK, :BLK]
    ba[...] = full[BLK : BLK + 1, :BLK]
    bx[...] = right[BLK : BLK + 1, :BLK]
    own = 1.0 / (1.0 + jnp.exp(-decay_ref[...].astype(f32)))
    da[...] = full[BLK + 1 : BLK + 2, :BLK] * own


def finish(parts, decay, after):
    square, row = (jax.ShapeDtypeStruct((n, BLK), jnp.float32) for n in (BLK, 1))
    return pl.pallas_call(
        functools.partial(finish_kernel, len(parts)),
        in_specs=[VMEM] * (len(parts) + 1) + [ANY],
        out_specs=[VMEM] * 5,
        out_shape=[square, square, row, row, row],
        compiler_params=params(16),
    )(*kept(*parts, decay.reshape(1, BLK)), *kept(after, where=pltpu.HBM))


def wire(wa, wx, ba, bx, decay):
    bf16 = jnp.bfloat16
    tail = jnp.zeros((WROWS - BLK - 2, TWO), bf16)
    body = jnp.concatenate(
        [
            jnp.concatenate([wa, wx], axis=1),
            jnp.concatenate([ba, bx])[None],
            jnp.concatenate([decay, jnp.zeros((BLK,), bf16)])[None],
            tail,
        ],
        axis=0,
    )
    return jnp.pad(body, ((0, 0), (0, WCOLS - TWO)))


def per_device(inputs, cotangent, wa, wx, ba, bx, decay):
    bf16, f32 = jnp.bfloat16, jnp.float32
    plane, line = ("cuts", "yh", "core"), ("cuts", "z")
    z = lax.axis_index("z").astype(jnp.int32).reshape(1)
    everyone = [(i, k) for i in range(NI) for k in range(NZ)]
    fetch = [(i * NZ + (k ^ i), i * NZ + k) for i, k in everyone]

    got = lax.all_to_all(pack(z, inputs, cotangent), plane, 0, 0, tiled=True)
    w = lax.ppermute(wire(wa, wx, ba, bx, decay), line, fetch)
    total = SEQ * NSEQ * NZ
    out, grads = main_call(float(total) ** -0.5, got, w, w[:, :TWO].T)
    back = lax.all_to_all(out, plane, 0, 0, tiled=True)
    near = lax.ppermute(grads, line, fetch)
    shifts = [[(i, (i + 2 * k) % NI) for i in range(NI)] for k in (1, 2, 3)]
    four = sum(p.astype(f32) for p in [near] + [lax.ppermute(near, "cuts", shift) for shift in shifts])
    four, back = lax.optimization_barrier((four.astype(bf16), back))
    parts = [four, lax.ppermute(four, "cuts", [(i, i ^ 1) for i in range(NI)])]
    input_grad = unpack(z, back)
    grad_a, grad_x, *rows = finish(parts, decay, input_grad)
    return (input_grad, grad_a, grad_x, *(row.reshape(BLK) for row in rows))


def solution(mesh):
    fine = Mesh(mesh.devices.reshape(NI, NZ, NY, NC), ("cuts", "z", "yh", "core"))
    zero = ("z", "yh", "core")
    rows = P(("cuts",) + zero, None)
    return jax.shard_map(
        per_device,
        mesh=fine,
        in_specs=(rows, rows, P(zero, None), P(zero, None), P(zero), P(zero), P(zero)),
        out_specs=(rows, P(zero, None), P(zero, None), P(zero), P(zero), P(zero)),
        check_vma=False,
    )
```

```python
import functools

import jax
import jax.numpy as jnp
from jax import lax
from jax.experimental import pallas as pl
from jax.experimental.pallas import tpu as pltpu
from jax.sharding import Mesh
from jax.sharding import PartitionSpec as P

BLK = 176
TWO = 2 * BLK
WROWS = 192
WCOLS = 384
NZ, NY, NC = 8, 2, 2
NQ = NY * NC
NI = 8
SEQ = 128
NSEQ = NI * NQ


def pack_kernel(z_ref, x_hbm, c_hbm, out_hbm, x_s, c_s, out_s, in_sem, out_sem):
    wide = 2 * NQ * BLK
    loads = []
    for p in range(NZ // 2):
        for k, (src, dst) in enumerate(((x_hbm, x_s), (c_hbm, c_s))):
            cols = slice(p * wide, (p + 1) * wide)
            loads.append(pltpu.make_async_copy(src.at[:, cols], dst.at[:, cols], in_sem.at[k, p]))
            loads[-1].start()
    stores = []
    for p in range(NZ // 2):
        turned = []
        for k, ref in enumerate((x_s, c_s)):
            loads[2 * p + k].wait()
            turned.append(ref[:, p * wide : (p + 1) * wide].T)
        for half in range(2):
            group = (2 * p + half) ^ z_ref[0]
            for q in range(NQ):
                rows = slice((half * NQ + q) * BLK, (half * NQ + q + 1) * BLK)
                for k in range(2):
                    out_s[group * NQ + q, k * BLK : (k + 1) * BLK, :] = turned[k][rows]
            slots = pl.ds(group * NQ, NQ)
            stores.append(pltpu.make_async_copy(out_s.at[slots], out_hbm.at[slots], out_sem.at[2 * p + half]))
            stores[-1].start()
    for copy in stores:
        copy.wait()


def unpack_kernel(z_ref, in_ref, out_hbm, out_s, out_sem):
    wide = 2 * NQ * BLK
    turn = z_ref[0] * NQ
    stores = []
    for p in range(NZ // 2):
        cols = slice(p * wide, (p + 1) * wide)
        heads = [in_ref[(2 * NQ * p + h) ^ turn] for h in range(2 * NQ)]
        out_s[:, cols] = jnp.concatenate(heads, axis=0).T
        stores.append(pltpu.make_async_copy(out_s.at[:, cols], out_hbm.at[:, cols], out_sem.at[p]))
        stores[-1].start()
    for copy in stores:
        copy.wait()


SMEM = pl.BlockSpec(memory_space=pltpu.SMEM)
ANY = pl.BlockSpec(memory_space=pl.ANY)
VMEM = pl.BlockSpec(memory_space=pltpu.VMEM)


def kept(*arrays, where=pltpu.VMEM):
    return [pltpu.with_memory_space_constraint(a, where) for a in arrays]


def params(mebibytes):
    return pltpu.CompilerParams(vmem_limit_bytes=mebibytes * 1024 * 1024)


def pack(z, x, c, interpret=False):
    sem = pltpu.SemaphoreType.DMA
    return pl.pallas_call(
        pack_kernel,
        in_specs=[SMEM, ANY, ANY],
        out_specs=ANY,
        out_shape=pltpu.HBM((NSEQ, TWO, SEQ), x.dtype),
        scratch_shapes=[
            pltpu.VMEM(x.shape, x.dtype),
            pltpu.VMEM(x.shape, x.dtype),
            pltpu.VMEM((NSEQ, TWO, SEQ), x.dtype),
            sem((2, NZ // 2)),
            sem((NZ,)),
        ],
        compiler_params=params(16),
        interpret=interpret,
    )(z, *kept(x, c, where=pltpu.HBM))


def unpack(z, y, interpret=False):
    return pl.pallas_call(
        unpack_kernel,
        in_specs=[SMEM, VMEM],
        out_specs=ANY,
        out_shape=pltpu.HBM((SEQ, NSEQ * BLK), y.dtype),
        scratch_shapes=[pltpu.VMEM((SEQ, NSEQ * BLK), y.dtype), pltpu.SemaphoreType.DMA((NZ // 2,))],
        compiler_params=params(16),
        interpret=interpret,
    )(z, *kept(y))


LN2 = 0.6931471805599453
LOG2E = 1.4426950408889634


def sigmoid(pre):
    return pl.reciprocal(1.0 + jnp.exp2(jnp.minimum(pre * -LOG2E, 80.0)), approx=True)


def one_minus_square(u):
    series, power = 0.0, 1.0
    terms = []
    for k in range(1, 7):
        power = power * (2.0 * LN2) / k
        terms.append(-power)
    series = terms[-1]
    for t in terms[-2::-1]:
        series = series * u + t
    return series * u


CH = 16
LOTS = 2
PART = 8


def main_kernel(
    factor, m_ref, w_ref, wt_ref, out_hbm, g_ref,
    x_s, d_s, q_s, coef_s, out_ref, tri, pre_s, u_s, own_s, f1_s, gain_s, ub_s, log_s, fwd_in, rev_in, fwd_s, rev_s, back_s, out_sem,
):
    f32, bf16 = jnp.float32, jnp.bfloat16
    row = lax.broadcasted_iota(jnp.int32, (WROWS - BLK, NSEQ * SEQ), 0)
    x_s[BLK:, :] = jnp.where(row == 0, 1.0, 0.0).astype(x_s.dtype)
    decay = wt_ref[:BLK, BLK + 1 : BLK + 2].astype(f32)
    soft = jnp.maximum(decay, 0.0) + jnp.log1p(jnp.exp(-jnp.abs(decay)))
    coef_s[...] = jnp.broadcast_to((-8.0 * LOG2E) * soft, (BLK, SEQ))
    back_s[...] = LN2 / coef_s[...]
    q_s[...] = jnp.zeros_like(q_s)
    src = lax.broadcasted_iota(jnp.int32, (2 * SEQ, 2 * SEQ), 0)
    dst = lax.broadcasted_iota(jnp.int32, (2 * SEQ, 2 * SEQ), 1)
    same = (src < SEQ) == (dst < SEQ)
    for k, seen in enumerate((src <= dst, src < dst, src >= dst)):
        tri[k] = jnp.where(seen & same, 1.0, 0.0).astype(bf16)

    for s in range(NSEQ):
        x_s[:BLK, s * SEQ : (s + 1) * SEQ] = m_ref[s, :BLK, :]
    pre_s[...] = jnp.dot(wt_ref[...], x_s[...], preferred_element_type=f32)

    def gates(p, lot):
        for r in range(0, BLK, CH):
            for s, cols, side in halves(p):
                rows = slice(r, r + CH)
                x = m_ref[s, rows, :].astype(f32)
                rgate = sigmoid(pre_s[rows, cols])
                igate = 0.5 + 0.5 * jnp.tanh(0.5 * pre_s[BLK + r : BLK + r + CH, cols])
                u = coef_s[rows, :] * rgate
                var = one_minus_square(u)
                inv = lax.rsqrt(var)
                scale = var * inv
                gain = scale * igate
                drive = gain * x
                u_s[lot, rows, side] = u
                own_s[lot, rows, side] = igate * x * (inv - scale)
                f1_s[lot, rows, side] = drive - drive * igate
                gain_s[lot, rows, side] = gain
                ub_s[lot, rows, side] = u.astype(bf16)

    def weigh(p, lot):
        for r in range(0, BLK, CH):
            for s, cols, side in halves(p):
                rows = slice(r, r + CH)
                total = log_s[lot, rows, side]
                x = m_ref[s, rows, :].astype(f32)
                cot = m_ref[s, BLK + r : BLK + r + CH, :].astype(f32)
                fwd_in[lot, rows, side] = (gain_s[lot, rows, side] * x * jnp.exp2(-total)).astype(bf16)
                rev_in[lot, rows, side] = (cot * jnp.exp2(total)).astype(bf16)

    def deltas(p, lot):
        for r in range(0, BLK, CH):
            rows = slice(r, r + CH)
            part = q_s[rows, :]
            for _, cols, side in halves(p):
                total = log_s[lot, rows, side]
                u = u_s[lot, rows, side]
                adj = rev_s[lot, rows, side] * jnp.exp2(-total)
                v = adj * (fwd_s[lot, rows, side] * jnp.exp2(total) - own_s[lot, rows, side]) * u
                part = part + v
                rest = LN2 - u * back_s[rows, :]
                d_s[rows, cols] = (v * rest).astype(bf16)
                d_s[BLK + r : BLK + r + CH, cols] = (adj * f1_s[lot, rows, side]).astype(bf16)
                pre_s[rows, cols] = adj * gain_s[lot, rows, side]
            q_s[rows, :] = part

    def halves(p):
        for half in range(2):
            s = 2 * p + half
            yield s, pl.ds(pl.multiple_of(s * SEQ, SEQ), SEQ), slice(half * SEQ, (half + 1) * SEQ)

    def sums(dst, src, lot, k):
        dst[lot] = jnp.dot(src[lot], tri[k], preferred_element_type=f32)

    def several(i, _):
        for lot in range(LOTS + 2):
            if lot < LOTS:
                gates(LOTS * i + lot, lot)
                sums(log_s, ub_s, lot, 0)
            if 1 <= lot <= LOTS:
                weigh(LOTS * i + lot - 1, lot - 1)
                sums(fwd_s, fwd_in, lot - 1, 1)
                sums(rev_s, rev_in, lot - 1, 2)
            if lot >= 2:
                deltas(LOTS * i + lot - 2, lot - 2)
        return 0

    lax.fori_loop(0, NSEQ // (2 * LOTS), several, 0)

    stores = []
    for j in range(0, NSEQ, PART):
        cols = slice(j * SEQ, (j + PART) * SEQ)
        back = jnp.dot(w_ref[:BLK, :TWO], d_s[:, cols], preferred_element_type=f32) + pre_s[:BLK, cols]
        for s in range(PART):
            out_ref[j + s] = back[:, s * SEQ : (s + 1) * SEQ].astype(out_ref.dtype)
        block = pl.ds(j, PART)
        stores.append(pltpu.make_async_copy(out_ref.at[block], out_hbm.at[block], out_sem.at[j // PART]))
        stores[-1].start()

    nt = (((1,), (1,)), ((), ()))
    grad = lax.dot_general(x_s[...], d_s[...], nt, preferred_element_type=f32) * factor
    g_ref[:, :TWO] = grad.astype(g_ref.dtype)
    g_ref[:, TWO:] = jnp.zeros((WROWS, WCOLS - TWO), g_ref.dtype)
    decay_row = jnp.sum((q_s[...] / coef_s[...]).T, axis=0, keepdims=True) * (-8.0 * factor)
    tail = grad[BLK:, :BLK]
    row = lax.broadcasted_iota(jnp.int32, tail.shape, 0)
    g_ref[BLK:, :BLK] = jnp.where(row == 1, decay_row, tail).astype(g_ref.dtype)
    for copy in stores:
        copy.wait()


def main_call(factor, m, w, wt, grad_dtype=jnp.bfloat16, interpret=False):
    f32, bf16 = jnp.float32, jnp.bfloat16
    vmem = pltpu.VMEM
    flat, half = (vmem((LOTS, BLK, 2 * SEQ), kind) for kind in (f32, bf16))
    return pl.pallas_call(
        functools.partial(main_kernel, factor),
        out_shape=[pltpu.HBM((NSEQ, BLK, SEQ), bf16), vmem((WROWS, WCOLS), grad_dtype)],
        in_specs=[VMEM] * 3,
        out_specs=[ANY, VMEM],
        scratch_shapes=[
            vmem((WROWS, NSEQ * SEQ), bf16),
            vmem((TWO, NSEQ * SEQ), bf16),
            vmem((BLK, SEQ), f32),
            vmem((BLK, SEQ), f32),
            vmem((NSEQ, BLK, SEQ), bf16),
            vmem((3, 2 * SEQ, 2 * SEQ), bf16),
            vmem((TWO, NSEQ * SEQ), f32),
            flat, flat, flat, flat,
            half, flat, half, half, flat, flat,
            vmem((BLK, SEQ), f32),
            pltpu.SemaphoreType.DMA((NSEQ // PART,)),
        ],
        compiler_params=params(48),
        interpret=interpret,
    )(*kept(m, w, wt))


def finish_kernel(count, *refs):
    parts, decay_ref, outs = refs[:count], refs[count], refs[count + 2 :]
    f32 = jnp.float32
    full = sum(p[...].astype(f32) for p in parts)
    wa, wx, ba, bx, da = outs
    right = pltpu.roll(full, WCOLS - BLK, 1)
    wa[...] = full[:BLK, :BLK]
    wx[...] = right[:BLK, :BLK]
    ba[...] = full[BLK : BLK + 1, :BLK]
    bx[...] = right[BLK : BLK + 1, :BLK]
    own = 1.0 / (1.0 + jnp.exp(-decay_ref[...].astype(f32)))
    da[...] = full[BLK + 1 : BLK + 2, :BLK] * own


def finish(parts, decay, after):
    square, row = (jax.ShapeDtypeStruct((n, BLK), jnp.float32) for n in (BLK, 1))
    return pl.pallas_call(
        functools.partial(finish_kernel, len(parts)),
        in_specs=[VMEM] * (len(parts) + 1) + [ANY],
        out_specs=[VMEM] * 5,
        out_shape=[square, square, row, row, row],
        compiler_params=params(16),
    )(*kept(*parts, decay.reshape(1, BLK)), *kept(after, where=pltpu.HBM))


def wire(wa, wx, ba, bx, decay):
    bf16 = jnp.bfloat16
    tail = jnp.zeros((WROWS - BLK - 2, TWO), bf16)
    body = jnp.concatenate(
        [
            jnp.concatenate([wa, wx], axis=1),
            jnp.concatenate([ba, bx])[None],
            jnp.concatenate([decay, jnp.zeros((BLK,), bf16)])[None],
            tail,
        ],
        axis=0,
    )
    return jnp.pad(body, ((0, 0), (0, WCOLS - TWO)))


def per_device(inputs, cotangent, wa, wx, ba, bx, decay):
    bf16, f32 = jnp.bfloat16, jnp.float32
    plane, line = ("cuts", "yh", "core"), ("cuts", "z")
    z = lax.axis_index("z").astype(jnp.int32).reshape(1)
    everyone = [(i, k) for i in range(NI) for k in range(NZ)]
    fetch = [(i * NZ + (k ^ i), i * NZ + k) for i, k in everyone]

    got = lax.all_to_all(pack(z, inputs, cotangent), plane, 0, 0, tiled=True)
    w = lax.ppermute(wire(wa, wx, ba, bx, decay), line, fetch)
    total = SEQ * NSEQ * NZ
    out, grads = main_call(float(total) ** -0.5, got, w, w[:, :TWO].T)
    back = lax.all_to_all(out, plane, 0, 0, tiled=True)
    near = lax.ppermute(grads, line, fetch)
    shifts = [[(i, (i + 2 * k) % NI) for i in range(NI)] for k in (2, 1, 3)]
    four = sum(p.astype(f32) for p in [near] + [lax.ppermute(near, "cuts", shift) for shift in shifts])
    four, back = lax.optimization_barrier((four.astype(bf16), back))
    parts = [four, lax.ppermute(four, "cuts", [(i, i ^ 1) for i in range(NI)])]
    input_grad = unpack(z, back)
    grad_a, grad_x, *rows = finish(parts, decay, input_grad)
    return (input_grad, grad_a, grad_x, *(row.reshape(BLK) for row in rows))


def solution(mesh):
    fine = Mesh(mesh.devices.reshape(NI, NZ, NY, NC), ("cuts", "z", "yh", "core"))
    zero = ("z", "yh", "core")
    rows = P(("cuts",) + zero, None)
    return jax.shard_map(
        per_device,
        mesh=fine,
        in_specs=(rows, rows, P(zero, None), P(zero, None), P(zero), P(zero), P(zero)),
        out_specs=(rows, P(zero, None), P(zero, None), P(zero), P(zero), P(zero)),
        check_vma=False,
    )
```

```python
import functools

import jax
import jax.numpy as jnp
from jax import lax
from jax.experimental import pallas as pl
from jax.experimental.pallas import tpu as pltpu
from jax.sharding import Mesh
from jax.sharding import PartitionSpec as P

BLK = 176
TWO = 2 * BLK
WROWS = 192
WCOLS = 384
NZ, NY, NC = 8, 2, 2
NQ = NY * NC
NI = 8
SEQ = 128
NSEQ = NI * NQ


def pack_kernel(z_ref, x_hbm, c_hbm, out_hbm, x_s, c_s, out_s, in_sem, out_sem):
    wide = 2 * NQ * BLK
    loads = []
    for p in range(NZ // 2):
        for k, (src, dst) in enumerate(((x_hbm, x_s), (c_hbm, c_s))):
            cols = slice(p * wide, (p + 1) * wide)
            loads.append(pltpu.make_async_copy(src.at[:, cols], dst.at[:, cols], in_sem.at[k, p]))
            loads[-1].start()
    stores = []
    for p in range(NZ // 2):
        turned = []
        for k, ref in enumerate((x_s, c_s)):
            loads[2 * p + k].wait()
            turned.append(ref[:, p * wide : (p + 1) * wide].T)
        for half in range(2):
            group = (2 * p + half) ^ z_ref[0]
            for q in range(NQ):
                rows = slice((half * NQ + q) * BLK, (half * NQ + q + 1) * BLK)
                for k in range(2):
                    out_s[group * NQ + q, k * BLK : (k + 1) * BLK, :] = turned[k][rows]
            slots = pl.ds(group * NQ, NQ)
            stores.append(pltpu.make_async_copy(out_s.at[slots], out_hbm.at[slots], out_sem.at[2 * p + half]))
            stores[-1].start()
    for copy in stores:
        copy.wait()


def unpack_kernel(z_ref, in_ref, out_hbm, out_s, out_sem):
    wide = 2 * NQ * BLK
    turn = z_ref[0] * NQ
    stores = []
    for p in range(NZ // 2):
        cols = slice(p * wide, (p + 1) * wide)
        heads = [in_ref[(2 * NQ * p + h) ^ turn] for h in range(2 * NQ)]
        out_s[:, cols] = jnp.concatenate(heads, axis=0).T
        stores.append(pltpu.make_async_copy(out_s.at[:, cols], out_hbm.at[:, cols], out_sem.at[p]))
        stores[-1].start()
    for copy in stores:
        copy.wait()


SMEM = pl.BlockSpec(memory_space=pltpu.SMEM)
ANY = pl.BlockSpec(memory_space=pl.ANY)
VMEM = pl.BlockSpec(memory_space=pltpu.VMEM)


def kept(*arrays, where=pltpu.VMEM):
    return [pltpu.with_memory_space_constraint(a, where) for a in arrays]


def params(mebibytes):
    return pltpu.CompilerParams(vmem_limit_bytes=mebibytes * 1024 * 1024)


def pack(z, x, c, interpret=False):
    sem = pltpu.SemaphoreType.DMA
    return pl.pallas_call(
        pack_kernel,
        in_specs=[SMEM, ANY, ANY],
        out_specs=ANY,
        out_shape=pltpu.HBM((NSEQ, TWO, SEQ), x.dtype),
        scratch_shapes=[
            pltpu.VMEM(x.shape, x.dtype),
            pltpu.VMEM(x.shape, x.dtype),
            pltpu.VMEM((NSEQ, TWO, SEQ), x.dtype),
            sem((2, NZ // 2)),
            sem((NZ,)),
        ],
        compiler_params=params(16),
        interpret=interpret,
    )(z, *kept(x, c, where=pltpu.HBM))


def unpack(z, y, interpret=False):
    return pl.pallas_call(
        unpack_kernel,
        in_specs=[SMEM, VMEM],
        out_specs=ANY,
        out_shape=pltpu.HBM((SEQ, NSEQ * BLK), y.dtype),
        scratch_shapes=[pltpu.VMEM((SEQ, NSEQ * BLK), y.dtype), pltpu.SemaphoreType.DMA((NZ // 2,))],
        compiler_params=params(16),
        interpret=interpret,
    )(z, *kept(y))


LN2 = 0.6931471805599453
LOG2E = 1.4426950408889634


def sigmoid(pre):
    return pl.reciprocal(1.0 + jnp.exp2(jnp.minimum(pre * -LOG2E, 115.0)), approx=True)


def one_minus_square(u):
    series, power = 0.0, 1.0
    terms = []
    for k in range(1, 7):
        power = power * (2.0 * LN2) / k
        terms.append(-power)
    series = terms[-1]
    for t in terms[-2::-1]:
        series = series * u + t
    return series * u


CH = 16
LOTS = 2
PART = 8


def main_kernel(
    factor, m_ref, w_ref, wt_ref, out_hbm, g_ref,
    x_s, d_s, q_s, coef_s, out_ref, tri, pre_s, u_s, own_s, f1_s, gain_s, ub_s, log_s, fwd_in, rev_in, fwd_s, rev_s, back_s, out_sem,
):
    f32, bf16 = jnp.float32, jnp.bfloat16
    row = lax.broadcasted_iota(jnp.int32, (WROWS - BLK, NSEQ * SEQ), 0)
    x_s[BLK:, :] = jnp.where(row == 0, 1.0, 0.0).astype(x_s.dtype)
    decay = wt_ref[:BLK, BLK + 1 : BLK + 2].astype(f32)
    soft = jnp.maximum(decay, 0.0) + jnp.log1p(jnp.exp(-jnp.abs(decay)))
    coef_s[...] = jnp.broadcast_to((-8.0 * LOG2E) * soft, (BLK, SEQ))
    back_s[...] = LN2 / coef_s[...]
    q_s[...] = jnp.zeros_like(q_s)
    src = lax.broadcasted_iota(jnp.int32, (2 * SEQ, 2 * SEQ), 0)
    dst = lax.broadcasted_iota(jnp.int32, (2 * SEQ, 2 * SEQ), 1)
    same = (src < SEQ) == (dst < SEQ)
    for k, seen in enumerate((src <= dst, src < dst, src >= dst)):
        tri[k] = jnp.where(seen & same, 1.0, 0.0).astype(bf16)

    for s in range(NSEQ):
        x_s[:BLK, s * SEQ : (s + 1) * SEQ] = m_ref[s, :BLK, :]
    pre_s[...] = jnp.dot(wt_ref[...], x_s[...], preferred_element_type=f32)

    def gates(p, lot):
        for r in range(0, BLK, CH):
            for s, cols, side in halves(p):
                rows = slice(r, r + CH)
                x = m_ref[s, rows, :].astype(f32)
                rgate = sigmoid(pre_s[rows, cols])
                igate = 0.5 + 0.5 * jnp.tanh(0.5 * pre_s[BLK + r : BLK + r + CH, cols])
                u = coef_s[rows, :] * rgate
                var = one_minus_square(u)
                inv = lax.rsqrt(var)
                scale = var * inv
                gain = scale * igate
                drive = gain * x
                u_s[lot, rows, side] = u
                own_s[lot, rows, side] = igate * x * (inv - scale)
                f1_s[lot, rows, side] = drive - drive * igate
                gain_s[lot, rows, side] = gain
                ub_s[lot, rows, side] = u.astype(bf16)

    def weigh(p, lot):
        for r in range(0, BLK, CH):
            for s, cols, side in halves(p):
                rows = slice(r, r + CH)
                total = log_s[lot, rows, side]
                x = m_ref[s, rows, :].astype(f32)
                cot = m_ref[s, BLK + r : BLK + r + CH, :].astype(f32)
                fwd_in[lot, rows, side] = (gain_s[lot, rows, side] * x * jnp.exp2(-total)).astype(bf16)
                rev_in[lot, rows, side] = (cot * jnp.exp2(total)).astype(bf16)

    def deltas(p, lot):
        for r in range(0, BLK, CH):
            rows = slice(r, r + CH)
            part = q_s[rows, :]
            for _, cols, side in halves(p):
                total = log_s[lot, rows, side]
                u = u_s[lot, rows, side]
                adj = rev_s[lot, rows, side] * jnp.exp2(-total)
                v = adj * (fwd_s[lot, rows, side] * jnp.exp2(total) - own_s[lot, rows, side]) * u
                part = part + v
                rest = LN2 - u * back_s[rows, :]
                d_s[rows, cols] = (v * rest).astype(bf16)
                d_s[BLK + r : BLK + r + CH, cols] = (adj * f1_s[lot, rows, side]).astype(bf16)
                pre_s[rows, cols] = adj * gain_s[lot, rows, side]
            q_s[rows, :] = part

    def halves(p):
        for half in range(2):
            s = 2 * p + half
            yield s, pl.ds(pl.multiple_of(s * SEQ, SEQ), SEQ), slice(half * SEQ, (half + 1) * SEQ)

    def sums(dst, src, lot, k):
        dst[lot] = jnp.dot(src[lot], tri[k], preferred_element_type=f32)

    def several(i, _):
        for lot in range(LOTS + 2):
            if lot < LOTS:
                gates(LOTS * i + lot, lot)
                sums(log_s, ub_s, lot, 0)
            if 1 <= lot <= LOTS:
                weigh(LOTS * i + lot - 1, lot - 1)
                sums(fwd_s, fwd_in, lot - 1, 1)
                sums(rev_s, rev_in, lot - 1, 2)
            if lot >= 2:
                deltas(LOTS * i + lot - 2, lot - 2)
        return 0

    lax.fori_loop(0, NSEQ // (2 * LOTS), several, 0)

    stores = []
    for j in range(0, NSEQ, PART):
        cols = slice(j * SEQ, (j + PART) * SEQ)
        back = jnp.dot(w_ref[:BLK, :TWO], d_s[:, cols], preferred_element_type=f32) + pre_s[:BLK, cols]
        for s in range(PART):
            out_ref[j + s] = back[:, s * SEQ : (s + 1) * SEQ].astype(out_ref.dtype)
        block = pl.ds(j, PART)
        stores.append(pltpu.make_async_copy(out_ref.at[block], out_hbm.at[block], out_sem.at[j // PART]))
        stores[-1].start()

    nt = (((1,), (1,)), ((), ()))
    grad = lax.dot_general(x_s[...], d_s[...], nt, preferred_element_type=f32) * factor
    g_ref[:, :TWO] = grad.astype(g_ref.dtype)
    g_ref[:, TWO:] = jnp.zeros((WROWS, WCOLS - TWO), g_ref.dtype)
    decay_row = jnp.sum((q_s[...] / coef_s[...]).T, axis=0, keepdims=True) * (-8.0 * factor)
    tail = grad[BLK:, :BLK]
    row = lax.broadcasted_iota(jnp.int32, tail.shape, 0)
    g_ref[BLK:, :BLK] = jnp.where(row == 1, decay_row, tail).astype(g_ref.dtype)
    for copy in stores:
        copy.wait()


def main_call(factor, m, w, wt, grad_dtype=jnp.bfloat16, interpret=False):
    f32, bf16 = jnp.float32, jnp.bfloat16
    vmem = pltpu.VMEM
    flat, half = (vmem((LOTS, BLK, 2 * SEQ), kind) for kind in (f32, bf16))
    return pl.pallas_call(
        functools.partial(main_kernel, factor),
        out_shape=[pltpu.HBM((NSEQ, BLK, SEQ), bf16), vmem((WROWS, WCOLS), grad_dtype)],
        in_specs=[VMEM] * 3,
        out_specs=[ANY, VMEM],
        scratch_shapes=[
            vmem((WROWS, NSEQ * SEQ), bf16),
            vmem((TWO, NSEQ * SEQ), bf16),
            vmem((BLK, SEQ), f32),
            vmem((BLK, SEQ), f32),
            vmem((NSEQ, BLK, SEQ), bf16),
            vmem((3, 2 * SEQ, 2 * SEQ), bf16),
            vmem((TWO, NSEQ * SEQ), f32),
            flat, flat, flat, flat,
            half, flat, half, half, flat, flat,
            vmem((BLK, SEQ), f32),
            pltpu.SemaphoreType.DMA((NSEQ // PART,)),
        ],
        compiler_params=params(48),
        interpret=interpret,
    )(*kept(m, w, wt))


def same_kernel(in_ref, near_ref, out_ref):
    del in_ref, near_ref, out_ref


def behind(x, after):
    return pl.pallas_call(
        same_kernel,
        in_specs=[ANY, ANY],
        out_specs=ANY,
        out_shape=pltpu.HBM(x.shape, x.dtype),
        input_output_aliases={0: 0},
    )(*kept(x, where=pltpu.HBM), *kept(after, where=pltpu.HBM))


def finish_kernel(count, *refs):
    parts, decay_ref, outs = refs[:count], refs[count], refs[count + 2 :]
    f32 = jnp.float32
    full = sum(p[...].astype(f32) for p in parts)
    wa, wx, ba, bx, da = outs
    right = pltpu.roll(full, WCOLS - BLK, 1)
    wa[...] = full[:BLK, :BLK]
    wx[...] = right[:BLK, :BLK]
    ba[...] = full[BLK : BLK + 1, :BLK]
    bx[...] = right[BLK : BLK + 1, :BLK]
    own = 1.0 / (1.0 + jnp.exp(-decay_ref[...].astype(f32)))
    da[...] = full[BLK + 1 : BLK + 2, :BLK] * own


def finish(parts, decay, after):
    square, row = (jax.ShapeDtypeStruct((n, BLK), jnp.float32) for n in (BLK, 1))
    return pl.pallas_call(
        functools.partial(finish_kernel, len(parts)),
        in_specs=[VMEM] * (len(parts) + 1) + [ANY],
        out_specs=[VMEM] * 5,
        out_shape=[square, square, row, row, row],
        compiler_params=params(16),
    )(*kept(*parts, decay.reshape(1, BLK)), *kept(after, where=pltpu.HBM))


def wire(wa, wx, ba, bx, decay):
    bf16 = jnp.bfloat16
    tail = jnp.zeros((WROWS - BLK - 2, TWO), bf16)
    body = jnp.concatenate(
        [
            jnp.concatenate([wa, wx], axis=1),
            jnp.concatenate([ba, bx])[None],
            jnp.concatenate([decay, jnp.zeros((BLK,), bf16)])[None],
            tail,
        ],
        axis=0,
    )
    return jnp.pad(body, ((0, 0), (0, WCOLS - TWO)))


def per_device(inputs, cotangent, wa, wx, ba, bx, decay):
    bf16, f32 = jnp.bfloat16, jnp.float32
    plane, line = ("cuts", "yh", "core"), ("cuts", "z")
    z = lax.axis_index("z").astype(jnp.int32).reshape(1)
    everyone = [(i, k) for i in range(NI) for k in range(NZ)]
    fetch = [(i * NZ + (k ^ i), i * NZ + k) for i, k in everyone]

    got = lax.all_to_all(pack(z, inputs, cotangent), plane, 0, 0, tiled=True)
    w = lax.ppermute(wire(wa, wx, ba, bx, decay), line, fetch)
    total = SEQ * NSEQ * NZ
    out, grads = main_call(float(total) ** -0.5, got, w, w[:, :TWO].T)
    near = lax.ppermute(grads, line, fetch)
    back = lax.all_to_all(behind(out, z), plane, 0, 0, tiled=True)
    shifts = [[(i, (i + 2 * k) % NI) for i in range(NI)] for k in (1, 2, 3)]
    four = sum(p.astype(f32) for p in [near] + [lax.ppermute(near, "cuts", shift) for shift in shifts])
    four, back = lax.optimization_barrier((four.astype(bf16), back))
    parts = [four, lax.ppermute(four, "cuts", [(i, i ^ 1) for i in range(NI)])]
    input_grad = unpack(z, back)
    grad_a, grad_x, *rows = finish(parts, decay, input_grad)
    return (input_grad, grad_a, grad_x, *(row.reshape(BLK) for row in rows))


def solution(mesh):
    fine = Mesh(mesh.devices.reshape(NI, NZ, NY, NC), ("cuts", "z", "yh", "core"))
    zero = ("z", "yh", "core")
    rows = P(("cuts",) + zero, None)
    return jax.shard_map(
        per_device,
        mesh=fine,
        in_specs=(rows, rows, P(zero, None), P(zero, None), P(zero), P(zero), P(zero)),
        out_specs=(rows, P(zero, None), P(zero, None), P(zero), P(zero), P(zero)),
        check_vma=False,
    )
```

```python
import functools

import jax
import jax.numpy as jnp
from jax import lax
from jax.experimental import pallas as pl
from jax.experimental.pallas import tpu as pltpu
from jax.sharding import Mesh
from jax.sharding import PartitionSpec as P

BLK = 176
TWO = 2 * BLK
WROWS = 192
WCOLS = 384
NZ, NY, NC = 8, 2, 2
NQ = NY * NC
NI = 8
SEQ = 128
NSEQ = NI * NQ


def pack_kernel(z_ref, x_hbm, c_hbm, out_hbm, x_s, c_s, out_s, in_sem, out_sem):
    wide = 2 * NQ * BLK
    loads = []
    for p in range(NZ // 2):
        for k, (src, dst) in enumerate(((x_hbm, x_s), (c_hbm, c_s))):
            cols = slice(p * wide, (p + 1) * wide)
            loads.append(pltpu.make_async_copy(src.at[:, cols], dst.at[:, cols], in_sem.at[k, p]))
            loads[-1].start()
    stores = []
    for p in range(NZ // 2):
        turned = []
        for k, ref in enumerate((x_s, c_s)):
            loads[2 * p + k].wait()
            turned.append(ref[:, p * wide : (p + 1) * wide].T)
        for half in range(2):
            group = (2 * p + half) ^ z_ref[0]
            for q in range(NQ):
                rows = slice((half * NQ + q) * BLK, (half * NQ + q + 1) * BLK)
                for k in range(2):
                    out_s[group * NQ + q, k * BLK : (k + 1) * BLK, :] = turned[k][rows]
            slots = pl.ds(group * NQ, NQ)
            stores.append(pltpu.make_async_copy(out_s.at[slots], out_hbm.at[slots], out_sem.at[2 * p + half]))
            stores[-1].start()
    for copy in stores:
        copy.wait()


def unpack_kernel(z_ref, in_ref, out_hbm, out_s, out_sem):
    wide = 2 * NQ * BLK
    turn = z_ref[0] * NQ
    stores = []
    for p in range(NZ // 2):
        cols = slice(p * wide, (p + 1) * wide)
        heads = [in_ref[(2 * NQ * p + h) ^ turn] for h in range(2 * NQ)]
        out_s[:, cols] = jnp.concatenate(heads, axis=0).T
        stores.append(pltpu.make_async_copy(out_s.at[:, cols], out_hbm.at[:, cols], out_sem.at[p]))
        stores[-1].start()
    for copy in stores:
        copy.wait()


SMEM = pl.BlockSpec(memory_space=pltpu.SMEM)
ANY = pl.BlockSpec(memory_space=pl.ANY)
VMEM = pl.BlockSpec(memory_space=pltpu.VMEM)


def kept(*arrays, where=pltpu.VMEM):
    return [pltpu.with_memory_space_constraint(a, where) for a in arrays]


def params(mebibytes):
    return pltpu.CompilerParams(vmem_limit_bytes=mebibytes * 1024 * 1024)


def pack(z, x, c, interpret=False):
    sem = pltpu.SemaphoreType.DMA
    return pl.pallas_call(
        pack_kernel,
        in_specs=[SMEM, ANY, ANY],
        out_specs=ANY,
        out_shape=pltpu.HBM((NSEQ, TWO, SEQ), x.dtype),
        scratch_shapes=[
            pltpu.VMEM(x.shape, x.dtype),
            pltpu.VMEM(x.shape, x.dtype),
            pltpu.VMEM((NSEQ, TWO, SEQ), x.dtype),
            sem((2, NZ // 2)),
            sem((NZ,)),
        ],
        compiler_params=params(16),
        interpret=interpret,
    )(z, *kept(x, c, where=pltpu.HBM))


def unpack(z, y, interpret=False):
    return pl.pallas_call(
        unpack_kernel,
        in_specs=[SMEM, VMEM],
        out_specs=ANY,
        out_shape=pltpu.HBM((SEQ, NSEQ * BLK), y.dtype),
        scratch_shapes=[pltpu.VMEM((SEQ, NSEQ * BLK), y.dtype), pltpu.SemaphoreType.DMA((NZ // 2,))],
        compiler_params=params(16),
        interpret=interpret,
    )(z, *kept(y))


LN2 = 0.6931471805599453
LOG2E = 1.4426950408889634


def sigmoid(pre):
    return pl.reciprocal(1.0 + jnp.exp2(jnp.minimum(pre * -LOG2E, 115.0)), approx=True)


def one_minus_square(u):
    series, power = 0.0, 1.0
    terms = []
    for k in range(1, 7):
        power = power * (2.0 * LN2) / k
        terms.append(-power)
    series = terms[-1]
    for t in terms[-2::-1]:
        series = series * u + t
    return series * u


CH = 16
LOTS = 2
PART = 8


def main_kernel(
    factor, m_ref, w_ref, wt_ref, out_hbm, g_ref,
    x_s, d_s, q_s, coef_s, out_ref, tri, pre_s, u_s, own_s, f1_s, gain_s, ub_s, log_s, fwd_in, rev_in, fwd_s, rev_s, back_s, out_sem,
):
    f32, bf16 = jnp.float32, jnp.bfloat16
    row = lax.broadcasted_iota(jnp.int32, (WROWS - BLK, NSEQ * SEQ), 0)
    x_s[BLK:, :] = jnp.where(row == 0, 1.0, 0.0).astype(x_s.dtype)
    decay = wt_ref[:BLK, BLK + 1 : BLK + 2].astype(f32)
    soft = jnp.maximum(decay, 0.0) + jnp.log1p(jnp.exp(-jnp.abs(decay)))
    coef_s[...] = jnp.broadcast_to((-8.0 * LOG2E) * soft, (BLK, SEQ))
    back_s[...] = LN2 / coef_s[...]
    q_s[...] = jnp.zeros_like(q_s)
    src = lax.broadcasted_iota(jnp.int32, (2 * SEQ, 2 * SEQ), 0)
    dst = lax.broadcasted_iota(jnp.int32, (2 * SEQ, 2 * SEQ), 1)
    same = (src < SEQ) == (dst < SEQ)
    for k, seen in enumerate((src <= dst, src < dst, src >= dst)):
        tri[k] = jnp.where(seen & same, 1.0, 0.0).astype(bf16)

    for s in range(NSEQ):
        x_s[:BLK, s * SEQ : (s + 1) * SEQ] = m_ref[s, :BLK, :]
    pre_s[...] = jnp.dot(wt_ref[...], x_s[...], preferred_element_type=f32)

    def gates(p, lot):
        for r in range(0, BLK, CH):
            for s, cols, side in halves(p):
                rows = slice(r, r + CH)
                x = m_ref[s, rows, :].astype(f32)
                rgate = sigmoid(pre_s[rows, cols])
                igate = 0.5 + 0.5 * jnp.tanh(0.5 * pre_s[BLK + r : BLK + r + CH, cols])
                u = coef_s[rows, :] * rgate
                var = one_minus_square(u)
                inv = lax.rsqrt(var)
                scale = var * inv
                gain = scale * igate
                drive = gain * x
                u_s[lot, rows, side] = u
                own_s[lot, rows, side] = igate * x * (inv - scale)
                f1_s[lot, rows, side] = drive - drive * igate
                gain_s[lot, rows, side] = gain
                ub_s[lot, rows, side] = u.astype(bf16)

    def weigh(p, lot):
        for r in range(0, BLK, CH):
            for s, cols, side in halves(p):
                rows = slice(r, r + CH)
                total = log_s[lot, rows, side]
                x = m_ref[s, rows, :].astype(f32)
                cot = m_ref[s, BLK + r : BLK + r + CH, :].astype(f32)
                fwd_in[lot, rows, side] = (gain_s[lot, rows, side] * x * jnp.exp2(-total)).astype(bf16)
                rev_in[lot, rows, side] = (cot * jnp.exp2(total)).astype(bf16)

    def deltas(p, lot):
        for r in range(0, BLK, CH):
            rows = slice(r, r + CH)
            part = q_s[rows, :]
            for _, cols, side in halves(p):
                total = log_s[lot, rows, side]
                u = u_s[lot, rows, side]
                adj = rev_s[lot, rows, side] * jnp.exp2(-total)
                v = adj * (fwd_s[lot, rows, side] * jnp.exp2(total) - own_s[lot, rows, side]) * u
                part = part + v
                rest = LN2 - u * back_s[rows, :]
                d_s[rows, cols] = (v * rest).astype(bf16)
                d_s[BLK + r : BLK + r + CH, cols] = (adj * f1_s[lot, rows, side]).astype(bf16)
                pre_s[rows, cols] = adj * gain_s[lot, rows, side]
            q_s[rows, :] = part

    def halves(p):
        for half in range(2):
            s = 2 * p + half
            yield s, pl.ds(pl.multiple_of(s * SEQ, SEQ), SEQ), slice(half * SEQ, (half + 1) * SEQ)

    def sums(dst, src, lot, k):
        dst[lot] = jnp.dot(src[lot], tri[k], preferred_element_type=f32)

    def several(i, _):
        for lot in range(LOTS + 2):
            if lot < LOTS:
                gates(LOTS * i + lot, lot)
                sums(log_s, ub_s, lot, 0)
            if 1 <= lot <= LOTS:
                weigh(LOTS * i + lot - 1, lot - 1)
                sums(fwd_s, fwd_in, lot - 1, 1)
                sums(rev_s, rev_in, lot - 1, 2)
            if lot >= 2:
                deltas(LOTS * i + lot - 2, lot - 2)
        return 0

    lax.fori_loop(0, NSEQ // (2 * LOTS), several, 0)

    stores = []
    for j in range(0, NSEQ, PART):
        cols = slice(j * SEQ, (j + PART) * SEQ)
        back = jnp.dot(w_ref[:BLK, :TWO], d_s[:, cols], preferred_element_type=f32) + pre_s[:BLK, cols]
        for s in range(PART):
            out_ref[j + s] = back[:, s * SEQ : (s + 1) * SEQ].astype(out_ref.dtype)
        block = pl.ds(j, PART)
        stores.append(pltpu.make_async_copy(out_ref.at[block], out_hbm.at[block], out_sem.at[j // PART]))
        stores[-1].start()

    nt = (((1,), (1,)), ((), ()))
    grad = lax.dot_general(x_s[...], d_s[...], nt, preferred_element_type=f32) * factor
    g_ref[:, :TWO] = grad.astype(g_ref.dtype)
    g_ref[:, TWO:] = jnp.zeros((WROWS, WCOLS - TWO), g_ref.dtype)
    decay_row = jnp.sum((q_s[...] / coef_s[...]).T, axis=0, keepdims=True) * (-8.0 * factor)
    tail = grad[BLK:, :BLK]
    row = lax.broadcasted_iota(jnp.int32, tail.shape, 0)
    g_ref[BLK:, :BLK] = jnp.where(row == 1, decay_row, tail).astype(g_ref.dtype)
    for copy in stores:
        copy.wait()


def main_call(factor, m, w, wt, grad_dtype=jnp.bfloat16, interpret=False):
    f32, bf16 = jnp.float32, jnp.bfloat16
    vmem = pltpu.VMEM
    flat, half = (vmem((LOTS, BLK, 2 * SEQ), kind) for kind in (f32, bf16))
    return pl.pallas_call(
        functools.partial(main_kernel, factor),
        out_shape=[pltpu.HBM((NSEQ, BLK, SEQ), bf16), vmem((WROWS, WCOLS), grad_dtype)],
        in_specs=[VMEM] * 3,
        out_specs=[ANY, VMEM],
        scratch_shapes=[
            vmem((WROWS, NSEQ * SEQ), bf16),
            vmem((TWO, NSEQ * SEQ), bf16),
            vmem((BLK, SEQ), f32),
            vmem((BLK, SEQ), f32),
            vmem((NSEQ, BLK, SEQ), bf16),
            vmem((3, 2 * SEQ, 2 * SEQ), bf16),
            vmem((TWO, NSEQ * SEQ), f32),
            flat, flat, flat, flat,
            half, flat, half, half, flat, flat,
            vmem((BLK, SEQ), f32),
            pltpu.SemaphoreType.DMA((NSEQ // PART,)),
        ],
        compiler_params=params(48),
        interpret=interpret,
    )(*kept(m, w, wt))


def finish_kernel(count, *refs):
    parts, decay_ref, outs = refs[:count], refs[count], refs[count + 2 :]
    f32 = jnp.float32
    full = sum(p[...].astype(f32) for p in parts)
    wa, wx, ba, bx, da = outs
    right = pltpu.roll(full, WCOLS - BLK, 1)
    wa[...] = full[:BLK, :BLK]
    wx[...] = right[:BLK, :BLK]
    ba[...] = full[BLK : BLK + 1, :BLK]
    bx[...] = right[BLK : BLK + 1, :BLK]
    own = 1.0 / (1.0 + jnp.exp(-decay_ref[...].astype(f32)))
    da[...] = full[BLK + 1 : BLK + 2, :BLK] * own


def finish(parts, decay, after):
    square, row = (jax.ShapeDtypeStruct((n, BLK), jnp.float32) for n in (BLK, 1))
    return pl.pallas_call(
        functools.partial(finish_kernel, len(parts)),
        in_specs=[VMEM] * (len(parts) + 1) + [ANY],
        out_specs=[VMEM] * 5,
        out_shape=[square, square, row, row, row],
        compiler_params=params(16),
    )(*kept(*parts, decay.reshape(1, BLK)), *kept(after, where=pltpu.HBM))


def wire(wa, wx, ba, bx, decay):
    bf16 = jnp.bfloat16
    tail = jnp.zeros((WROWS - BLK - 2, TWO), bf16)
    body = jnp.concatenate(
        [
            jnp.concatenate([wa, wx], axis=1),
            jnp.concatenate([ba, bx])[None],
            jnp.concatenate([decay, jnp.zeros((BLK,), bf16)])[None],
            tail,
        ],
        axis=0,
    )
    return jnp.pad(body, ((0, 0), (0, WCOLS - TWO)))


def per_device(inputs, cotangent, wa, wx, ba, bx, decay):
    bf16, f32 = jnp.bfloat16, jnp.float32
    plane, line = ("cuts", "yh", "core"), ("cuts", "z")
    z = lax.axis_index("z").astype(jnp.int32).reshape(1)
    everyone = [(i, k) for i in range(NI) for k in range(NZ)]
    fetch = [(i * NZ + (k ^ i), i * NZ + k) for i, k in everyone]

    got = lax.all_to_all(pack(z, inputs, cotangent), plane, 0, 0, tiled=True)
    w = lax.ppermute(wire(wa, wx, ba, bx, decay), line, fetch)
    total = SEQ * NSEQ * NZ
    out, grads = main_call(float(total) ** -0.5, got, w, w[:, :TWO].T)
    back = lax.all_to_all(out, plane, 0, 0, tiled=True)
    near = lax.ppermute(grads, line, fetch)
    four = near
    for step in (2, 4):
        met = lax.ppermute(four, "cuts", [(i, i ^ step) for i in range(NI)])
        four = (four.astype(f32) + met.astype(f32)).astype(bf16)
    four, back = lax.optimization_barrier((four, back))
    parts = [four, lax.ppermute(four, "cuts", [(i, i ^ 1) for i in range(NI)])]
    input_grad = unpack(z, back)
    grad_a, grad_x, *rows = finish(parts, decay, input_grad)
    return (input_grad, grad_a, grad_x, *(row.reshape(BLK) for row in rows))


def solution(mesh):
    fine = Mesh(mesh.devices.reshape(NI, NZ, NY, NC), ("cuts", "z", "yh", "core"))
    zero = ("z", "yh", "core")
    rows = P(("cuts",) + zero, None)
    return jax.shard_map(
        per_device,
        mesh=fine,
        in_specs=(rows, rows, P(zero, None), P(zero, None), P(zero), P(zero), P(zero)),
        out_specs=(rows, P(zero, None), P(zero, None), P(zero), P(zero), P(zero)),
        check_vma=False,
    )
```
